32 devices in a mesh: dp: 8 (over z, x), tensor: 4 (over y, core).
Axes of the slice: x: 2, y: 2, z: 4, core: 2. Of those that a mesh axis runs over, the one named last changes fastest.
Arguments:
- tokens: bfloat16 [4096, 768], P(('dp', 'tensor')), may hold values from -6 to 6
- lengths: int32 [8, 3], P('dp'), may hold values from 1 to 480, 512 in all within a row
- routes: int32 [4096, 1], P('dp'), may hold values from 0 to 7; in each aligned block of 128 rows (0 to 127, 128 to 255, ...) at most 24 rows name the same one
- norm_attn: bfloat16 [768], P('dp'), may hold values from 0.099609375 to 1.8984375
- w_query: bfloat16 [768, 768], P('dp', 'tensor'), may hold values from -0.21875 to 0.21875
- w_key: bfloat16 [768, 768], P('dp', 'tensor'), may hold values from -0.21875 to 0.21875
- w_value: bfloat16 [768, 768], P('dp', 'tensor'), may hold values from -0.21875 to 0.21875
- w_attn_out: bfloat16 [768, 768], P('tensor', 'dp'), may hold values from -1.25 to 1.25
- norm_moe: bfloat16 [768], P('dp'), may hold values from 0.099609375 to 1.8984375
- w_router: bfloat16 [768, 8], P('dp'), may hold values from -0.15625 to 0.15625
- w_expert_in: bfloat16 [8, 768, 3072], P('dp', None, 'tensor'), may hold values from -0.21875 to 0.21875
- w_expert_out: bfloat16 [8, 3072, 768], P('dp', 'tensor'), may hold values from -0.875 to 0.875
- cotangent: bfloat16 [4096, 768], P(('dp', 'tensor')), may hold values from -6 to 6
Outputs:
- result: bfloat16 [4096, 768], P(('dp', 'tensor'))
- grad_tokens: float32 [4096, 768], P(('dp', 'tensor'))
- grad_norm_attn: float32 [768], P('dp')
- grad_query: float32 [768, 768], P('dp', 'tensor')
- grad_key: float32 [768, 768], P('dp', 'tensor')
- grad_value: float32 [768, 768], P('dp', 'tensor')
- grad_attn_out: float32 [768, 768], P('tensor', 'dp')
- grad_norm_moe: float32 [768], P('dp')
- grad_router: float32 [768, 8], P('dp')
- grad_expert_in: float32 [8, 768, 3072], P('dp', None, 'tensor')
- grad_expert_out: float32 [8, 3072, 768], P('dp', 'tensor')
The draws below stay inside these ranges and needn't reach their ends.
Inputs may be any that keep to these rules, and one draw needn't show every extreme that they name: `routes`: in each aligned block of 128 tokens no expert is named by more than 24 tokens. `lengths`: each row sums to 512.
All inputs are finite; a program needn't handle non-finite values.
Results may differ from the reference program's by a relative error of at most 0.012.
The reference program's roundings to bfloat16 on the way count: a program that leaves them out, or rounds other values in their place, can miss the bound.
Values may be sent and summed in bfloat16 or wider, within the bound.
No kernel may reach another device: no remote copies, remote signals or barrier semaphores. Data moves between devices by JAX's collectives and lax.ppermute only.
A program may use at most 128 MiB of HBM per device.

```python
import math
import jax
import jax.numpy as jnp
import numpy as np
from jax import lax

D = 768
HEADS = 12
HEAD_DIM = 64
FF = 3072
TOK_DEV = 512
SEQ_MAX = 480
EXPERTS = 8
TOKENS = 4096
TOK_PIECE = 128
SEQS_DEV = 3
CAP = 24
N_DP = 8


def shard_levels(rng, shape, shards, low, high):
    gain, own = 1.0, jax.random.fold_in(rng, 6)
    for position, blocks in shards:
        draws = jnp.exp(jax.random.uniform(jax.random.fold_in(own, position), (blocks,), jnp.float32, low / len(shards), high / len(shards)))
        gain = gain * jnp.repeat(draws, shape[position] // blocks).reshape([-1 if axis == position else 1 for axis in range(len(shape))])
    return gain


def length_profile(number_of, total, most, slope):
    weights = [(1 << 20) // math.isqrt(rank ** slope) + 1 for rank in range(2, number_of + 1)]
    surplus, holding = total - most - (number_of - 1), [1] * (number_of - 1)
    while surplus > 0:
        candidates = [i for i in range(number_of - 1) if holding[i] < most]
        whole, left = sum([weights[i] for i in candidates]), surplus
        for i in candidates:
            more = min(most - holding[i], max(1, left * weights[i] // whole), surplus)
            holding[i] = holding[i] + more
            surplus = surplus - more
    return np.array([most] + holding)


def ragged(rng, count, total, most, lean):
    if count == 2:
        one = jax.random.randint(rng, (), max(1, total - most), min(most, total - 1) + 1)
        return jnp.stack([one, total - one])
    sizes = jnp.asarray(length_profile(count, total, most, lean), jnp.int32)
    couples = (count - 1) // 2
    giver, receiver = sizes[1:1 + 2 * couples:2], sizes[2:2 + 2 * couples:2]
    room = jnp.minimum(giver - 1, most - receiver)
    moved = jax.random.randint(jax.random.fold_in(rng, 1), (couples,), 0, 1 << 20) % (room + 1)
    sizes = sizes.at[1:1 + 2 * couples:2].set(giver - moved).at[2:2 + 2 * couples:2].set(receiver + moved)
    return sizes[jax.random.permutation(jax.random.fold_in(rng, 2), count)]


def deal_out(rng, own, number, rows, amount, top, limit, lean):
    order = jax.random.permutation(rng, amount)
    heavy_load, common = portions_of(amount, rows * top, limit, lean, True), portions_of(amount, rows * top, limit, lean, False)
    places = jnp.arange(amount)

    def named(tallies, rotation):
        used = int((tallies > 0).sum())
        fixed = max(1, used // 4)
        passed = fixed + (places - fixed + rotation * (used - fixed)) % max(1, amount - fixed)
        return jnp.zeros((amount,), jnp.int32).at[order[jnp.where(places < fixed, places, passed)]].set(jnp.asarray(tallies, jnp.int32))

    tallies = jnp.where(number % 4 == 0, named(heavy_load, number // 4), named(common, number - number // 4 - 1))
    mixed = jax.random.permutation(jax.random.fold_in(own, 3), amount)
    giver, receiver = mixed[0:amount // 2 * 2:2], mixed[1:amount // 2 * 2:2]
    room = jnp.minimum(tallies[giver] - 1, limit - tallies[receiver]) // 2
    room = jnp.where((giver == order[0]) | (receiver == order[0]) | (tallies[receiver] == 0), 0, jnp.maximum(room, 0))
    passed = jax.random.randint(jax.random.fold_in(own, 4), (amount // 2,), 0, 1 << 20) % (room + 1)
    tallies = tallies.at[giver].add(-passed).at[receiver].add(passed)
    items = jnp.searchsorted(jnp.cumsum(tallies), jnp.arange(rows * top), side="right").astype(jnp.int32)
    table = items.reshape(top, rows).T
    table = table[jax.random.permutation(jax.random.fold_in(own, 1), rows)]
    rotation = jax.random.randint(jax.random.fold_in(own, 2), (rows, 1), 0, top)
    return jnp.take_along_axis(table, (jnp.arange(top)[None, :] + rotation) % top, axis=1)


def portions_of(number_of, total, limit, slope, full):
    loads = [(1 << 20) // math.isqrt(standing ** slope) + 1 for standing in range(1, number_of + 1)]
    largest = limit if full else min(limit, max(-(-total // number_of), total * loads[0] // sum(loads)))
    least = 1 if total - largest >= number_of - 1 else 0
    counts, spare = [largest] + [least] * (number_of - 1), total - largest - least * (number_of - 1)
    while spare > 0:
        movable = [i for i in range(1, number_of) if counts[i] < largest] or [i for i in range(1, number_of) if counts[i] < limit]
        whole, budget = sum([loads[i] for i in movable]), spare
        for i in movable:
            more = min(limit - counts[i], max(1, budget * loads[i] // whole), spare)
            counts[i] = counts[i] + more
            spare = spare - more
    return np.array(counts)


def bell_draw(key, dims, spread, limit, pieces=(), kind=jnp.bfloat16):
    array = spread * jax.random.normal(key, dims, jnp.float32)
    if pieces:
        array = array * shard_levels(key, dims, pieces, -0.22, 0.18)
    return jnp.clip(array, -limit, limit).astype(kind)


def setup_inputs(seed: int = 0) -> dict:
    keys = jax.random.split(jax.random.key(seed), 14)
    tokens = bell_draw(keys[0], (TOKENS, D), 1.0, 6.0, ((0, 32),))
    lengths = jax.vmap(lambda own: ragged(own, SEQS_DEV, TOK_DEV, SEQ_MAX, 2))(jax.random.split(keys[1], N_DP)).reshape((N_DP, SEQS_DEV)).astype(jnp.int32)
    routes_keys = jax.random.split(jax.random.fold_in(keys[2], 1), TOKENS // TOK_PIECE)
    routes_turns = jax.random.permutation(jax.random.fold_in(keys[2], 3), TOKENS // TOK_PIECE)
    routes = jax.vmap(lambda own, number: deal_out(jax.random.fold_in(keys[2], 2), own, number, TOK_PIECE, EXPERTS, 1, CAP, 1))(routes_keys, routes_turns).reshape((TOKENS, 1))
    norm_attn = jnp.clip(1.0 + 0.18 * jax.random.normal(keys[3], (D,), jnp.float32), 0.099609375, 1.8984375).astype(jnp.bfloat16)
    w_query = bell_draw(keys[4], (D, D), D ** -0.5, 0.21875, ((0, 8), (1, 4)))
    w_key = bell_draw(keys[5], (D, D), D ** -0.5, 0.21875, ((0, 8), (1, 4)))
    w_value = bell_draw(keys[6], (D, D), D ** -0.5, 0.21875, ((0, 8), (1, 4)))
    w_attn_out = bell_draw(keys[7], (D, D), (max(1, D // 32)) ** -0.5, 1.25, ((0, 4), (1, 8)))
    norm_moe = jnp.clip(1.0 + 0.18 * jax.random.normal(keys[8], (D,), jnp.float32), 0.099609375, 1.8984375).astype(jnp.bfloat16)
    w_router = bell_draw(keys[9], (D, EXPERTS), (2 * D) ** -0.5, 0.15625, ((0, 8),))
    w_expert_in = bell_draw(keys[10], (EXPERTS, D, FF), D ** -0.5, 0.21875, ((0, 8), (2, 4)))
    w_expert_out = bell_draw(keys[11], (EXPERTS, FF, D), (max(1, FF // (EXPERTS * EXPERTS))) ** -0.5, 0.875, ((0, 8), (1, 4)))
    cotangent = bell_draw(keys[12], (TOKENS, D), 1.0, 6.0, ((0, 32),))
    return {"tokens": tokens, "lengths": lengths, "routes": routes, "norm_attn": norm_attn, "w_query": w_query, "w_key": w_key, "w_value": w_value, "w_attn_out": w_attn_out, "norm_moe": norm_moe, "w_router": w_router, "w_expert_in": w_expert_in, "w_expert_out": w_expert_out, "cotangent": cotangent}


EPSILON = 1e-06
NEGATIVE = -1e+30

@jax.custom_vjp
def low(v):
    return lax.optimization_barrier(v.astype(jnp.bfloat16)).astype(jnp.float32)

@jax.custom_vjp
def low_back(v):
    return v

def low_keep(v):
    return (low(v), None)

def low_pass(kept, grad):
    return (grad,)

def back_keep(v):
    return (v, None)

def back_low(kept, grad):
    return (low(grad),)
low.defvjp(low_keep, low_pass)
low_back.defvjp(back_keep, back_low)

def matmul(left_side, right_side):
    return jnp.dot(left_side, right_side, precision=lax.Precision.HIGHEST)

def rms_norm(values, gain_vec):
    return values * lax.rsqrt(lax.optimization_barrier(jnp.mean(values * values, axis=1, keepdims=True)) + EPSILON) * gain_vec

def segment_ids(lengths_row, row_count):
    seq_ends = jnp.cumsum(lengths_row)
    positions = jnp.arange(row_count, dtype=jnp.int32)
    return lax.optimization_barrier(jnp.sum((positions[:, None] >= seq_ends[None, :]).astype(jnp.int32), axis=1))

def reference(tokens, lengths, routes, norm_attn, w_query, w_key, w_value, w_attn_out, norm_moe, w_router, w_expert_in, w_expert_out, cotangent):
    segments = jax.vmap(lambda lengths_row: segment_ids(lengths_row, TOK_DEV))(lengths)
    route_ids = routes[:, 0]
    piece_total = TOKENS // TOK_PIECE
    chosen = (route_ids[:, None] == jnp.arange(EXPERTS, dtype=jnp.int32)[None, :]).astype(jnp.int32)
    chosen = chosen.reshape(piece_total, TOK_PIECE, EXPERTS)
    earlier = jnp.cumsum(chosen, axis=1) - chosen
    slot_index = lax.optimization_barrier(jnp.sum(earlier * chosen, axis=2)).reshape(TOKENS)
    block_rows = piece_total * CAP
    dest = route_ids * block_rows + jnp.arange(TOKENS, dtype=jnp.int32) // TOK_PIECE * CAP + slot_index
    picked = (route_ids[:, None] == jnp.arange(EXPERTS, dtype=jnp.int32)[None, :]).astype(jnp.float32)

    def forward(inputs, gain_attn, query_w, key_w, value_w, out_w, gain_moe, router_w, expert_in, expert_out):
        normed = low(rms_norm(inputs, gain_attn))

        def attend(pair_in):
            group_rows, segment = pair_in

            def project(weight):
                return low(low_back(matmul(group_rows, weight))).reshape(TOK_DEV, HEADS, HEAD_DIM)
            queries = project(query_w)
            key_rows = project(key_w)
            value_rows = project(value_w)
            scores = jnp.einsum('qhd,khd->hqk', queries, key_rows, precision=lax.Precision.HIGHEST) * HEAD_DIM ** (-0.5)
            scores = low_back(scores)
            positions = jnp.arange(TOK_DEV, dtype=jnp.int32)
            allowed = (segment[:, None] == segment[None, :]) & (positions[None, :] <= positions[:, None])
            scores = jnp.where(allowed[None], scores, NEGATIVE)
            weights = low(jax.nn.softmax(scores, axis=2))
            attended = jnp.einsum('hqk,khd->qhd', weights, value_rows, precision=lax.Precision.HIGHEST)
            attended = low(low_back(attended.reshape(TOK_DEV, D)))
            return low_back(matmul(attended, out_w))
        attn = lax.map(jax.checkpoint(attend), (normed.reshape(N_DP, TOK_DEV, D), segments)).reshape(TOKENS, D)
        middle = inputs + attn
        moe_input = low(rms_norm(middle, gain_moe))
        logits = low_back(matmul(moe_input, router_w))
        probabilities = jax.nn.softmax(logits, axis=1)
        gate_value = lax.optimization_barrier(jnp.sum(probabilities * picked, axis=1))
        buffer = jnp.zeros((EXPERTS * block_rows, D), jnp.float32).at[dest].set(moe_input)
        buffer = buffer.reshape(EXPERTS, block_rows, D)

        def expert(triple):
            arrived, weight_in, weight_out = triple
            hidden = low_back(matmul(arrived, weight_in))
            return matmul(low(jax.nn.gelu(hidden)), weight_out)
        produced = lax.map(jax.checkpoint(expert), (buffer, expert_in, expert_out))
        expert_sum = low_back(produced.reshape(EXPERTS * block_rows, D)[dest])
        return middle + gate_value[:, None] * expert_sum
    floats = [argument.astype(jnp.float32) for argument in (tokens, norm_attn, w_query, w_key, w_value, w_attn_out, norm_moe, w_router, w_expert_in, w_expert_out)]
    result, pullback = jax.vjp(forward, floats[0], floats[1], floats[2], floats[3], floats[4], floats[5], floats[6], floats[7], floats[8], floats[9])
    grads = pullback(cotangent.astype(jnp.float32))
    return (result.astype(jnp.bfloat16), grads[0], grads[1], grads[2], grads[3], grads[4], grads[5], grads[6], grads[7], grads[8], grads[9])
```

```python
import jax
import jax.numpy as jnp
from jax import lax
from jax.sharding import PartitionSpec as P

HEAD_DIM = 64
EPSILON = 1e-06
NEGATIVE = -1e30
LOW = jnp.bfloat16
FULL = jnp.float32


def dot(a, b):
    return jnp.dot(a, b, preferred_element_type=FULL)


def dot_nt(a, b):
    return lax.dot_general(a, b, (((1,), (1,)), ((), ())), preferred_element_type=FULL)


def dot_tn(a, b):
    return lax.dot_general(a, b, (((0,), (0,)), ((), ())), preferred_element_type=FULL)


def after(value, *others):
    return lax.optimization_barrier((value, *others))[0]


def swap(values, axis, bit):
    count = lax.axis_size(axis)
    return lax.ppermute(values, axis, [(i, i ^ bit) for i in range(count)])


def tensor_bits():
    count = lax.axis_size("tensor")
    bits = []
    bit = count // 2
    while bit:
        bits.append(bit)
        bit //= 2
    return bits


def block_offsets():
    offsets = [0]
    for bit in tensor_bits():
        offsets = offsets + [o ^ bit for o in offsets]
    return offsets


def gather_rows(rows):
    for bit in tensor_bits():
        rows = jnp.concatenate([rows, swap(rows, "tensor", bit)], axis=0)
    return rows


def scatter_rows(partial):
    for bit in reversed(tensor_bits()):
        half = partial.shape[0] // 2
        came = swap(partial[half:].astype(LOW), "tensor", bit)
        partial = partial[:half].astype(FULL) + came.astype(FULL)
    return partial


def ring_order(count):
    return list(range(0, count, 2)) + list(range(1, count, 2))[::-1]


def ring_gather(block, split):
    count = lax.axis_size("dp")
    order = ring_order(count)
    place = [order.index(d) for d in range(count)]
    me = lax.axis_index("dp")
    my_place = jnp.array(place, jnp.int32)[me]
    order_of = jnp.array(order, jnp.int32)
    right = [(order[k], order[(k + 1) % count]) for k in range(count)]
    left = [(b, a) for a, b in right]
    first = jnp.zeros((count, split, block.shape[1]), block.dtype)
    second = jnp.zeros((count, block.shape[0] - split, block.shape[1]), block.dtype)

    def put(arrays, rows, source):
        one, two = arrays
        return (
            lax.dynamic_update_index_in_dim(one, rows[:split], source, 0),
            lax.dynamic_update_index_in_dim(two, rows[split:], source, 0),
        )

    arrays = put((first, second), block, me)
    ahead, behind = block, block
    middle = split // 32 * 16
    for step in range(1, count // 2 + 1):
        source_right = order_of[(my_place - step) % count]
        source_left = order_of[(my_place + step) % count]
        if step < count // 2:
            ahead = lax.ppermute(ahead, "dp", right)
            behind = lax.ppermute(behind, "dp", left)
            arrays = put(arrays, ahead, source_right)
            arrays = put(arrays, behind, source_left)
        else:
            top = lax.ppermute(ahead[:middle], "dp", right)
            bottom = lax.ppermute(behind[middle:], "dp", left)
            arrays = put(arrays, jnp.concatenate([top, bottom], axis=0), source_right)
    return arrays


def exchange(buffer):
    return lax.all_to_all(buffer, "dp", split_axis=0, concat_axis=0, tiled=True)


def on_device(
    tokens,
    lengths,
    routes,
    norm_attn,
    w_query,
    w_key,
    w_value,
    w_attn_out,
    norm_moe,
    w_router,
    w_expert_in,
    w_expert_out,
    cotangent,
):
    owners = lax.axis_size("dp")
    pieces = lax.axis_size("tensor")
    expert_index = lax.axis_index("dp")
    piece_index = lax.axis_index("tensor")
    piece_rows, width = tokens.shape
    shard = w_query.shape[0]
    local_width = w_query.shape[1]
    experts = w_router.shape[1]
    capacity = 3 * piece_rows // (2 * experts)
    heads = local_width // HEAD_DIM

    gains = jnp.concatenate([norm_attn, norm_moe]).reshape(1, 2 * shard)
    small = jnp.concatenate(
        [w_router.reshape(1, -1), jnp.pad(gains, ((0, 0), (0, width - 2 * shard)))], axis=0
    )
    small = jnp.pad(small, ((0, 14), (0, 0)))
    large = jnp.concatenate([w_query, w_key, w_value, w_attn_out.T], axis=1)
    weights, smalls = ring_gather(jnp.concatenate([large, small], axis=0), shard)
    weights = weights.reshape(owners * shard, 4 * local_width)
    w_qkv = weights[:, : 3 * local_width]
    w_out_t = weights[:, 3 * local_width :]
    router = smalls[:, 0, :].reshape(owners * shard, experts)
    gain_one = smalls[:, 1, :shard].reshape(width).astype(FULL)
    gain_two = smalls[:, 1, shard : 2 * shard].reshape(width).astype(FULL)

    route = lax.dynamic_slice_in_dim(routes[:, 0], piece_index * piece_rows, piece_rows)
    expert_ids = jnp.arange(experts, dtype=jnp.int32)
    chosen = (route[:, None] == expert_ids[None, :]).astype(LOW)
    ids = jnp.arange(piece_rows, dtype=jnp.int32)
    before = (ids[None, :] < ids[:, None]).astype(LOW)
    earlier = dot(before, chosen)
    slot = jnp.sum(earlier * chosen.astype(FULL), axis=1).astype(jnp.int32)
    place = route * capacity + slot
    slots = experts * capacity
    spread = (jnp.arange(slots, dtype=jnp.int32)[:, None] == place[None, :]).astype(LOW)

    def dispatch(rows):
        return exchange(dot(spread, rows).astype(LOW).reshape(experts, capacity, width)).reshape(
            slots, width
        )

    def collect(rows):
        back = exchange(rows.reshape(experts, capacity, width)).reshape(slots, width)
        return dot_tn(spread, back)

    group = gather_rows(tokens).astype(FULL)
    group_rows = group.shape[0]
    group_root = lax.rsqrt(jnp.mean(group * group, axis=1, keepdims=True) + EPSILON)
    group_one = (group * group_root * gain_one).astype(LOW)
    qkv = dot(group_one, w_qkv).astype(LOW)

    def by_head(values):
        return values.reshape(group_rows, heads, HEAD_DIM)

    queries = by_head(qkv[:, :local_width])
    key_rows = by_head(qkv[:, local_width : 2 * local_width])
    value_rows = by_head(qkv[:, 2 * local_width :])
    block_piece = piece_index ^ jnp.array(block_offsets(), jnp.int32)
    positions = (block_piece[:, None] * piece_rows + ids[None, :]).reshape(group_rows)
    ends = jnp.cumsum(lengths[0])
    segment = jnp.sum((positions[:, None] >= ends[None, :]).astype(jnp.int32), axis=1)
    allowed = (segment[:, None] == segment[None, :]) & (positions[None, :] <= positions[:, None])
    scale = HEAD_DIM ** (-0.5)
    scores = jnp.einsum("qhd,khd->hqk", queries, key_rows, preferred_element_type=FULL) * scale
    scores = jnp.where(allowed[None], scores, NEGATIVE)
    largest = jnp.max(scores, axis=2, keepdims=True)
    shifted = jnp.exp(scores - largest)
    probs = shifted / jnp.sum(shifted, axis=2, keepdims=True)
    probs_low = probs.astype(LOW)
    attended = jnp.einsum("hqk,khd->qhd", probs_low, value_rows, preferred_element_type=FULL)
    attended = attended.reshape(group_rows, local_width).astype(LOW)
    attn = scatter_rows(dot_nt(attended, w_out_t))
    inputs = tokens.astype(FULL)
    middle = inputs + attn
    root_two = lax.rsqrt(jnp.mean(middle * middle, axis=1, keepdims=True) + EPSILON)
    normed_two = middle * root_two
    moe_input = (normed_two * gain_two).astype(LOW)

    weight_in = w_expert_in[0]
    weight_out = w_expert_out[0]
    cot_rows = dispatch(after(cotangent, qkv))
    own_rows = dispatch(moe_input)
    cot_all = gather_rows(after(cot_rows, moe_input))
    arrived = gather_rows(own_rows)
    pulled = dot_nt(cot_all, weight_out)
    hidden = dot(arrived, weight_in)
    active_full, gelu_pull = jax.vjp(jax.nn.gelu, hidden)
    active = active_full.astype(LOW)
    router_p = jax.nn.softmax(dot(arrived, router), axis=1)
    is_mine = (expert_ids == expert_index)[None, :]
    gate = jnp.sum(jnp.where(is_mine, router_p, 0.0), axis=1, keepdims=True)
    grad_hidden = gelu_pull(gate * pulled)[0].astype(LOW)
    grad_gate = jnp.sum(active.astype(FULL) * pulled, axis=1, keepdims=True)
    grad_logits = (gate * grad_gate * (is_mine.astype(FULL) - router_p)).astype(LOW)
    grad_two_part = dot_nt(grad_hidden, weight_in) + dot_nt(grad_logits, router)
    grad_two = collect(scatter_rows(grad_two_part).astype(LOW))

    expert_part = gate * dot(active, weight_out)
    expert_rows = scatter_rows(after(expert_part, grad_two_part)).astype(LOW)
    result = (middle + collect(expert_rows)).astype(LOW)
    grad_buffer = (gate * cot_all.astype(FULL)).astype(LOW)
    grad_expert_out = dot_tn(active, grad_buffer)
    grad_expert_in = dot_tn(arrived, grad_hidden)
    grad_router_part = dot_tn(grad_logits, arrived)

    upstream = cotangent.astype(FULL)
    scaled_two = grad_two * gain_two
    grad_gain_two = jnp.sum(grad_two * normed_two, axis=0, keepdims=True)
    grad_middle = upstream + root_two * (
        scaled_two - normed_two * jnp.mean(scaled_two * normed_two, axis=1, keepdims=True)
    )

    grad_attn = gather_rows(grad_middle.astype(LOW))
    grad_out_t = dot_tn(grad_attn, attended)
    grad_attended = by_head(dot(grad_attn, w_out_t).astype(LOW))
    grad_probs = jnp.einsum(
        "qhd,khd->hqk", grad_attended, value_rows, preferred_element_type=FULL
    )
    inner = jnp.sum(probs * grad_probs, axis=2, keepdims=True)
    grad_scores = (probs * (grad_probs - inner)).astype(LOW)
    grad_query = jnp.einsum("hqk,khd->qhd", grad_scores, key_rows, preferred_element_type=FULL)
    grad_key = jnp.einsum("hqk,qhd->khd", grad_scores, queries, preferred_element_type=FULL)
    grad_value = jnp.einsum("hqk,qhd->khd", probs_low, grad_attended, preferred_element_type=FULL)
    grad_qkv = jnp.concatenate(
        [
            (grad_query * scale).reshape(group_rows, local_width).astype(LOW),
            (grad_key * scale).reshape(group_rows, local_width).astype(LOW),
            grad_value.reshape(group_rows, local_width).astype(LOW),
        ],
        axis=1,
    )
    grad_w = jnp.concatenate([dot_tn(group_one, grad_qkv), grad_out_t], axis=1).astype(LOW)
    grad_one = scatter_rows(dot_nt(grad_qkv, w_qkv))

    root_one = group_root[:piece_rows]
    normed_one = inputs * root_one
    scaled_one = grad_one * gain_one
    grad_gain_one = jnp.sum(grad_one * normed_one, axis=0, keepdims=True)
    grad_tokens = grad_middle + root_one * (
        scaled_one - normed_one * jnp.mean(scaled_one * normed_one, axis=1, keepdims=True)
    )

    blocks = exchange(grad_w.reshape(owners, shard, 4 * local_width))
    grad_w_sum = jnp.sum(blocks.astype(FULL), axis=0)

    def sum_small(values):
        count = values.shape[0]
        parts = values.reshape(count, owners, shard).transpose(1, 0, 2)
        total = jnp.sum(exchange(parts), axis=0)
        for bit in reversed(tensor_bits()):
            total = total + swap(total, "tensor", bit)
        return total

    early = sum_small(jnp.concatenate([grad_router_part, grad_gain_two], axis=0))
    late = sum_small(grad_gain_one)
    return (
        result,
        grad_tokens,
        late[0],
        grad_w_sum[:, :local_width],
        grad_w_sum[:, local_width : 2 * local_width],
        grad_w_sum[:, 2 * local_width : 3 * local_width],
        grad_w_sum[:, 3 * local_width :].T,
        early[experts],
        early[:experts].T,
        grad_expert_in[None],
        grad_expert_out[None],
    )


def solution(mesh):
    return jax.shard_map(
        on_device,
        mesh=mesh,
        in_specs=(
            P(("dp", "tensor"), None),
            P("dp", None),
            P("dp", None),
            P("dp"),
            P("dp", "tensor"),
            P("dp", "tensor"),
            P("dp", "tensor"),
            P("tensor", "dp"),
            P("dp"),
            P("dp", None),
            P("dp", None, "tensor"),
            P("dp", "tensor", None),
            P(("dp", "tensor"), None),
        ),
        out_specs=(
            P(("dp", "tensor"), None),
            P(("dp", "tensor"), None),
            P("dp"),
            P("dp", "tensor"),
            P("dp", "tensor"),
            P("dp", "tensor"),
            P("tensor", "dp"),
            P("dp"),
            P("dp", None),
            P("dp", None, "tensor"),
            P("dp", "tensor", None),
        ),
        check_vma=False,
    )
```

```python
import functools

import jax
import jax.numpy as jnp
from jax import lax
from jax.experimental import pallas as pl
from jax.experimental.pallas import tpu as pltpu
from jax.sharding import PartitionSpec as P

HEAD_DIM = 64
EPSILON = 1e-06
NEGATIVE = -1e30
LOW = jnp.bfloat16
FULL = jnp.float32
SCALE = HEAD_DIM ** (-0.5)
MIB = 1 << 20


def dot(a, b):
    return jnp.dot(a, b, preferred_element_type=FULL)


def dot_nt(a, b):
    return lax.dot_general(a, b, (((1,), (1,)), ((), ())), preferred_element_type=FULL)


def dot_tn(a, b):
    return lax.dot_general(a, b, (((0,), (0,)), ((), ())), preferred_element_type=FULL)


def after(value, *others):
    return lax.optimization_barrier((value, *others))[0]


class Fetched:
    def __init__(self, ref, held, sem):
        self.held, self.waiting = held, True
        self.copy = pltpu.make_async_copy(ref, held, sem)
        self.copy.start()
        self.shape = held.shape

    def wait(self):
        if self.waiting:
            self.copy.wait()
            self.waiting = False

    def __getitem__(self, index):
        self.wait()
        return self.held[index]


class Stored:
    def __init__(self, ref, held, sem):
        self.ref, self.held, self.sem = ref, held, sem
        self.copy = None
        self.shape, self.dtype = held.shape, held.dtype

    def __getitem__(self, index):
        return self.held[index]

    def __setitem__(self, index, value):
        self.held[index] = value

    def flush(self):
        if self.copy is None:
            self.copy = pltpu.make_async_copy(self.held, self.ref, self.sem)
            self.copy.start()


def kernel_call(body, outs, name, fetch=(), store=(), smem=(), time=1, limit=24, scratch=()):
    def call(*operands):
        n_in, n_out, n_scratch = len(operands), len(outs), len(scratch)
        held = [pltpu.VMEM(operands[i].shape, operands[i].dtype) for i in fetch]
        held += [pltpu.VMEM(*outs[i]) for i in store]
        sems = [pltpu.SemaphoreType.DMA((len(held),))] if held else []

        def kernel(*refs):
            ins, results = list(refs[:n_in]), list(refs[n_in : n_in + n_out])
            rest = refs[n_in + n_out :]
            own, buffers = rest[:n_scratch], rest[n_scratch : n_scratch + len(held)]
            sem = rest[-1] if held else None
            at = 0
            for i in fetch:
                ins[i] = Fetched(ins[i], buffers[at], sem.at[at])
                at += 1
            for i in store:
                results[i] = Stored(results[i], buffers[at], sem.at[at])
                at += 1
            body(*ins, *results, *own)
            for i in fetch:
                ins[i].wait()
            for i in store:
                results[i].flush()
            for i in store:
                results[i].copy.wait()

        def spec(i, hbm):
            return pl.BlockSpec(memory_space=pltpu.HBM if i in hbm else pltpu.VMEM)

        operands = [
            pltpu.with_memory_space_constraint(x, pltpu.HBM) if i in fetch else x
            for i, x in enumerate(operands)
        ]
        return pl.pallas_call(
            kernel,
            out_shape=[
                pltpu.HBM(*outs[i]) if i in store else jax.ShapeDtypeStruct(*outs[i])
                for i in range(n_out)
            ],
            in_specs=[
                pl.BlockSpec(memory_space=pltpu.SMEM) if i in smem else spec(i, fetch)
                for i in range(n_in)
            ],
            out_specs=[spec(i, store) for i in range(n_out)],
            scratch_shapes=[*scratch, *held, *sems],
            compiler_params=pltpu.CompilerParams(vmem_limit_bytes=limit * MIB),
            cost_estimate=pl.CostEstimate(
                flops=int(time * 1.1e9), bytes_accessed=MIB, transcendentals=0
            ),
            name=name,
        )(*operands)

    return call


def move_kernel(*refs):
    count = len(refs) // 2
    sem = refs[-1]
    copies = [
        pltpu.make_async_copy(refs[k], refs[count + k], sem.at[k]) for k in range(count)
    ]
    for copy in copies:
        copy.start()
    for copy in copies:
        copy.wait()


def moved(arrays, source, target, name):
    kinds = [(x.shape, x.dtype) for x in arrays]
    if source is pltpu.HBM:
        arrays = [pltpu.with_memory_space_constraint(x, pltpu.HBM) for x in arrays]
    return pl.pallas_call(
        move_kernel,
        out_shape=[
            pltpu.HBM(*kind) if target is pltpu.HBM else jax.ShapeDtypeStruct(*kind)
            for kind in kinds
        ],
        in_specs=[pl.BlockSpec(memory_space=source) for _ in kinds],
        out_specs=[pl.BlockSpec(memory_space=target) for _ in kinds],
        scratch_shapes=[pltpu.SemaphoreType.DMA((len(kinds),))],
        compiler_params=pltpu.CompilerParams(vmem_limit_bytes=16 * MIB),
        cost_estimate=pl.CostEstimate(flops=2 * 10**9, bytes_accessed=MIB, transcendentals=0),
        name=name,
    )(*arrays)


def save(*arrays):
    return moved(arrays, pltpu.VMEM, pltpu.HBM, "save")


def load(*arrays):
    return moved(arrays, pltpu.HBM, pltpu.VMEM, "load")


def swap(values, axis, bit):
    count = lax.axis_size(axis)
    return lax.ppermute(values, axis, [(i, i ^ bit) for i in range(count)])


def exchange(buffer):
    return lax.all_to_all(buffer, "dp", split_axis=0, concat_axis=0, tiled=True)


OFFSETS = (0, 2, 1, 3)


def swap_far(rows):
    return swap(rows, "tensor", 2)


def swap_near(rows):
    return swap(rows, "tensor", 1)


def ring_source(place, count):
    place = lax.rem(place + 2 * count, count)
    return jnp.where(place < count // 2, 2 * place, 2 * (count - 1 - place) + 1)


def ring_perms(count):
    order = list(range(0, count, 2)) + list(range(1, count, 2))[::-1]
    right = [(order[k], order[(k + 1) % count]) for k in range(count)]
    return right, [(b, a) for a, b in right]


def ring_gather(block):
    count = lax.axis_size("dp")
    right, left = ring_perms(count)
    behind, ahead = [block], [block]
    for _ in range(1, count // 2):
        behind.append(lax.ppermute(behind[-1], "dp", right))
        ahead.append(lax.ppermute(ahead[-1], "dp", left))
    middle = block.shape[0] // 32 * 16
    top = lax.ppermute(behind[-1][:middle], "dp", right)
    bottom = lax.ppermute(ahead[-1][middle:], "dp", left)
    return behind[1:], ahead[1:], top, bottom


def ring_place(me, count):
    return jnp.where(lax.rem(me, 2) == 0, me // 2, count - 1 - me // 2)


def ring_reduce(grad_w, scalars, blocks_shape):
    count = lax.axis_size("dp")
    right, left = ring_perms(count)
    shard, width = blocks_shape
    middle = shard // 32 * 16
    top, bottom = kernel_call(
        functools.partial(ring_first_kernel, count),
        [((middle, width), LOW), ((shard - middle, width), LOW)],
        "ring_first",
        smem=(0,),
    )(scalars, grad_w)
    ahead = lax.ppermute(top, "dp", right)
    behind = lax.ppermute(bottom, "dp", left)
    marks = [top]
    for step in range(count // 2 - 1, 0, -1):
        ahead, behind = kernel_call(
            functools.partial(ring_add_kernel, count, step),
            [((shard, width), LOW), ((shard, width), LOW)],
            "ring_add",
            smem=(0,),
        )(scalars, grad_w, ahead, behind)
        marks.append(ahead)
        ahead = lax.ppermute(ahead, "dp", right)
        behind = lax.ppermute(behind, "dp", left)
    return ahead, behind, marks


def root_of(values):
    return lax.rsqrt(jnp.mean(values * values, axis=1, keepdims=True) + EPSILON)


def pack_kernel(wq, wk, wv, wo, router, gain_one, gain_two, out):
    shard, local = wq.shape
    out[0:shard, 0:local] = wq[...]
    out[0:shard, local : 2 * local] = wk[...]
    out[0:shard, 2 * local : 3 * local] = wv[...]
    out[0:shard, 3 * local :] = wo[...].astype(FULL).T.astype(LOW)
    experts = router.shape[0]
    rows = out.shape[0] - shard
    small = jnp.concatenate(
        [
            router[...].astype(FULL),
            gain_one[...].astype(FULL),
            gain_two[...].astype(FULL),
            jnp.zeros((rows - experts - 2, shard), FULL),
        ],
        axis=0,
    )
    out[shard:, :] = jnp.zeros((rows, out.shape[1]), LOW)
    out[shard:, 0:shard] = small.astype(LOW)


def spread_kernel(capacity, slots, scalars, routes, cot, spread, rows):
    count = cot.shape[0]
    piece = scalars[1]
    route = routes[pl.ds(pl.multiple_of(piece * count, count), count), :]
    experts = slots // capacity
    ids = lax.broadcasted_iota(jnp.int32, (count, experts), 1)
    chosen = jnp.where(route == ids, 1.0, 0.0)
    first = lax.broadcasted_iota(jnp.int32, (count, count), 0)
    second = lax.broadcasted_iota(jnp.int32, (count, count), 1)
    before = jnp.where(second < first, 1.0, 0.0).astype(LOW)
    earlier = dot(before, chosen.astype(LOW))
    slot = jnp.sum(earlier * chosen, axis=1, keepdims=True).astype(jnp.int32)
    place = route * capacity + slot
    lanes = lax.broadcasted_iota(jnp.int32, (count, slots), 1)
    one_hot = jnp.where(place == lanes, 1.0, 0.0).astype(LOW)
    spread[...] = one_hot
    rows[...] = dot_tn(one_hot, cot[...]).astype(LOW)


def assemble_kernel(count, scalars, *refs):
    blocks, (weights, smalls) = refs[:-2], refs[-2:]
    me = scalars[0]
    place = ring_place(me, count)
    shard = weights.shape[0] // count
    half = count // 2
    steps = [0] + [-s for s in range(1, half)] + list(range(1, half))
    for step, block in zip(steps, blocks):
        source = ring_source(place + step, count) if step else me
        weights[pl.ds(pl.multiple_of(source * shard, 16), shard), :] = block[0:shard, :]
        smalls[source] = block[shard:, 0:shard].astype(FULL)


def finish(count, scalars, blocks, weights, smalls, small_out):
    shard = weights.shape[0] // count
    weights[...] = blocks[0][...]
    smalls[...] = blocks[1][...]
    top, bottom = blocks[2:]
    source = ring_source(ring_place(scalars[0], count) + count // 2, count)
    middle = top.shape[0]
    start = pl.multiple_of(source * shard, 16)
    weights[pl.ds(start, middle), :] = top[...]
    rest = shard - middle
    weights[pl.ds(pl.multiple_of(start + middle, 16), rest), :] = bottom[0:rest, :]
    smalls[source] = bottom[rest:, 0:shard].astype(FULL)
    for d in range(count):
        small_out[:, d * shard : (d + 1) * shard] = smalls[d]


def positions_of(piece, rows, shape, dim):
    index = lax.broadcasted_iota(jnp.int32, shape, dim)
    block = index // rows
    flip = jnp.where(block == 1, 2, jnp.where(block == 2, 1, block))
    return (piece ^ flip) * rows + lax.rem(index, rows)


def attend_kernel(count, sequences, has_blocks, *refs):
    scalars, tokens, far, near, near_far = refs[:5]
    given = 4 if has_blocks else 2
    blocks = refs[5 : 5 + given]
    outs = refs[5 + given :]
    keep, keep_far, send, send_far, ones, qkv_out, attended, probs_out, group = outs[:9]
    if has_blocks:
        weights, small_out, smalls = outs[9:]
        finish(count, scalars, blocks, weights, smalls, small_out)
        small = small_out
    else:
        weights, small = blocks
    rows = tokens.shape[0]
    total = 4 * rows
    local = attended.shape[1]
    experts = count
    gain = small[experts : experts + 1, :]
    piece = scalars[1]
    for index, ref in enumerate((tokens, far, near, near_far)):
        group[index * rows : (index + 1) * rows, :] = ref[...]
        values = ref[...].astype(FULL)
        ones[index * rows : (index + 1) * rows, :] = (values * root_of(values) * gain).astype(LOW)
    qkv = dot(ones[...], weights[:, 0 : 3 * local]).astype(LOW)
    qkv_out[...] = qkv
    query_pos = positions_of(piece, rows, (total, 1), 0)
    key_pos = positions_of(piece, rows, (1, total), 1)
    start = jnp.zeros((total, 1), jnp.int32)
    end = jnp.int32(0)
    for s in range(sequences):
        end = end + scalars[2 + s]
        start = jnp.where(query_pos >= end, end, start)
    bias = jnp.where((key_pos <= query_pos) & (key_pos >= start), 0.0, NEGATIVE)
    for h in range(local // HEAD_DIM):
        at = h * HEAD_DIM
        q = qkv[:, at : at + HEAD_DIM]
        k = qkv[:, local + at : local + at + HEAD_DIM]
        v = qkv[:, 2 * local + at : 2 * local + at + HEAD_DIM]
        scores = dot_nt(q, k) * SCALE + bias
        shifted = jnp.exp(scores - jnp.max(scores, axis=1, keepdims=True))
        probs = shifted * (1.0 / jnp.sum(shifted, axis=1, keepdims=True))
        probs_out[h] = probs
        attended[:, at : at + HEAD_DIM] = dot(probs.astype(LOW), v).astype(LOW)
    w_out_t = weights[:, 3 * local :]
    keep[...] = dot_nt(attended[0:rows, :], w_out_t)
    keep_far[...] = dot_nt(attended[rows : 2 * rows, :], w_out_t)
    send[...] = dot_nt(attended[2 * rows : 3 * rows, :], w_out_t).astype(LOW)
    send_far[...] = dot_nt(attended[3 * rows :, :], w_out_t).astype(LOW)


def middle_kernel(gain_row, tokens, keep, near, far, small, spread, middle, rows):
    total = tokens[...].astype(FULL) + (
        keep[...] + near[...].astype(FULL) + far[...].astype(FULL)
    )
    middle[...] = total
    moe = (total * root_of(total) * small[gain_row : gain_row + 1, :]).astype(LOW)
    rows[...] = dot_tn(spread[...], moe).astype(LOW)


def far_kernel(keep_far, near, out):
    out[...] = (keep_far[...] + near[...].astype(FULL)).astype(LOW)


GELU_A = 0.7978845608028654
GELU_B = 0.044715


def expert_kernel(
    experts,
    scalars,
    x_keep,
    x_send,
    cot_keep,
    cot_send,
    w_in,
    w_out,
    small,
    part_keep,
    part_send,
    active_out,
    hidden_out,
    buffer_out,
    gate_out,
    router_out,
    x,
    cot,
):
    rows = x_keep.shape[0]
    x[0:rows, :] = x_keep[...]
    x[rows:, :] = x_send[...]
    cot[0:rows, :] = cot_keep[...]
    cot[rows:, :] = cot_send[...]
    hidden = dot(x[...], w_in[...])
    pulled = dot_nt(cot[...], w_out[...])
    router_t = small[0:experts, :].astype(LOW)
    mine = lax.broadcasted_iota(jnp.int32, (2 * rows, experts), 1) == scalars[0]
    logits = dot_nt(x[...], router_t)
    raised = jnp.exp(logits - jnp.max(logits, axis=1, keepdims=True))
    chances = raised / jnp.sum(raised, axis=1, keepdims=True)
    gate = jnp.sum(jnp.where(mine, chances, 0.0), axis=1, keepdims=True)
    square = hidden * hidden
    wave = jnp.tanh(GELU_A * hidden * (1.0 + GELU_B * square))
    half = 0.5 + 0.5 * wave
    active = (hidden * half).astype(LOW)
    active_out[...] = active
    slope = half + 0.5 * GELU_A * hidden * (1.0 - wave * wave) * (1.0 + 3.0 * GELU_B * square)
    grad_hidden = (gate * pulled * slope).astype(LOW)
    hidden_out[...] = grad_hidden
    grad_gate = jnp.sum(active.astype(FULL) * pulled, axis=1, keepdims=True)
    grad_logits = (gate * grad_gate * (jnp.where(mine, 1.0, 0.0) - chances)).astype(LOW)
    buffer_out[...] = (gate * cot[...].astype(FULL)).astype(LOW)
    gate_out[...] = gate
    router_out[...] = dot_tn(grad_logits, x[...])
    part = dot_nt(grad_hidden, w_in[...]) + dot(grad_logits, router_t)
    part_keep[...] = part[0:rows, :]
    part_send[...] = part[rows:, :].astype(LOW)


def forward_kernel(
    first, first_gate, second, second_gate, w_out, keep, send, keep_far, send_far
):
    rows = keep.shape[0]
    part = second_gate[...] * dot(second[...], w_out[...])
    keep_far[...] = part[0:rows, :]
    send_far[...] = part[rows:, :].astype(LOW)
    part = first_gate[...] * dot(first[...], w_out[...])
    keep[...] = part[0:rows, :]
    send[...] = part[rows:, :].astype(LOW)


def join_kernel(keep, near, far, out):
    out[...] = (keep[...] + near[...].astype(FULL) + far[...].astype(FULL)).astype(LOW)


def grad_w_kernel(*refs):
    *parts, out = refs
    lefts, rights = parts[:-2], parts[-2:]

    def whole(parts):
        return jnp.concatenate([part[...] for part in parts], axis=0)

    out[0] = dot_tn(whole(lefts), whole(rights))


def result_kernel(middle, spread, back, out):
    out[...] = (middle[...] + dot(spread[...], back[...])).astype(LOW)


def back_kernel(gain_row, middle, cot, spread, back, small, grad_middle, grad_low, grad_gain):
    grad_two = dot(spread[...], back[...])
    values = middle[...]
    root = root_of(values)
    normed = values * root
    scaled = grad_two * small[gain_row : gain_row + 1, :]
    grad_gain[...] = jnp.sum(grad_two * normed, axis=0, keepdims=True)
    total = cot[...].astype(FULL) + root * (
        scaled - normed * jnp.mean(scaled * normed, axis=1, keepdims=True)
    )
    grad_middle[...] = total
    grad_low[...] = total.astype(LOW)


def attend_back_kernel(
    experts,
    own,
    far,
    near,
    near_far,
    ones,
    qkv,
    attended,
    probs,
    weights,
    group,
    router_one,
    router_two,
    gain_two,
    keep,
    keep_far,
    send,
    send_far,
    grad_w,
    payload,
    grads,
    joined,
):
    rows = own.shape[0]
    local = attended.shape[1]
    joined[0:rows, :] = own[...]
    joined[rows : 2 * rows, :] = far[...]
    joined[2 * rows : 3 * rows, :] = near[...]
    joined[3 * rows :, :] = near_far[...]
    w_out_t = weights[:, 3 * local :]
    grad_attended = dot(joined[...], w_out_t).astype(LOW)
    for h in range(local // HEAD_DIM):
        at = h * HEAD_DIM
        q = qkv[:, at : at + HEAD_DIM]
        k = qkv[:, local + at : local + at + HEAD_DIM]
        v = qkv[:, 2 * local + at : 2 * local + at + HEAD_DIM]
        upstream = grad_attended[:, at : at + HEAD_DIM]
        grad_p = dot_nt(upstream, v)
        p = probs[h]
        inner = jnp.sum(p * grad_p, axis=1, keepdims=True)
        grad_s = (p * (grad_p - inner)).astype(LOW)
        grads[:, at : at + HEAD_DIM] = (dot(grad_s, k) * SCALE).astype(LOW)
        grads[:, local + at : local + at + HEAD_DIM] = (dot_tn(grad_s, q) * SCALE).astype(LOW)
        grads[:, 2 * local + at : 2 * local + at + HEAD_DIM] = dot_tn(
            p.astype(LOW), upstream
        ).astype(LOW)
    grad_w[:, 3 * local :] = dot_tn(joined[...], attended[...]).astype(LOW)
    grad_w[:, 0 : 3 * local] = dot_tn(ones[...], grads[...]).astype(LOW)
    w_qkv = weights[:, 0 : 3 * local]

    def normed(values):
        values = values.astype(FULL)
        return values * root_of(values)

    gain_one = None
    for index, out in enumerate((keep, keep_far, send, send_far)):
        part = dot_nt(grads[index * rows : (index + 1) * rows, :], w_qkv)
        out[...] = part.astype(out.dtype)
        if index == 0:
            out.flush()
        gain = jnp.sum(
            part * normed(group[index * rows : (index + 1) * rows, :]), axis=0, keepdims=True
        )
        gain_one = gain if gain_one is None else gain_one + gain
    owners, height, shard = payload.shape
    whole = jnp.concatenate(
        [
            router_one[...] + router_two[...],
            gain_one,
            gain_two[...],
            jnp.zeros((height - experts - 2, gain_one.shape[1]), FULL),
        ],
        axis=0,
    )
    for d in range(owners):
        payload[d] = whole[:, d * shard : (d + 1) * shard]


def last_kernel(gain_row, tokens, keep, near, far, grad_middle, small, grad_tokens):
    rows = tokens.shape[0]
    values = tokens[...].astype(FULL)
    root = root_of(values)
    normed = values * root
    grad_one = keep[...] + near[...].astype(FULL) + far[...].astype(FULL)
    scaled = grad_one * small[gain_row : gain_row + 1, :]
    grad_tokens[...] = grad_middle[...] + root * (
        scaled - normed * jnp.mean(scaled * normed, axis=1, keepdims=True)
    )


def ring_rows(count, shard, scalars, offset):
    source = ring_source(ring_place(scalars[0], count) + offset, count)
    return pl.multiple_of(source * shard, 16)


def ring_first_kernel(count, scalars, grad_w, top, bottom):
    middle = top.shape[0]
    rest = bottom.shape[0]
    start = ring_rows(count, middle + rest, scalars, count // 2)
    top[...] = grad_w[pl.ds(start, middle), :]
    bottom[...] = grad_w[pl.ds(pl.multiple_of(start + middle, 16), rest), :]


def ring_add_kernel(count, step, scalars, grad_w, ahead, behind, to_right, to_left):
    shard = to_right.shape[0]
    right = ring_rows(count, shard, scalars, step)
    left = ring_rows(count, shard, scalars, -step)
    if ahead.shape[0] == shard:
        to_right[...] = (
            grad_w[pl.ds(right, shard), :].astype(FULL) + ahead[...].astype(FULL)
        ).astype(LOW)
        to_left[...] = (
            grad_w[pl.ds(left, shard), :].astype(FULL) + behind[...].astype(FULL)
        ).astype(LOW)
        return
    middle = ahead.shape[0]
    rest = shard - middle
    to_right[0:middle, :] = (
        grad_w[pl.ds(right, middle), :].astype(FULL) + ahead[...].astype(FULL)
    ).astype(LOW)
    to_right[middle:, :] = grad_w[pl.ds(pl.multiple_of(right + middle, 16), rest), :]
    to_left[0:middle, :] = grad_w[pl.ds(left, middle), :]
    to_left[middle:, :] = (
        grad_w[pl.ds(pl.multiple_of(left + middle, 16), rest), :].astype(FULL)
        + behind[...].astype(FULL)
    ).astype(LOW)


def write_sums(total, query, key, value, out):
    local = query.shape[1]
    query[...] = total[:, 0:local]
    key[...] = total[:, local : 2 * local]
    value[...] = total[:, 2 * local : 3 * local]
    out[...] = total[:, 3 * local :].T


def ring_last_kernel(count, scalars, grad_w, ahead, behind, query, key, value, out):
    shard = ahead.shape[0]
    start = pl.multiple_of(scalars[0] * shard, 16)
    total = grad_w[pl.ds(start, shard), :].astype(FULL) + (
        ahead[...].astype(FULL) + behind[...].astype(FULL)
    )
    write_sums(total, query, key, value, out)


def sum_kernel(blocks, query, key, value, out):
    total = blocks[0].astype(FULL)
    for d in range(1, blocks.shape[0]):
        total = total + blocks[d].astype(FULL)
    write_sums(total, query, key, value, out)


def on_device(
    tokens,
    lengths,
    routes,
    norm_attn,
    w_query,
    w_key,
    w_value,
    w_attn_out,
    norm_moe,
    w_router,
    w_expert_in,
    w_expert_out,
    cotangent,
):
    owners = lax.axis_size("dp")
    expert_index = lax.axis_index("dp")
    piece_index = lax.axis_index("tensor")
    piece_rows, width = tokens.shape
    shard, local = w_query.shape
    experts = w_router.shape[1]
    capacity = 3 * piece_rows // (2 * experts)
    slots = experts * capacity
    heads = local // HEAD_DIM
    total_rows = 4 * piece_rows
    small_rows = -(-(experts + 2) // 16) * 16
    scalars = jnp.concatenate(
        [jnp.stack([expert_index, piece_index]).astype(jnp.int32), lengths[0]]
    )
    sequences = lengths.shape[1]

    (packed,) = kernel_call(
        pack_kernel, [((shard + small_rows, 4 * local), LOW)], "pack", fetch=range(7)
    )(
        w_query,
        w_key,
        w_value,
        w_attn_out,
        w_router.T,
        norm_attn.reshape(1, shard),
        norm_moe.reshape(1, shard),
    )
    has_blocks = shard % 16 == 0
    scratch = []
    if has_blocks:
        behind, ahead, top, bottom = ring_gather(packed)
        partial = kernel_call(
            functools.partial(assemble_kernel, owners),
            [((width, 4 * local), LOW), ((owners, small_rows, shard), FULL)],
            "assemble",
            smem=(0,),
        )(scalars, packed, *behind, *ahead)
        blocks = [*partial, top, bottom]
        early = behind[0]
        scratch = [pltpu.VMEM((owners, small_rows, shard), FULL)]
    else:
        gathered = lax.all_gather(packed, "dp", axis=0, tiled=False)
        flat = gathered[:, shard:, :shard].transpose(1, 0, 2).reshape(small_rows, width)
        blocks = [gathered[:, :shard].reshape(width, 4 * local), flat.astype(FULL)]
        early = packed
    token_far = swap_far(after(tokens, early))
    token_near = swap_near(after(tokens, early))

    spread, cot_rows = kernel_call(
        functools.partial(spread_kernel, capacity, slots),
        [((piece_rows, slots), LOW), ((slots, width), LOW)],
        "spread",
        smem=(0,),
        fetch=(1, 2),
        store=(0, 1),
        time=2,
    )(scalars, routes, after(cotangent, early))
    token_near_far = swap_near(after(token_far, spread))

    cot_own = exchange(after(cot_rows, blocks[0]).reshape(experts, capacity, width))
    cot_own = cot_own.reshape(slots, width)

    outs = [
        ((piece_rows, width), FULL),
        ((piece_rows, width), FULL),
        ((piece_rows, width), LOW),
        ((piece_rows, width), LOW),
        ((total_rows, width), LOW),
        ((total_rows, 3 * local), LOW),
        ((total_rows, local), LOW),
        ((heads, total_rows, total_rows), FULL),
        ((total_rows, width), LOW),
    ]
    if has_blocks:
        outs += [((width, 4 * local), LOW), ((small_rows, width), FULL)]
    made = kernel_call(
        functools.partial(attend_kernel, owners, sequences, has_blocks),
        outs,
        "attend",
        smem=(0,),
        fetch=(1,),
        scratch=scratch,
        time=4,
    )(scalars, tokens, token_far, token_near, token_near_far, *blocks)
    keep, keep_far, send, send_far = made[:4]
    weights, small = made[9:] if has_blocks else blocks

    def scatter(keep_far, send, send_far, *others):
        near_far = swap_near(send_far)
        near = swap_near(send)
        (out,) = kernel_call(far_kernel, [(keep_far.shape, LOW)], "far")(
            keep_far, after(near_far, *others)
        )
        return near, swap_far(out), out

    near, far, mark = scatter(keep_far, send, send_far, cot_own)
    ones, qkv, attended, probs, group, weights_kept, small_kept = save(
        after(made[4], mark), *made[5:9], weights, small
    )
    tokens_here, spread_here = load(after(tokens, mark), spread)
    middle, own_rows = kernel_call(
        functools.partial(middle_kernel, experts + 1),
        [((piece_rows, width), FULL), ((slots, width), LOW)],
        "middle",
    )(tokens_here, keep, near, after(far, ones, spread_here), small, spread_here)
    (middle_kept,) = save(after(middle, own_rows))

    def over_dp(rows):
        return exchange(rows.reshape(experts, capacity, width)).reshape(slots, width)

    own = over_dp(own_rows)
    cot_far = swap_far(after(cot_own, own_rows))
    cot_near = swap_near(cot_own)
    cot_near_far = swap_near(cot_far)
    own_far = swap_far(after(own, cot_near_far))
    own_near = swap_near(own)
    weight_in = w_expert_in[0]
    weight_out = w_expert_out[0]
    hidden_size = weight_in.shape[1]

    def expert_part(x_keep, x_send, cot_keep, cot_send):
        rows = 2 * slots
        return kernel_call(
            functools.partial(expert_kernel, experts),
            [
                ((slots, width), FULL),
                ((slots, width), LOW),
                ((rows, hidden_size), LOW),
                ((rows, hidden_size), LOW),
                ((rows, width), LOW),
                ((rows, 1), FULL),
                ((experts, width), FULL),
                ((rows, width), LOW),
            ],
            "expert",
            smem=(0,),
            time=4,
            scratch=[pltpu.VMEM((rows, width), LOW)],
        )(scalars, x_keep, x_send, cot_keep, cot_send, weight_in, weight_out, small)

    small = small_kept
    keep, send, active_one, hidden_one, buffer_one, gate_one, router_one, rows_one = expert_part(
        own, own_near, cot_own, cot_near
    )
    keep_far, send_far, active_two, hidden_two, buffer_two, gate_two, router_two, rows_two = (
        expert_part(own_far, swap_near(after(own_far, send)), cot_far, cot_near_far)
    )
    near, far, mark = scatter(keep_far, send, send_far)
    forward_keep, forward_send, forward_keep_far, forward_send_far = kernel_call(
        forward_kernel,
        [((slots, width), kind) for kind in (FULL, LOW, FULL, LOW)],
        "forward",
        time=2,
    )(active_one, gate_one, active_two, gate_two, after(weight_out, mark))
    (grad_expert_out,) = kernel_call(
        grad_w_kernel, [((1, *weight_out.shape), FULL)], "grad_out", store=(0,), time=3
    )(active_one, active_two, after(buffer_one, forward_send), buffer_two)
    (back_rows,) = kernel_call(join_kernel, [((slots, width), LOW)], "join")(
        keep, near, after(far, grad_expert_out)
    )
    back = over_dp(back_rows)
    out_near, out_far, out_mark = scatter(
        forward_keep_far, forward_send, after(forward_send_far, back_rows)
    )
    (grad_expert_in,) = kernel_call(
        grad_w_kernel, [((1, *weight_in.shape), FULL)], "grad_in", store=(0,), time=3
    )(rows_one, rows_two, after(hidden_one, out_mark), hidden_two)
    middle_here, cot_here, spread_here, small_here = load(
        after(middle_kept, out_mark), cotangent, spread, small_kept
    )
    (out_rows,) = kernel_call(join_kernel, [((slots, width), LOW)], "join")(
        forward_keep, out_near, out_far
    )

    grad_middle, grad_low, grad_gain_two = kernel_call(
        functools.partial(back_kernel, experts + 1),
        [((piece_rows, width), FULL), ((piece_rows, width), LOW), ((1, width), FULL)],
        "back",
    )(middle_here, cot_here, spread_here, after(back, grad_expert_in), small_here)
    grad_far = swap_far(grad_low)
    grad_near = swap_near(grad_low)
    out_back = over_dp(after(out_rows, grad_near))
    (grad_middle_kept,) = save(after(grad_middle, grad_low))
    here = load(
        *(after(ones, grad_low), qkv, attended, probs, weights_kept, group)
    )
    grad_near_far = swap_near(grad_far)
    keep, keep_far, send, send_far, grad_w, payload = kernel_call(
        functools.partial(attend_back_kernel, experts),
        [
            ((piece_rows, width), FULL),
            ((piece_rows, width), FULL),
            ((piece_rows, width), LOW),
            ((piece_rows, width), LOW),
            ((width, 4 * local), LOW),
            ((owners, small_rows, shard), FULL),
        ],
        "attend_back",
        store=(0,),
        time=5,
        scratch=[pltpu.VMEM((total_rows, 3 * local), LOW), pltpu.VMEM((total_rows, width), LOW)],
    )(
        grad_low,
        grad_far,
        grad_near,
        grad_near_far,
        *here,
        router_one,
        router_two,
        grad_gain_two,
    )
    last = [((shard, local), FULL)] * 3 + [((local, shard), FULL)]
    near, far, mark = scatter(keep_far, send, send_far)
    marks = [mark] * 4
    if has_blocks:
        ahead, behind, marks = ring_reduce(grad_w, scalars, (shard, 4 * local))
        grad_query, grad_key, grad_value, grad_out = kernel_call(
            functools.partial(ring_last_kernel, owners),
            last,
            "ring_last",
            smem=(0,),
            store=range(4),
        )(scalars, grad_w, ahead, behind)
    else:
        grad_query, grad_key, grad_value, grad_out = kernel_call(
            sum_kernel, last, "sum", store=range(4)
        )(exchange(grad_w.reshape(owners, shard, 4 * local)))
    payload = payload + swap(payload, "tensor", 1)
    payload = payload + swap(payload, "tensor", 2)
    sums = jnp.sum(after(exchange(after(payload, marks[1], out_back)), marks[2]), axis=0)
    (grad_tokens,) = kernel_call(
        functools.partial(last_kernel, experts),
        [((piece_rows, width), FULL)],
        "last",
        fetch=(0, 1, 4, 5),
        store=(0,),
    )(tokens, keep, near, far, after(grad_middle_kept, marks[3]), small_kept)
    (result,) = kernel_call(
        result_kernel, [((piece_rows, width), LOW)], "result", fetch=(0, 1), store=(0,)
    )(after(middle_kept, marks[3]), spread, out_back)
    return (
        result,
        grad_tokens,
        sums[experts],
        grad_query,
        grad_key,
        grad_value,
        grad_out,
        sums[experts + 1],
        sums[:experts].T,
        grad_expert_in,
        grad_expert_out,
    )


def solution(mesh):
    return jax.shard_map(
        on_device,
        mesh=mesh,
        in_specs=(
            P(("dp", "tensor"), None),
            P("dp", None),
            P("dp", None),
            P("dp"),
            P("dp", "tensor"),
            P("dp", "tensor"),
            P("dp", "tensor"),
            P("tensor", "dp"),
            P("dp"),
            P("dp", None),
            P("dp", None, "tensor"),
            P("dp", "tensor", None),
            P(("dp", "tensor"), None),
        ),
        out_specs=(
            P(("dp", "tensor"), None),
            P(("dp", "tensor"), None),
            P("dp"),
            P("dp", "tensor"),
            P("dp", "tensor"),
            P("dp", "tensor"),
            P("tensor", "dp"),
            P("dp"),
            P("dp", None),
            P("dp", None, "tensor"),
            P("dp", "tensor", None),
        ),
        check_vma=False,
    )
```

```python
import functools

import jax
import jax.numpy as jnp
from jax import lax
from jax.experimental import pallas as pl
from jax.experimental.pallas import tpu as pltpu
from jax.sharding import PartitionSpec as P

HEAD_DIM = 64
EPSILON = 1e-06
NEGATIVE = -1e30
LOW = jnp.bfloat16
FULL = jnp.float32
SCALE = HEAD_DIM ** (-0.5)
MIB = 1 << 20


def dot(a, b):
    return jnp.dot(a, b, preferred_element_type=FULL)


def dot_nt(a, b):
    return lax.dot_general(a, b, (((1,), (1,)), ((), ())), preferred_element_type=FULL)


def dot_tn(a, b):
    return lax.dot_general(a, b, (((0,), (0,)), ((), ())), preferred_element_type=FULL)


class Fetched:
    def __init__(self, ref, held, sem):
        self.held, self.waiting = held, True
        self.copy = pltpu.make_async_copy(ref, held, sem)
        self.copy.start()
        self.shape = held.shape

    def wait(self):
        if self.waiting:
            self.copy.wait()
            self.waiting = False

    def __getitem__(self, index):
        self.wait()
        return self.held[index]


class Stored:
    def __init__(self, ref, held, sem):
        self.ref, self.held, self.sem = ref, held, sem
        self.copy = None
        self.shape, self.dtype = held.shape, held.dtype

    def __getitem__(self, index):
        return self.held[index]

    def __setitem__(self, index, value):
        self.held[index] = value

    def flush(self):
        if self.copy is None:
            self.copy = pltpu.make_async_copy(self.held, self.ref, self.sem)
            self.copy.start()


def kernel_call(body, outs, name, fetch=(), store=(), smem=(), time=1, limit=24, scratch=(), raw=(), alias=(), wait=(), wait_hbm=()):
    def call(*operands):
        n_in, n_out, n_scratch = len(operands), len(outs), len(scratch)
        held = [pltpu.VMEM(operands[i].shape, operands[i].dtype) for i in fetch]
        held += [pltpu.VMEM(*outs[i]) for i in store]
        sems = [pltpu.SemaphoreType.DMA((len(held),))] if held else []

        def kernel(*refs):
            ins, refs = list(refs[:n_in]), refs[n_in + len(wait) + len(wait_hbm) :]
            results, rest = list(refs[:n_out]), refs[n_out:]
            own, buffers = rest[:n_scratch], rest[n_scratch : n_scratch + len(held)]
            sem = rest[-1] if held else None
            at = 0
            for i in fetch:
                ins[i] = Fetched(ins[i], buffers[at], sem.at[at])
                at += 1
            for i in store:
                results[i] = Stored(results[i], buffers[at], sem.at[at])
                at += 1
            body(*ins, *results, *own)
            for i in fetch:
                ins[i].wait()
            for i in store:
                results[i].flush()
            for i in store:
                results[i].copy.wait()

        def spec(i, hbm):
            return pl.BlockSpec(memory_space=pltpu.HBM if i in hbm else pltpu.VMEM)

        kept = (*store, *raw)

        operands = [
            pltpu.with_memory_space_constraint(x, pltpu.HBM) if i in fetch else x
            for i, x in enumerate(operands)
        ]
        return pl.pallas_call(
            kernel,
            out_shape=[
                pltpu.HBM(*outs[i]) if i in kept else jax.ShapeDtypeStruct(*outs[i])
                for i in range(n_out)
            ],
            in_specs=[
                pl.BlockSpec(memory_space=pltpu.SMEM) if i in smem else spec(i, fetch)
                for i in range(n_in)
            ]
            + [pl.BlockSpec(memory_space=pl.ANY) for _ in wait]
            + [pl.BlockSpec(memory_space=pltpu.HBM) for _ in wait_hbm],
            out_specs=[spec(i, kept) for i in range(n_out)],
            input_output_aliases=dict(alias),
            scratch_shapes=[*scratch, *held, *sems],
            compiler_params=pltpu.CompilerParams(vmem_limit_bytes=limit * MIB),
            cost_estimate=pl.CostEstimate(
                flops=int(time * 1.1e9), bytes_accessed=MIB, transcendentals=0
            ),
            name=name,
        )(
            *operands,
            *wait,
            *(pltpu.with_memory_space_constraint(x, pltpu.HBM) for x in wait_hbm),
        )

    return call


def move_kernel(count, *refs):
    sources, targets, sem = refs[:count], refs[-1 - count : -1], refs[-1]
    copies = [
        pltpu.make_async_copy(source, target, sem.at[k])
        for k, (source, target) in enumerate(zip(sources, targets))
    ]
    for copy in copies:
        copy.start()
    for copy in copies:
        copy.wait()


def moved(arrays, source, target, name, wait):
    kinds = [(x.shape, x.dtype) for x in arrays]
    if source is pltpu.HBM:
        arrays = [pltpu.with_memory_space_constraint(x, pltpu.HBM) for x in arrays]
    return pl.pallas_call(
        functools.partial(move_kernel, len(kinds)),
        out_shape=[
            pltpu.HBM(*kind) if target is pltpu.HBM else jax.ShapeDtypeStruct(*kind)
            for kind in kinds
        ],
        in_specs=[pl.BlockSpec(memory_space=source) for _ in kinds]
        + [pl.BlockSpec(memory_space=pl.ANY) for _ in wait],
        out_specs=[pl.BlockSpec(memory_space=target) for _ in kinds],
        scratch_shapes=[pltpu.SemaphoreType.DMA((len(kinds),))],
        compiler_params=pltpu.CompilerParams(vmem_limit_bytes=16 * MIB),
        cost_estimate=pl.CostEstimate(flops=2 * 10**9, bytes_accessed=MIB, transcendentals=0),
        name=name,
    )(*arrays, *wait)


def save(*arrays, wait=()):
    return moved(arrays, pltpu.VMEM, pltpu.HBM, "save", wait)


def load(*arrays, wait=()):
    return moved(arrays, pltpu.HBM, pltpu.VMEM, "load", wait)


def swap(values, axis, bit):
    count = lax.axis_size(axis)
    return lax.ppermute(values, axis, [(i, i ^ bit) for i in range(count)])


def exchange(buffer):
    return lax.all_to_all(buffer, "dp", split_axis=0, concat_axis=0, tiled=True)


OFFSETS = (0, 2, 1, 3)


def swap_far(rows):
    return swap(rows, "tensor", 2)


def swap_near(rows):
    return swap(rows, "tensor", 1)


def ring_source(place, count):
    place = lax.rem(place + 2 * count, count)
    return jnp.where(place < count // 2, 2 * place, 2 * (count - 1 - place) + 1)


def ring_perms(count):
    order = list(range(0, count, 2)) + list(range(1, count, 2))[::-1]
    right = [(order[k], order[(k + 1) % count]) for k in range(count)]
    return right, [(b, a) for a, b in right]


def ring_gather(block):
    count = lax.axis_size("dp")
    right, left = ring_perms(count)
    behind, ahead = [block], [block]
    for _ in range(1, count // 2):
        behind.append(lax.ppermute(behind[-1], "dp", right))
        ahead.append(lax.ppermute(ahead[-1], "dp", left))
    middle = block.shape[0] // 32 * 16
    top = lax.ppermute(behind[-1][:middle], "dp", right)
    bottom = lax.ppermute(ahead[-1][middle:], "dp", left)
    return behind[1:], ahead[1:], top, bottom


def ring_place(me, count):
    return jnp.where(lax.rem(me, 2) == 0, me // 2, count - 1 - me // 2)


def fence_kernel(source, out):
    out[...] = source[0 : out.shape[0], 0 : out.shape[1]].astype(out.dtype)


def fence(source, wait=()):
    (out,) = kernel_call(fence_kernel, [((16, 128), LOW)], "fence", time=40, wait=wait)(source)
    return out


def add_kernel(*refs):
    total = refs[0][...].astype(FULL)
    for ref in refs[1:-1]:
        total = total + ref[...].astype(FULL)
    refs[-1][...] = total.astype(refs[-1].dtype)


def add(*values, wait=()):
    kind = (values[0].shape, values[0].dtype)
    return kernel_call(add_kernel, [kind], "add", time=0.1, wait=wait)(*values)[0]


def ring_reduce(top, bottom, rest, shard, fillers, arrived=()):
    count = lax.axis_size("dp")
    right, left = ring_perms(count)
    width = rest.shape[1]
    ahead = lax.ppermute(top, "dp", right)
    behind = lax.ppermute(bottom, "dp", left)
    done = ()
    for index, step in enumerate(range(count // 2 - 1, -1, -1)):
        if index < len(fillers):
            done, arrived = fillers[index](fence(rest, arrived))
        if not step:
            return rest, ahead, behind
        block = (shard, width)
        to_right, to_left, rest = kernel_call(
            ring_add_kernel,
            [(block, LOW), (block, LOW), ((rest.shape[0] - 2 * shard, width), LOW)],
            "ring_add",
            wait=done,
        )(rest, ahead, behind)
        ahead = lax.ppermute(to_right, "dp", right)
        behind = lax.ppermute(to_left, "dp", left)


def root_of(values):
    return lax.rsqrt(jnp.mean(values * values, axis=1, keepdims=True) + EPSILON)


def pack_kernel(wq, wk, wv, wo, router, gain_one, gain_two, out):
    shard, local = wq.shape
    out[0:shard, 0:local] = wq[...]
    out[0:shard, local : 2 * local] = wk[...]
    out[0:shard, 2 * local : 3 * local] = wv[...]
    out[0:shard, 3 * local :] = wo[...].astype(FULL).T.astype(LOW)
    experts = router.shape[0]
    rows = out.shape[0] - shard
    small = jnp.concatenate(
        [
            router[...].astype(FULL),
            gain_one[...].astype(FULL),
            gain_two[...].astype(FULL),
            jnp.zeros((rows - experts - 2, shard), FULL),
        ],
        axis=0,
    )
    out[shard:, :] = jnp.zeros((rows, out.shape[1]), LOW)
    out[shard:, 0:shard] = small.astype(LOW)


def spread_kernel(capacity, slots, scalars, routes, cot, spread, rows):
    count = cot.shape[0]
    piece = scalars[1]
    route = routes[pl.ds(pl.multiple_of(piece * count, count), count), :]
    experts = slots // capacity
    ids = lax.broadcasted_iota(jnp.int32, (count, experts), 1)
    chosen = jnp.where(route == ids, 1.0, 0.0)
    first = lax.broadcasted_iota(jnp.int32, (count, count), 0)
    second = lax.broadcasted_iota(jnp.int32, (count, count), 1)
    before = jnp.where(second < first, 1.0, 0.0).astype(LOW)
    earlier = dot(before, chosen.astype(LOW))
    slot = jnp.sum(earlier * chosen, axis=1, keepdims=True).astype(jnp.int32)
    place = route * capacity + slot
    lanes = lax.broadcasted_iota(jnp.int32, (count, slots), 1)
    one_hot = jnp.where(place == lanes, 1.0, 0.0).astype(LOW)
    spread[...] = one_hot
    rows[...] = dot_tn(one_hot, cot[...]).astype(LOW)


def assemble_kernel(count, scalars, *refs):
    blocks, (weights, smalls) = refs[:-2], refs[-2:]
    me = scalars[0]
    place = ring_place(me, count)
    shard = weights.shape[0] // count
    half = count // 2
    steps = [0] + [-s for s in range(1, half)] + list(range(1, half))
    for step, block in zip(steps, blocks):
        source = ring_source(place + step, count) if step else me
        weights[pl.ds(pl.multiple_of(source * shard, 16), shard), :] = block[0:shard, :]
        smalls[source] = block[shard:, 0:shard].astype(FULL)


def finish_small(count, scalars, blocks, smalls, small_out):
    smalls[...] = blocks[1][...]
    top, bottom = blocks[2:]
    shard = smalls.shape[2]
    source = ring_source(ring_place(scalars[0], count) + count // 2, count)
    smalls[source] = bottom[shard - top.shape[0] :, 0:shard].astype(FULL)
    for d in range(count):
        small_out[:, d * shard : (d + 1) * shard] = smalls[d]


def finish(count, scalars, blocks, weights_out, sem):
    weights = blocks[0]
    shard = weights.shape[0] // count
    top, bottom = blocks[2:]
    source = ring_source(ring_place(scalars[0], count) + count // 2, count)
    middle = top.shape[0]
    start = pl.multiple_of(source * shard, 16)
    rest = shard - middle
    weights.wait()
    weights.held[pl.ds(start, middle), :] = top[...]
    weights.held[pl.ds(pl.multiple_of(start + middle, 16), rest), :] = bottom[0:rest, :]
    copy = pltpu.make_async_copy(
        weights.held.at[pl.ds(start, shard), :], weights_out.at[pl.ds(start, shard), :], sem
    )
    copy.start()
    return copy


def positions_of(piece, rows, shape, dim):
    index = lax.broadcasted_iota(jnp.int32, shape, dim)
    block = index // rows
    flip = jnp.where(block == 1, 2, jnp.where(block == 2, 1, block))
    return (piece ^ flip) * rows + lax.rem(index, rows)


def attend_kernel(count, sequences, has_blocks, *refs):
    scalars, tokens, far, near, near_far = refs[:5]
    given = 4 if has_blocks else 2
    blocks = refs[5 : 5 + given]
    outs = refs[5 + given :]
    heads = len(outs) - (12 if has_blocks else 8)
    keep, keep_far, send, send_far, ones, qkv_out, attended, group = outs[:8]
    probs_out = outs[8 : 8 + heads]
    copy = None
    if has_blocks:
        weights_out, small_out, smalls, sem = outs[8 + heads :]
        finish_small(count, scalars, blocks, smalls, small_out)
        weights, small = blocks[0], small_out
    else:
        weights, small = blocks
    rows = tokens.shape[0]
    total = 4 * rows
    local = attended.shape[1]
    experts = count
    gain = small[experts : experts + 1, :]
    piece = scalars[1]
    for index, ref in enumerate((tokens, far, near, near_far)):
        group[index * rows : (index + 1) * rows, :] = ref[...]
        values = ref[...].astype(FULL)
        ones[index * rows : (index + 1) * rows, :] = (values * root_of(values) * gain).astype(LOW)
    if has_blocks:
        copy = finish(count, scalars, blocks, weights_out, sem)
    qkv = dot(ones[...], weights[:, 0 : 3 * local]).astype(LOW)
    qkv_out[...] = qkv
    query_pos = positions_of(piece, rows, (total, 1), 0)
    key_pos = positions_of(piece, rows, (1, total), 1)
    start = jnp.zeros((total, 1), jnp.int32)
    end = jnp.int32(0)
    for s in range(sequences):
        end = end + scalars[2 + s]
        start = jnp.where(query_pos >= end, end, start)
    bias = jnp.where((key_pos <= query_pos) & (key_pos >= start), 0.0, NEGATIVE)
    for h in range(local // HEAD_DIM):
        at = h * HEAD_DIM
        q = qkv[:, at : at + HEAD_DIM]
        k = qkv[:, local + at : local + at + HEAD_DIM]
        v = qkv[:, 2 * local + at : 2 * local + at + HEAD_DIM]
        scores = dot_nt(q, k) * SCALE + bias
        shifted = jnp.exp(scores - jnp.max(scores, axis=1, keepdims=True))
        probs = (shifted * (1.0 / jnp.sum(shifted, axis=1, keepdims=True))).astype(LOW)
        probs_out[h][...] = probs
        attended[:, at : at + HEAD_DIM] = dot(probs, v).astype(LOW)
    qkv_out.flush()
    for probs in probs_out:
        probs.flush()
    w_out_t = weights[:, 3 * local :]
    keep[...] = dot_nt(attended[0:rows, :], w_out_t)
    keep_far[...] = dot_nt(attended[rows : 2 * rows, :], w_out_t)
    send[...] = dot_nt(attended[2 * rows : 3 * rows, :], w_out_t).astype(LOW)
    send_far[...] = dot_nt(attended[3 * rows :, :], w_out_t).astype(LOW)
    if copy is not None:
        copy.wait()


def middle_kernel(gain_row, tokens, keep, near, far, small, spread, middle, rows):
    total = tokens[...].astype(FULL) + (
        keep[...] + near[...].astype(FULL) + far[...].astype(FULL)
    )
    middle[...] = total
    moe = (total * root_of(total) * small[gain_row : gain_row + 1, :]).astype(LOW)
    rows[...] = dot_tn(spread[...], moe).astype(LOW)


def far_kernel(keep_far, near, out):
    out[...] = (keep_far[...] + near[...].astype(FULL)).astype(LOW)


GELU_A = 0.7978845608028654
GELU_B = 0.044715


def flush(ref):
    if isinstance(ref, Stored):
        ref.flush()


def expert_kernel(
    experts,
    scalars,
    x_keep,
    x_send,
    cot_keep,
    cot_send,
    w_in,
    w_out,
    small,
    part_keep,
    part_send,
    active_out,
    hidden_out,
    buffer_out,
    gate_out,
    router_out,
    x,
    cot,
):
    rows = x_keep.shape[0]
    x[0:rows, :] = x_keep[...]
    x[rows:, :] = x_send[...]
    cot[0:rows, :] = cot_keep[...]
    cot[rows:, :] = cot_send[...]
    flush(x)
    hidden = dot(x[...], w_in[...])
    pulled = dot_nt(cot[...], w_out[...])
    router_t = small[0:experts, :].astype(LOW)
    mine = lax.broadcasted_iota(jnp.int32, (2 * rows, experts), 1) == scalars[0]
    logits = dot_nt(x[...], router_t)
    raised = jnp.exp(logits - jnp.max(logits, axis=1, keepdims=True))
    chances = raised / jnp.sum(raised, axis=1, keepdims=True)
    gate = jnp.sum(jnp.where(mine, chances, 0.0), axis=1, keepdims=True)
    square = hidden * hidden
    wave = jnp.tanh(GELU_A * hidden * (1.0 + GELU_B * square))
    half = 0.5 + 0.5 * wave
    active = (hidden * half).astype(LOW)
    active_out[...] = active
    slope = half + 0.5 * GELU_A * hidden * (1.0 - wave * wave) * (1.0 + 3.0 * GELU_B * square)
    grad_hidden = (gate * pulled * slope).astype(LOW)
    hidden_out[...] = grad_hidden
    flush(hidden_out)
    grad_gate = jnp.sum(active.astype(FULL) * pulled, axis=1, keepdims=True)
    grad_logits = (gate * grad_gate * (jnp.where(mine, 1.0, 0.0) - chances)).astype(LOW)
    buffer_out[...] = (gate * cot[...].astype(FULL)).astype(LOW)
    gate_out[...] = gate
    router_out[...] = dot_tn(grad_logits, x[...])
    flush(router_out)
    part = dot_nt(grad_hidden, w_in[...]) + dot(grad_logits, router_t)
    part_keep[...] = part[0:rows, :]
    part_send[...] = part[rows:, :].astype(LOW)


def forward_kernel(
    first, first_gate, second, second_gate, w_out, keep, send, keep_far, send_far
):
    rows = keep.shape[0]
    part = second_gate[...] * dot(second[...], w_out[...])
    keep_far[...] = part[0:rows, :]
    send_far[...] = part[rows:, :].astype(LOW)
    part = first_gate[...] * dot(first[...], w_out[...])
    keep[...] = part[0:rows, :]
    keep.flush()
    send[...] = part[rows:, :].astype(LOW)


def join_kernel(keep, near, far, out):
    out[...] = (keep[...] + near[...].astype(FULL) + far[...].astype(FULL)).astype(LOW)


def grad_w_kernel(*refs):
    *parts, out = refs
    lefts, rights = parts[:-2], parts[-2:]

    def whole(parts):
        return jnp.concatenate([part[...] for part in parts], axis=0)

    out[0] = dot_tn(whole(lefts), whole(rights))


def back_kernel(gain_row, middle, cot, spread, back, small, grad_middle, grad_low, grad_gain):
    grad_two = dot(spread[...], back[...])
    values = middle[...]
    root = root_of(values)
    normed = values * root
    scaled = grad_two * small[gain_row : gain_row + 1, :]
    grad_gain[...] = jnp.sum(grad_two * normed, axis=0, keepdims=True)
    total = cot[...].astype(FULL) + root * (
        scaled - normed * jnp.mean(scaled * normed, axis=1, keepdims=True)
    )
    grad_middle[...] = total
    grad_low[...] = total.astype(LOW)


def attend_back_kernel(
    experts,
    heads,
    scalars,
    own,
    far,
    near,
    near_far,
    weights,
    qkv,
    attended,
    ones,
    group,
    *refs,
):
    probs = refs[:heads]
    router_one, router_two, gain_two, keep, keep_far, send, send_far, payload = refs[
        heads : heads + 8
    ]
    *ring_rows, grad_w, grads, joined, flipped = refs[heads + 8 :]
    rows = own.shape[0]
    local = attended.shape[1]
    joined[0:rows, :] = own[...]
    joined[rows : 2 * rows, :] = far[...]
    joined[2 * rows : 3 * rows, :] = near[...]
    joined[3 * rows :, :] = near_far[...]
    w_out_t = weights[:, 3 * local :]
    grad_attended = dot(joined[...], w_out_t).astype(LOW)
    for h in range(local // HEAD_DIM):
        at = h * HEAD_DIM
        q = qkv[:, at : at + HEAD_DIM]
        k = qkv[:, local + at : local + at + HEAD_DIM]
        v = qkv[:, 2 * local + at : 2 * local + at + HEAD_DIM]
        upstream = grad_attended[:, at : at + HEAD_DIM]
        grad_p = dot_nt(upstream, v)
        low = probs[h][...]
        p = low.astype(FULL)
        inner = jnp.sum(p * grad_p, axis=1, keepdims=True)
        grad_s = (p * (grad_p - inner)).astype(LOW)
        grads[:, at : at + HEAD_DIM] = (dot(grad_s, k) * SCALE).astype(LOW)
        flipped[at : at + HEAD_DIM, :] = dot_tn(q, grad_s) * SCALE
        flipped[local + at : local + at + HEAD_DIM, :] = dot_tn(upstream, low)
    grads[:, local:] = flipped[...].T.astype(LOW)
    grad_w[:, 3 * local :] = dot_tn(joined[...], attended[...]).astype(LOW)
    grad_w[:, 0 : 3 * local] = dot_tn(ones[...], grads[...]).astype(LOW)
    if ring_rows:
        top, bottom, rest = ring_rows
        middle = top.shape[0]
        shard = middle + bottom.shape[0]
        count = grad_w.shape[0] // shard
        place = ring_place(scalars[0], count)

        def start_of(step):
            return pl.multiple_of(ring_source(place + step, count) * shard, 16)

        start = start_of(count // 2)
        top[...] = grad_w[pl.ds(start, middle), :]
        bottom[...] = grad_w[pl.ds(pl.multiple_of(start + middle, 16), shard - middle), :]
        steps = [sign * k for k in range(count // 2 - 1, 0, -1) for sign in (1, -1)] + [0]
        for index, step in enumerate(steps):
            rest[index * shard : (index + 1) * shard, :] = grad_w[pl.ds(start_of(step), shard), :]
    w_qkv = weights[:, 0 : 3 * local]

    def normed(values):
        values = values.astype(FULL)
        return values * root_of(values)

    gain_one = None
    for index, out in enumerate((keep, keep_far, send, send_far)):
        part = dot_nt(grads[index * rows : (index + 1) * rows, :], w_qkv)
        out[...] = part.astype(out.dtype)
        if index == 0:
            out.flush()
        gain = jnp.sum(
            part * normed(group[index * rows : (index + 1) * rows, :]), axis=0, keepdims=True
        )
        gain_one = gain if gain_one is None else gain_one + gain
    owners, height, shard = payload.shape
    whole = jnp.concatenate(
        [
            router_one[...] + router_two[...],
            gain_one,
            gain_two[...],
            jnp.zeros((height - experts - 2, gain_one.shape[1]), FULL),
        ],
        axis=0,
    )
    for d in range(owners):
        payload[d] = whole[:, d * shard : (d + 1) * shard]


def last_kernel(
    experts,
    tokens,
    keep,
    near,
    far,
    grad_middle,
    small,
    middle,
    spread,
    back,
    grad_tokens,
    result,
):
    values = tokens[...].astype(FULL)
    root = root_of(values)
    normed = values * root
    grad_one = keep[...] + near[...].astype(FULL) + far[...].astype(FULL)
    scaled = grad_one * small[experts : experts + 1, :]
    grad_tokens[...] = grad_middle[...] + root * (
        scaled - normed * jnp.mean(scaled * normed, axis=1, keepdims=True)
    )
    grad_tokens.flush()
    result[...] = (middle[...] + dot(spread[...], back[...])).astype(LOW)


def ring_add_kernel(rest, ahead, behind, to_right, to_left, left_over):
    shard = to_right.shape[0]
    left_over[...] = rest[2 * shard :, :]
    if ahead.shape[0] == shard:
        to_right[...] = (rest[0:shard, :].astype(FULL) + ahead[...].astype(FULL)).astype(LOW)
        to_left[...] = (
            rest[shard : 2 * shard, :].astype(FULL) + behind[...].astype(FULL)
        ).astype(LOW)
        return
    middle = ahead.shape[0]
    to_right[0:middle, :] = (rest[0:middle, :].astype(FULL) + ahead[...].astype(FULL)).astype(LOW)
    to_right[middle:, :] = rest[middle:shard, :]
    to_left[0:middle, :] = rest[shard : shard + middle, :]
    to_left[middle:, :] = (
        rest[shard + middle : 2 * shard, :].astype(FULL) + behind[...].astype(FULL)
    ).astype(LOW)


def write_sums(total, query, key, value, out):
    local = query.shape[1]
    query[...] = total[:, 0:local]
    key[...] = total[:, local : 2 * local]
    value[...] = total[:, 2 * local : 3 * local]
    out[...] = total[:, 3 * local :].T


def ring_last_kernel(experts, mine, ahead, behind, parts, query, key, value, out, *small):
    total = mine[...].astype(FULL) + (ahead[...].astype(FULL) + behind[...].astype(FULL))
    write_sums(total, query, key, value, out)
    write_small(experts, parts, *small)


def write_small(experts, parts, gain_one, gain_two, router):
    total = jnp.sum(parts[...], axis=0)
    router[...] = total[0:experts, :]
    gain_one[...] = total[experts : experts + 1, :]
    gain_two[...] = total[experts + 1 : experts + 2, :]


def sum_kernel(experts, blocks, parts, query, key, value, out, *small):
    total = blocks[0].astype(FULL)
    for d in range(1, blocks.shape[0]):
        total = total + blocks[d].astype(FULL)
    write_sums(total, query, key, value, out)
    write_small(experts, parts, *small)


def on_device(
    tokens,
    lengths,
    routes,
    norm_attn,
    w_query,
    w_key,
    w_value,
    w_attn_out,
    norm_moe,
    w_router,
    w_expert_in,
    w_expert_out,
    cotangent,
):
    owners = lax.axis_size("dp")
    expert_index = lax.axis_index("dp")
    piece_index = lax.axis_index("tensor")
    piece_rows, width = tokens.shape
    shard, local = w_query.shape
    experts = w_router.shape[1]
    capacity = 3 * piece_rows // (2 * experts)
    slots = experts * capacity
    heads = local // HEAD_DIM
    total_rows = 4 * piece_rows
    small_rows = -(-(experts + 2) // 16) * 16
    scalars = jnp.concatenate(
        [jnp.stack([expert_index, piece_index]).astype(jnp.int32), lengths[0]]
    )
    sequences = lengths.shape[1]

    (packed,) = kernel_call(
        pack_kernel, [((shard + small_rows, 4 * local), LOW)], "pack", fetch=range(7)
    )(
        w_query,
        w_key,
        w_value,
        w_attn_out,
        w_router.T,
        norm_attn.reshape(1, shard),
        norm_moe.reshape(1, shard),
    )
    has_blocks = shard % 16 == 0
    scratch = []
    if has_blocks:
        behind, ahead, top, bottom = ring_gather(packed)
        partial = kernel_call(
            functools.partial(assemble_kernel, owners),
            [((width, 4 * local), LOW), ((owners, small_rows, shard), FULL)],
            "assemble",
            smem=(0,),
            store=(0,),
        )(scalars, packed, *behind, *ahead)
        blocks = [*partial, top, bottom]
        early = behind[0]
        scratch = [pltpu.VMEM((owners, small_rows, shard), FULL), pltpu.SemaphoreType.DMA]
    else:
        gathered = lax.all_gather(packed, "dp", axis=0, tiled=False)
        flat = gathered[:, shard:, :shard].transpose(1, 0, 2).reshape(small_rows, width)
        blocks = [gathered[:, :shard].reshape(width, 4 * local), flat.astype(FULL)]
        early = packed
    token_far = swap_far(tokens)
    token_near = swap_near(tokens)

    spread, cot_rows = kernel_call(
        functools.partial(spread_kernel, capacity, slots),
        [((piece_rows, slots), LOW), ((slots, width), LOW)],
        "spread",
        smem=(0,),
        fetch=(1, 2),
        store=(0,),
        time=2,
        wait=(early,),
    )(scalars, routes, cotangent)
    token_near_far = swap_near(token_far)

    cot_rows = add(cot_rows, wait=(blocks[1],))
    cot_own = exchange(cot_rows.reshape(experts, capacity, width))
    cot_own = cot_own.reshape(slots, width)

    outs = [
        ((piece_rows, width), FULL),
        ((piece_rows, width), FULL),
        ((piece_rows, width), LOW),
        ((piece_rows, width), LOW),
        ((total_rows, width), LOW),
        ((total_rows, 3 * local), LOW),
        ((total_rows, local), LOW),
        ((total_rows, width), LOW),
    ]
    outs += [((total_rows, total_rows), LOW)] * heads
    raw, alias, fetch = [], {}, [1]
    if has_blocks:
        outs += [((width, 4 * local), LOW), ((small_rows, width), FULL)]
        raw, alias, fetch = [len(outs) - 2], {5: len(outs) - 2}, [1, 5]
    made = kernel_call(
        functools.partial(attend_kernel, owners, sequences, has_blocks),
        outs,
        "attend",
        smem=(0,),
        fetch=fetch,
        store=(5, *range(8, 8 + heads)),
        raw=raw,
        alias=alias,
        scratch=scratch,
        time=4,
    )(scalars, tokens, token_far, token_near, token_near_far, *blocks)
    keep, keep_far, send, send_far = made[:4]
    ones, qkv, attended, group, *probs = made[4 : 8 + heads]
    weights, small = made[8 + heads :] if has_blocks else blocks

    def scatter(keep_far, send, send_far, wait=()):
        near_far = swap_near(send_far)
        near = swap_near(send)
        (out,) = kernel_call(far_kernel, [(keep_far.shape, LOW)], "far", time=0.1, wait=wait)(
            keep_far, near_far
        )
        return near, swap_far(out), out

    near, far, mark = scatter(keep_far, send, send_far)
    small_now = small
    ones, attended, group, small = save(ones, attended, group, small, wait=(mark,))
    tokens_here, spread_here = load(tokens, spread, wait=(mark, cot_own))
    middle, own_rows = kernel_call(
        functools.partial(middle_kernel, experts + 1),
        [((piece_rows, width), FULL), ((slots, width), LOW)],
        "middle",
        wait_hbm=(ones,),
    )(tokens_here, keep, near, far, small_now, spread_here)
    (middle,) = save(middle, wait=(own_rows,))

    def over_dp(rows):
        return exchange(rows.reshape(experts, capacity, width)).reshape(slots, width)

    own = over_dp(own_rows)
    cot_far = swap_far(cot_own)
    cot_near = swap_near(cot_own)
    cot_near_far = swap_near(cot_far)
    own_far = swap_far(own)
    own_near = swap_near(own)
    (small_expert,) = load(small, wait=(own_rows,))
    weight_in = w_expert_in[0]
    weight_out = w_expert_out[0]
    hidden_size = weight_in.shape[1]

    def expert_part(x_keep, x_send, cot_keep, cot_send, store):
        rows = 2 * slots
        return kernel_call(
            functools.partial(expert_kernel, experts),
            [
                ((slots, width), FULL),
                ((slots, width), LOW),
                ((rows, hidden_size), LOW),
                ((rows, hidden_size), LOW),
                ((rows, width), LOW),
                ((rows, 1), FULL),
                ((experts, width), FULL),
                ((rows, width), LOW),
            ],
            "expert",
            smem=(0,),
            store=store,
            time=4,
            scratch=[pltpu.VMEM((rows, width), LOW)],
        )(scalars, x_keep, x_send, cot_keep, cot_send, weight_in, weight_out, small_expert)

    keep, send, active_one, hidden_one, buffer_one, gate_one, router_one, rows_one = expert_part(
        own, own_near, cot_own, cot_near, (3, 6, 7)
    )
    own_far = add(own_far, wait=(send,))
    keep_far, send_far, active_two, hidden_two, buffer_two, gate_two, router_two, rows_two = (
        expert_part(own_far, swap_near(own_far), cot_far, cot_near_far, ())
    )
    near, far, mark = scatter(keep_far, send, send_far)
    rows_two, hidden_two, router_two = save(rows_two, hidden_two, router_two, wait=(mark,))
    forward_keep, forward_send, forward_keep_far, forward_send_far = kernel_call(
        forward_kernel,
        [((slots, width), kind) for kind in (FULL, LOW, FULL, LOW)],
        "forward",
        store=(0,),
        time=2,
        wait=(mark,),
    )(active_one, gate_one, active_two, gate_two, weight_out)
    (grad_expert_out,) = kernel_call(
        grad_w_kernel, [((1, *weight_out.shape), FULL)], "grad_out", store=(0,), time=3, wait=(mark,)
    )(active_one, active_two, buffer_one, buffer_two)
    (back_rows,) = kernel_call(
        join_kernel,
        [((slots, width), LOW)],
        "join",
        wait=(forward_send,),
        wait_hbm=(grad_expert_out, hidden_two),
    )(keep, near, far)
    back = over_dp(back_rows)
    out_near, out_far, out_mark = scatter(
        forward_keep_far, forward_send, forward_send_far, wait=(back_rows,)
    )
    (grad_expert_in,) = kernel_call(
        grad_w_kernel, [((1, *weight_in.shape), FULL)], "grad_in", fetch=range(4), store=(0,), time=3
    )(rows_one, rows_two, hidden_one, hidden_two)
    middle_here, cot_here, spread_here, small_here, forward_here = load(
        middle, cotangent, spread, small, forward_keep, wait=(out_mark,)
    )
    (out_rows,) = kernel_call(join_kernel, [((slots, width), LOW)], "join", time=0.1)(
        forward_here, out_near, out_far
    )
    out_back = over_dp(out_rows)

    grad_middle, grad_low, grad_gain_two = kernel_call(
        functools.partial(back_kernel, experts + 1),
        [((piece_rows, width), FULL), ((piece_rows, width), LOW), ((1, width), FULL)],
        "back",
        wait=(out_far,),
        wait_hbm=(grad_expert_in,),
    )(middle_here, cot_here, spread_here, back, small_here)
    grad_far = swap_far(grad_low)
    grad_near = swap_near(grad_low)
    (grad_middle,) = save(grad_middle)
    grad_far = add(grad_far, wait=(out_rows,))
    grad_near_far = swap_near(grad_far)
    outs = [
        ((piece_rows, width), FULL),
        ((piece_rows, width), FULL),
        ((piece_rows, width), LOW),
        ((piece_rows, width), LOW),
        ((owners, small_rows, shard), FULL),
    ]
    middle_row = shard // 32 * 16
    scratch = [
        pltpu.VMEM((total_rows, 3 * local), LOW),
        pltpu.VMEM((total_rows, width), LOW),
        pltpu.VMEM((2 * local, total_rows), FULL),
    ]
    if has_blocks:
        outs += [
            ((middle_row, 4 * local), LOW),
            ((shard - middle_row, 4 * local), LOW),
            ((width - shard, 4 * local), LOW),
        ]
        scratch = [pltpu.VMEM((width, 4 * local), LOW)] + scratch
    else:
        outs.append(((width, 4 * local), LOW))
    keep, keep_far, send, send_far, payload, *grad_w = kernel_call(
        functools.partial(attend_back_kernel, experts, heads),
        outs,
        "attend_back",
        smem=(0,),
        fetch=range(5, 12 + heads),
        store=(0,),
        time=2,
        scratch=scratch,
    )(
        scalars,
        grad_low,
        grad_far,
        grad_near,
        grad_near_far,
        *(weights, qkv, attended, ones, group, *probs, router_one, router_two),
        grad_gain_two,
    )
    last = [((shard, local), FULL)] * 3 + [((local, shard), FULL)]
    held = {}

    near_far, near = swap_near(send_far), swap_near(send)

    def first(mark):
        total = add(payload, swap(payload, "tensor", 1), wait=(mark,))
        came = swap(total, "tensor", 2)
        held["small"] = (total, came)
        return (total,), (came,)

    def second(mark):
        total = add(*held["small"], wait=(mark,))
        held["small"] = exchange(total)
        return (total,), ()

    def third(mark):
        (out,) = kernel_call(far_kernel, [(keep_far.shape, LOW)], "far", time=0.1, wait=(mark,))(
            keep_far, near_far
        )
        held["far"] = swap_far(out)
        return (out,), (held["far"],)

    def fourth(mark):
        held["last"] = kernel_call(
            functools.partial(last_kernel, experts),
            [
                ((piece_rows, width), FULL),
                ((piece_rows, width), LOW),
            ],
            "last",
            fetch=(0, 1, 4, 5, 6, 7),
            store=(0, 1),
            time=0.3,
            wait=(mark,),
        )(
            *(tokens, keep, near, held["far"], grad_middle, small, middle, spread, out_back)
        )
        return (), ()

    fillers = (first, second, third, fourth)
    last += [((1, shard), FULL), ((1, shard), FULL), ((experts, shard), FULL)]
    if has_blocks:
        parts = ring_reduce(*grad_w, shard, fillers, (out_back,))
        sums = kernel_call(
            functools.partial(ring_last_kernel, experts),
            last,
            "ring_last",
            store=range(7),
            wait_hbm=held["last"][:1],
        )(*parts, held["small"])
    else:
        for filler in fillers:
            filler(grad_w[0])
        sums = kernel_call(
            functools.partial(sum_kernel, experts), last, "sum", store=range(7)
        )(exchange(grad_w[0].reshape(owners, shard, 4 * local)), held["small"])
    grad_query, grad_key, grad_value, grad_out, grad_norm_attn, grad_norm_moe, grad_router = sums
    grad_tokens, result = held["last"]
    return (
        result,
        grad_tokens,
        grad_norm_attn.reshape(shard),
        grad_query,
        grad_key,
        grad_value,
        grad_out,
        grad_norm_moe.reshape(shard),
        grad_router.T,
        grad_expert_in,
        grad_expert_out,
    )


def solution(mesh):
    return jax.shard_map(
        on_device,
        mesh=mesh,
        in_specs=(
            P(("dp", "tensor"), None),
            P("dp", None),
            P("dp", None),
            P("dp"),
            P("dp", "tensor"),
            P("dp", "tensor"),
            P("dp", "tensor"),
            P("tensor", "dp"),
            P("dp"),
            P("dp", None),
            P("dp", None, "tensor"),
            P("dp", "tensor", None),
            P(("dp", "tensor"), None),
        ),
        out_specs=(
            P(("dp", "tensor"), None),
            P(("dp", "tensor"), None),
            P("dp"),
            P("dp", "tensor"),
            P("dp", "tensor"),
            P("dp", "tensor"),
            P("tensor", "dp"),
            P("dp"),
            P("dp", None),
            P("dp", None, "tensor"),
            P("dp", "tensor", None),
        ),
        check_vma=False,
    )
```

```python
import functools

import jax
import jax.numpy as jnp
from jax import lax
from jax.experimental import pallas as pl
from jax.experimental.pallas import tpu as pltpu
from jax.sharding import PartitionSpec as P

HEAD_DIM = 64
EPSILON = 1e-06
NEGATIVE = -1e30
LOW = jnp.bfloat16
FULL = jnp.float32
SCALE = HEAD_DIM ** (-0.5)
MIB = 1 << 20


def dot(a, b):
    return jnp.dot(a, b, preferred_element_type=FULL)


def dot_nt(a, b):
    return lax.dot_general(a, b, (((1,), (1,)), ((), ())), preferred_element_type=FULL)


def dot_tn(a, b):
    return lax.dot_general(a, b, (((0,), (0,)), ((), ())), preferred_element_type=FULL)


class Fetched:
    def __init__(self, ref, held, sem, late):
        self.held, self.waiting, self.late = held, True, late
        self.copy = pltpu.make_async_copy(ref, held, sem)
        self.shape = held.shape

    def wait(self):
        if self.waiting:
            self.copy.wait()
            self.waiting = False
            while self.late:
                self.late.pop(0).copy.start()

    def __getitem__(self, index):
        self.wait()
        return self.held[index]


class Stored:
    def __init__(self, ref, held, sem):
        self.ref, self.held, self.sem = ref, held, sem
        self.copy = None
        self.shape, self.dtype = held.shape, held.dtype

    def __getitem__(self, index):
        return self.held[index]

    def __setitem__(self, index, value):
        self.held[index] = value

    def flush(self):
        if self.copy is None:
            self.copy = pltpu.make_async_copy(self.held, self.ref, self.sem)
            self.copy.start()


def kernel_call(body, outs, name, fetch=(), store=(), smem=(), time=1, limit=24, scratch=(), raw=(), alias=(), wait=(), wait_hbm=(), first=99):
    def call(*operands):
        n_in, n_out, n_scratch = len(operands), len(outs), len(scratch)
        held = [pltpu.VMEM(operands[i].shape, operands[i].dtype) for i in fetch]
        held += [pltpu.VMEM(*outs[i]) for i in store]
        sems = [pltpu.SemaphoreType.DMA((len(held),))] if held else []

        def kernel(*refs):
            ins, refs = list(refs[:n_in]), refs[n_in + len(wait) + len(wait_hbm) :]
            results, rest = list(refs[:n_out]), refs[n_out:]
            own, buffers = rest[:n_scratch], rest[n_scratch : n_scratch + len(held)]
            sem = rest[-1] if held else None
            at, late = 0, []
            for i in fetch:
                ins[i] = Fetched(ins[i], buffers[at], sem.at[at], late)
                if at < first:
                    ins[i].copy.start()
                else:
                    late.append(ins[i])
                at += 1
            for i in store:
                results[i] = Stored(results[i], buffers[at], sem.at[at])
                at += 1
            body(*ins, *results, *own)
            for i in fetch:
                ins[i].wait()
            for i in store:
                results[i].flush()
            for i in store:
                results[i].copy.wait()

        def spec(i, hbm):
            return pl.BlockSpec(memory_space=pltpu.HBM if i in hbm else pltpu.VMEM)

        kept = (*store, *raw)

        operands = [
            pltpu.with_memory_space_constraint(x, pltpu.HBM) if i in fetch else x
            for i, x in enumerate(operands)
        ]
        return pl.pallas_call(
            kernel,
            out_shape=[
                pltpu.HBM(*outs[i]) if i in kept else jax.ShapeDtypeStruct(*outs[i])
                for i in range(n_out)
            ],
            in_specs=[
                pl.BlockSpec(memory_space=pltpu.SMEM) if i in smem else spec(i, fetch)
                for i in range(n_in)
            ]
            + [pl.BlockSpec(memory_space=pl.ANY) for _ in wait]
            + [pl.BlockSpec(memory_space=pltpu.HBM) for _ in wait_hbm],
            out_specs=[spec(i, kept) for i in range(n_out)],
            input_output_aliases=dict(alias),
            scratch_shapes=[*scratch, *held, *sems],
            compiler_params=pltpu.CompilerParams(vmem_limit_bytes=limit * MIB),
            cost_estimate=pl.CostEstimate(
                flops=int(time * 1.1e9), bytes_accessed=MIB, transcendentals=0
            ),
            name=name,
        )(
            *operands,
            *wait,
            *(pltpu.with_memory_space_constraint(x, pltpu.HBM) for x in wait_hbm),
        )

    return call


def move_kernel(count, *refs):
    sources, targets, sem = refs[:count], refs[-1 - count : -1], refs[-1]
    copies = [
        pltpu.make_async_copy(source, target, sem.at[k])
        for k, (source, target) in enumerate(zip(sources, targets))
    ]
    for copy in copies:
        copy.start()
    for copy in copies:
        copy.wait()


def moved(arrays, source, target, name, wait):
    kinds = [(x.shape, x.dtype) for x in arrays]
    if source is pltpu.HBM:
        arrays = [pltpu.with_memory_space_constraint(x, pltpu.HBM) for x in arrays]
    return pl.pallas_call(
        functools.partial(move_kernel, len(kinds)),
        out_shape=[
            pltpu.HBM(*kind) if target is pltpu.HBM else jax.ShapeDtypeStruct(*kind)
            for kind in kinds
        ],
        in_specs=[pl.BlockSpec(memory_space=source) for _ in kinds]
        + [pl.BlockSpec(memory_space=pl.ANY) for _ in wait],
        out_specs=[pl.BlockSpec(memory_space=target) for _ in kinds],
        scratch_shapes=[pltpu.SemaphoreType.DMA((len(kinds),))],
        compiler_params=pltpu.CompilerParams(vmem_limit_bytes=16 * MIB),
        cost_estimate=pl.CostEstimate(flops=2 * 10**9, bytes_accessed=MIB, transcendentals=0),
        name=name,
    )(*arrays, *wait)


def save(*arrays, wait=()):
    return moved(arrays, pltpu.VMEM, pltpu.HBM, "save", wait)


def load(*arrays, wait=()):
    return moved(arrays, pltpu.HBM, pltpu.VMEM, "load", wait)


def swap(values, axis, bit):
    count = lax.axis_size(axis)
    return lax.ppermute(values, axis, [(i, i ^ bit) for i in range(count)])


def exchange(buffer):
    return lax.all_to_all(buffer, "dp", split_axis=0, concat_axis=0, tiled=True)


OFFSETS = (0, 2, 1, 3)


def swap_far(rows):
    return swap(rows, "tensor", 2)


def swap_near(rows):
    return swap(rows, "tensor", 1)


def ring_source(place, count):
    place = lax.rem(place + 2 * count, count)
    return jnp.where(place < count // 2, 2 * place, 2 * (count - 1 - place) + 1)


def ring_perms(count):
    order = list(range(0, count, 2)) + list(range(1, count, 2))[::-1]
    right = [(order[k], order[(k + 1) % count]) for k in range(count)]
    return right, [(b, a) for a, b in right]


def ring_gather(block):
    count = lax.axis_size("dp")
    right, left = ring_perms(count)
    behind, ahead = [block], [block]
    for _ in range(1, count // 2):
        behind.append(lax.ppermute(behind[-1], "dp", right))
        ahead.append(lax.ppermute(ahead[-1], "dp", left))
    middle = block.shape[0] // 32 * 16
    top = lax.ppermute(behind[-1][:middle], "dp", right)
    bottom = lax.ppermute(ahead[-1][middle:], "dp", left)
    return behind[1:], ahead[1:], top, bottom


def ring_place(me, count):
    return jnp.where(lax.rem(me, 2) == 0, me // 2, count - 1 - me // 2)


def fence_kernel(source, out):
    out[...] = source[0 : out.shape[0], 0 : out.shape[1]].astype(out.dtype)


def fence(source, wait=()):
    (out,) = kernel_call(fence_kernel, [((16, 128), LOW)], "fence", time=40, wait=wait)(source)
    return out


def add_kernel(*refs):
    total = refs[0][...].astype(FULL)
    for ref in refs[1:-1]:
        total = total + ref[...].astype(FULL)
    refs[-1][...] = total.astype(refs[-1].dtype)


def add(*values, wait=(), wait_hbm=()):
    kind = (values[0].shape, values[0].dtype)
    return kernel_call(add_kernel, [kind], "add", time=0.1, wait=wait, wait_hbm=wait_hbm)(*values)[0]


def ring_reduce(top, bottom, rest, shard, fillers, arrived=()):
    count = lax.axis_size("dp")
    right, left = ring_perms(count)
    width = rest.shape[1]
    ahead = lax.ppermute(top, "dp", right)
    behind = lax.ppermute(bottom, "dp", left)
    done, kept = (), ()
    for index, step in enumerate(range(count // 2 - 1, -1, -1)):
        if index < len(fillers):
            done, arrived, kept = fillers[index](fence(rest, arrived))
        if not step:
            return rest, ahead, behind
        block = (shard, width)
        to_right, to_left, rest = kernel_call(
            ring_add_kernel,
            [(block, LOW), (block, LOW), ((rest.shape[0] - 2 * shard, width), LOW)],
            "ring_add",
            wait=done,
            wait_hbm=kept,
        )(rest, ahead, behind)
        ahead = lax.ppermute(to_right, "dp", right)
        behind = lax.ppermute(to_left, "dp", left)


def root_of(values):
    return lax.rsqrt(jnp.mean(values * values, axis=1, keepdims=True) + EPSILON)


def pack_kernel(wq, wk, wv, wo, router, gain_one, gain_two, out):
    shard, local = wq.shape
    out[0:shard, 0:local] = wq[...]
    out[0:shard, local : 2 * local] = wk[...]
    out[0:shard, 2 * local : 3 * local] = wv[...]
    out[0:shard, 3 * local :] = wo[...].astype(FULL).T.astype(LOW)
    experts = router.shape[0]
    rows = out.shape[0] - shard
    small = jnp.concatenate(
        [
            router[...].astype(FULL),
            gain_one[...].astype(FULL),
            gain_two[...].astype(FULL),
            jnp.zeros((rows - experts - 2, shard), FULL),
        ],
        axis=0,
    )
    out[shard:, :] = jnp.zeros((rows, out.shape[1]), LOW)
    out[shard:, 0:shard] = small.astype(LOW)


def spread_kernel(capacity, slots, scalars, routes, cot, spread, rows):
    count = cot.shape[0]
    piece = scalars[1]
    route = routes[pl.ds(pl.multiple_of(piece * count, count), count), :]
    experts = slots // capacity
    ids = lax.broadcasted_iota(jnp.int32, (count, experts), 1)
    chosen = jnp.where(route == ids, 1.0, 0.0)
    first = lax.broadcasted_iota(jnp.int32, (count, count), 0)
    second = lax.broadcasted_iota(jnp.int32, (count, count), 1)
    before = jnp.where(second < first, 1.0, 0.0).astype(LOW)
    earlier = dot(before, chosen.astype(LOW))
    slot = jnp.sum(earlier * chosen, axis=1, keepdims=True).astype(jnp.int32)
    place = route * capacity + slot
    lanes = lax.broadcasted_iota(jnp.int32, (count, slots), 1)
    one_hot = jnp.where(place == lanes, 1.0, 0.0).astype(LOW)
    spread[...] = one_hot
    rows[...] = dot_tn(one_hot, cot[...]).astype(LOW)


def assemble_kernel(count, scalars, *refs):
    blocks, (weights, smalls) = refs[:-2], refs[-2:]
    me = scalars[0]
    place = ring_place(me, count)
    shard = weights.shape[0] // count
    half = count // 2
    steps = [0] + [-s for s in range(1, half)] + list(range(1, half))
    for step, block in zip(steps, blocks):
        source = ring_source(place + step, count) if step else me
        weights[pl.ds(pl.multiple_of(source * shard, 16), shard), :] = block[0:shard, :]
        smalls[source] = block[shard:, 0:shard].astype(FULL)


def finish_small(count, scalars, blocks, smalls, small_out):
    smalls[...] = blocks[1][...]
    top, bottom = blocks[2:]
    shard = smalls.shape[2]
    source = ring_source(ring_place(scalars[0], count) + count // 2, count)
    smalls[source] = bottom[shard - top.shape[0] :, 0:shard].astype(FULL)
    for d in range(count):
        small_out[:, d * shard : (d + 1) * shard] = smalls[d]


def finish(count, scalars, blocks, weights_out, sem):
    weights = blocks[0]
    shard = weights.shape[0] // count
    top, bottom = blocks[2:]
    source = ring_source(ring_place(scalars[0], count) + count // 2, count)
    middle = top.shape[0]
    start = pl.multiple_of(source * shard, 16)
    rest = shard - middle
    weights.wait()
    weights.held[pl.ds(start, middle), :] = top[...]
    weights.held[pl.ds(pl.multiple_of(start + middle, 16), rest), :] = bottom[0:rest, :]
    copy = pltpu.make_async_copy(
        weights.held.at[pl.ds(start, shard), :], weights_out.at[pl.ds(start, shard), :], sem
    )
    copy.start()
    return copy


def positions_of(piece, rows, shape, dim):
    index = lax.broadcasted_iota(jnp.int32, shape, dim)
    block = index // rows
    flip = jnp.where(block == 1, 2, jnp.where(block == 2, 1, block))
    return (piece ^ flip) * rows + lax.rem(index, rows)


def attend_kernel(count, sequences, has_blocks, *refs):
    scalars, tokens, far, near, near_far = refs[:5]
    given = 4 if has_blocks else 2
    blocks = refs[5 : 5 + given]
    outs = refs[5 + given :]
    heads = len(outs) - (12 if has_blocks else 8)
    keep, keep_far, send, send_far, ones, qkv_out, attended, group = outs[:8]
    probs_out = outs[8 : 8 + heads]
    copy = None
    if has_blocks:
        weights_out, small_out, smalls, sem = outs[8 + heads :]
        finish_small(count, scalars, blocks, smalls, small_out)
        weights, small = blocks[0], small_out
    else:
        weights, small = blocks
    rows = tokens.shape[0]
    total = 4 * rows
    local = attended.shape[1]
    experts = count
    gain = small[experts : experts + 1, :]
    piece = scalars[1]
    for index, ref in ((1, far), (2, near), (3, near_far), (0, tokens)):
        group[index * rows : (index + 1) * rows, :] = ref[...]
        values = ref[...].astype(FULL)
        ones[index * rows : (index + 1) * rows, :] = (values * root_of(values) * gain).astype(LOW)
    if has_blocks:
        copy = finish(count, scalars, blocks, weights_out, sem)
    qkv = dot(ones[...], weights[:, 0 : 3 * local]).astype(LOW)
    qkv_out[...] = qkv
    qkv_out.flush()
    query_pos = positions_of(piece, rows, (total, 1), 0)
    key_pos = positions_of(piece, rows, (1, total), 1)
    start = jnp.zeros((total, 1), jnp.int32)
    end = jnp.int32(0)
    for s in range(sequences):
        end = end + scalars[2 + s]
        start = jnp.where(query_pos >= end, end, start)
    bias = jnp.where((key_pos <= query_pos) & (key_pos >= start), 0.0, NEGATIVE)
    for h in range(local // HEAD_DIM):
        at = h * HEAD_DIM
        q = qkv[:, at : at + HEAD_DIM]
        k = qkv[:, local + at : local + at + HEAD_DIM]
        v = qkv[:, 2 * local + at : 2 * local + at + HEAD_DIM]
        scores = dot_nt(q, k) * SCALE + bias
        shifted = jnp.exp(scores - jnp.max(scores, axis=1, keepdims=True))
        probs = (shifted * (1.0 / jnp.sum(shifted, axis=1, keepdims=True))).astype(LOW)
        probs_out[h][...] = probs
        attended[:, at : at + HEAD_DIM] = dot(probs, v).astype(LOW)
    for probs in probs_out:
        probs.flush()
    w_out_t = weights[:, 3 * local :]
    keep[...] = dot_nt(attended[0:rows, :], w_out_t)
    keep_far[...] = dot_nt(attended[rows : 2 * rows, :], w_out_t)
    send[...] = dot_nt(attended[2 * rows : 3 * rows, :], w_out_t).astype(LOW)
    send_far[...] = dot_nt(attended[3 * rows :, :], w_out_t).astype(LOW)
    if copy is not None:
        copy.wait()


def middle_kernel(gain_row, tokens, keep, near, far, small, spread, middle, rows):
    total = tokens[...].astype(FULL) + (
        keep[...] + near[...].astype(FULL) + far[...].astype(FULL)
    )
    middle[...] = total
    moe = (total * root_of(total) * small[gain_row : gain_row + 1, :]).astype(LOW)
    rows[...] = dot_tn(spread[...], moe).astype(LOW)


def far_kernel(keep_far, near, out):
    out[...] = (keep_far[...] + near[...].astype(FULL)).astype(LOW)


GELU_A = 0.7978845608028654
GELU_B = 0.044715


def flush(ref):
    if isinstance(ref, Stored):
        ref.flush()


def expert_kernel(
    experts,
    scalars,
    x_keep,
    x_send,
    cot_keep,
    cot_send,
    w_in,
    w_out,
    small,
    part_keep,
    part_send,
    active_out,
    hidden_out,
    buffer_out,
    gate_out,
    router_out,
    x,
    cot,
):
    rows = x_keep.shape[0]
    x[0:rows, :] = x_keep[...]
    x[rows:, :] = x_send[...]
    cot[0:rows, :] = cot_keep[...]
    cot[rows:, :] = cot_send[...]
    flush(x)
    hidden = dot(x[...], w_in[...])
    pulled = dot_nt(cot[...], w_out[...])
    router_t = small[0:experts, :].astype(LOW)
    mine = lax.broadcasted_iota(jnp.int32, (2 * rows, experts), 1) == scalars[0]
    logits = dot_nt(x[...], router_t)
    raised = jnp.exp(logits - jnp.max(logits, axis=1, keepdims=True))
    chances = raised / jnp.sum(raised, axis=1, keepdims=True)
    gate = jnp.sum(jnp.where(mine, chances, 0.0), axis=1, keepdims=True)
    square = hidden * hidden
    wave = jnp.tanh(GELU_A * hidden * (1.0 + GELU_B * square))
    half = 0.5 + 0.5 * wave
    active = (hidden * half).astype(LOW)
    active_out[...] = active
    slope = half + 0.5 * GELU_A * hidden * (1.0 - wave * wave) * (1.0 + 3.0 * GELU_B * square)
    grad_hidden = (gate * pulled * slope).astype(LOW)
    hidden_out[...] = grad_hidden
    flush(hidden_out)
    grad_gate = jnp.sum(active.astype(FULL) * pulled, axis=1, keepdims=True)
    grad_logits = (gate * grad_gate * (jnp.where(mine, 1.0, 0.0) - chances)).astype(LOW)
    buffer_out[...] = (gate * cot[...].astype(FULL)).astype(LOW)
    gate_out[...] = gate
    router_out[...] = dot_tn(grad_logits, x[...])
    flush(router_out)
    part = dot_nt(grad_hidden, w_in[...]) + dot(grad_logits, router_t)
    part_keep[...] = part[0:rows, :]
    part_send[...] = part[rows:, :].astype(LOW)


def forward_kernel(
    first, first_gate, second, second_gate, w_out, keep, send, keep_far, send_far
):
    rows = keep.shape[0]
    part = second_gate[...] * dot(second[...], w_out[...])
    keep_far[...] = part[0:rows, :]
    send_far[...] = part[rows:, :].astype(LOW)
    part = first_gate[...] * dot(first[...], w_out[...])
    keep[...] = part[0:rows, :]
    keep.flush()
    send[...] = part[rows:, :].astype(LOW)


def join_kernel(keep, near, far, out):
    out[...] = (keep[...] + near[...].astype(FULL) + far[...].astype(FULL)).astype(LOW)


def grad_w_kernel(*refs):
    *parts, out = refs
    lefts, rights = parts[:-2], parts[-2:]

    def whole(parts):
        return jnp.concatenate([part[...] for part in parts], axis=0)

    out[0] = dot_tn(whole(lefts), whole(rights))


def back_kernel(gain_row, middle, cot, spread, back, small, grad_middle, grad_low, grad_gain):
    grad_two = dot(spread[...], back[...])
    values = middle[...]
    root = root_of(values)
    normed = values * root
    scaled = grad_two * small[gain_row : gain_row + 1, :]
    grad_gain[...] = jnp.sum(grad_two * normed, axis=0, keepdims=True)
    total = cot[...].astype(FULL) + root * (
        scaled - normed * jnp.mean(scaled * normed, axis=1, keepdims=True)
    )
    grad_middle[...] = total
    grad_low[...] = total.astype(LOW)


def attend_back_kernel(
    heads,
    scalars,
    own,
    far,
    near,
    near_far,
    weights,
    qkv,
    *refs,
):
    probs, (attended, ones, grads) = refs[:heads], refs[heads : heads + 3]
    *ring_rows, grad_w, joined, flipped = refs[heads + 3 :]
    rows = own.shape[0]
    local = attended.shape[1]
    joined[0:rows, :] = own[...]
    joined[rows : 2 * rows, :] = far[...]
    joined[2 * rows : 3 * rows, :] = near[...]
    joined[3 * rows :, :] = near_far[...]
    w_out_t = weights[:, 3 * local :]
    grad_attended = dot(joined[...], w_out_t).astype(LOW)
    for h in range(heads):
        at = h * HEAD_DIM
        q = qkv[:, at : at + HEAD_DIM]
        k = qkv[:, local + at : local + at + HEAD_DIM]
        v = qkv[:, 2 * local + at : 2 * local + at + HEAD_DIM]
        upstream = grad_attended[:, at : at + HEAD_DIM]
        grad_p = dot_nt(upstream, v)
        low = probs[h][...]
        p = low.astype(FULL)
        inner = jnp.sum(p * grad_p, axis=1, keepdims=True)
        grad_s = (p * (grad_p - inner)).astype(LOW)
        grads[:, at : at + HEAD_DIM] = (dot(grad_s, k) * SCALE).astype(LOW)
        flipped[at : at + HEAD_DIM, :] = dot_tn(q, grad_s) * SCALE
        flipped[local + at : local + at + HEAD_DIM, :] = dot_tn(upstream, low)
    grads[:, local:] = flipped[...].T.astype(LOW)
    grad_w[:, 3 * local :] = dot_tn(joined[...], attended[...]).astype(LOW)
    grad_w[:, 0 : 3 * local] = dot_tn(ones[...], grads[...]).astype(LOW)
    if ring_rows:
        top, bottom, rest = ring_rows
        middle = top.shape[0]
        shard = middle + bottom.shape[0]
        count = grad_w.shape[0] // shard
        place = ring_place(scalars[0], count)

        def start_of(step):
            return pl.multiple_of(ring_source(place + step, count) * shard, 16)

        start = start_of(count // 2)
        top[...] = grad_w[pl.ds(start, middle), :]
        bottom[...] = grad_w[pl.ds(pl.multiple_of(start + middle, 16), shard - middle), :]
        steps = [sign * k for k in range(count // 2 - 1, 0, -1) for sign in (1, -1)] + [0]
        for index, step in enumerate(steps):
            rest[index * shard : (index + 1) * shard, :] = grad_w[pl.ds(start_of(step), shard), :]


def grad_one_kernel(
    experts,
    grads,
    weights,
    group,
    router_one,
    router_two,
    gain_two,
    keep,
    keep_far,
    send,
    send_far,
    payload,
):
    rows = keep.shape[0]
    w_qkv = weights[:, 0 : grads.shape[1]]
    gain_one = None
    for index, out in enumerate((keep, keep_far, send, send_far)):
        at = slice(index * rows, (index + 1) * rows)
        part = dot_nt(grads[at, :], w_qkv)
        out[...] = part.astype(out.dtype)
        values = group[at, :].astype(FULL)
        gain = jnp.sum(part * (values * root_of(values)), axis=0, keepdims=True)
        gain_one = gain if gain_one is None else gain_one + gain
        if index == 0:
            keep.flush()
    owners, height, shard = payload.shape
    whole = jnp.concatenate(
        [
            router_one[...] + router_two[...],
            gain_one,
            gain_two[...],
            jnp.zeros((height - experts - 2, gain_one.shape[1]), FULL),
        ],
        axis=0,
    )
    for d in range(owners):
        payload[d] = whole[:, d * shard : (d + 1) * shard]


def last_kernel(
    experts,
    tokens,
    keep,
    near,
    far,
    grad_middle,
    small,
    middle,
    spread,
    back,
    grad_tokens,
    result,
):
    values = tokens[...].astype(FULL)
    root = root_of(values)
    normed = values * root
    grad_one = keep[...] + near[...].astype(FULL) + far[...].astype(FULL)
    scaled = grad_one * small[experts : experts + 1, :]
    grad_tokens[...] = grad_middle[...] + root * (
        scaled - normed * jnp.mean(scaled * normed, axis=1, keepdims=True)
    )
    grad_tokens.flush()
    result[...] = (middle[...] + dot(spread[...], back[...])).astype(LOW)


def ring_add_kernel(rest, ahead, behind, to_right, to_left, left_over):
    shard = to_right.shape[0]
    left_over[...] = rest[2 * shard :, :]
    if ahead.shape[0] == shard:
        to_right[...] = (rest[0:shard, :].astype(FULL) + ahead[...].astype(FULL)).astype(LOW)
        to_left[...] = (
            rest[shard : 2 * shard, :].astype(FULL) + behind[...].astype(FULL)
        ).astype(LOW)
        return
    middle = ahead.shape[0]
    to_right[0:middle, :] = (rest[0:middle, :].astype(FULL) + ahead[...].astype(FULL)).astype(LOW)
    to_right[middle:, :] = rest[middle:shard, :]
    to_left[0:middle, :] = rest[shard : shard + middle, :]
    to_left[middle:, :] = (
        rest[shard + middle : 2 * shard, :].astype(FULL) + behind[...].astype(FULL)
    ).astype(LOW)


def write_sums(total, query, key, value, out):
    local = query.shape[1]
    query[...] = total[:, 0:local]
    key[...] = total[:, local : 2 * local]
    value[...] = total[:, 2 * local : 3 * local]
    out[...] = total[:, 3 * local :].T


def ring_last_kernel(experts, mine, ahead, behind, parts, query, key, value, out, *small):
    total = mine[...].astype(FULL) + (ahead[...].astype(FULL) + behind[...].astype(FULL))
    write_sums(total, query, key, value, out)
    write_small(experts, parts, *small)


def write_small(experts, parts, gain_one, gain_two, router):
    total = jnp.sum(parts[...], axis=0)
    router[...] = total[0:experts, :]
    gain_one[...] = total[experts : experts + 1, :]
    gain_two[...] = total[experts + 1 : experts + 2, :]


def sum_kernel(experts, blocks, parts, query, key, value, out, *small):
    total = blocks[0].astype(FULL)
    for d in range(1, blocks.shape[0]):
        total = total + blocks[d].astype(FULL)
    write_sums(total, query, key, value, out)
    write_small(experts, parts, *small)


def on_device(
    tokens,
    lengths,
    routes,
    norm_attn,
    w_query,
    w_key,
    w_value,
    w_attn_out,
    norm_moe,
    w_router,
    w_expert_in,
    w_expert_out,
    cotangent,
):
    owners = lax.axis_size("dp")
    expert_index = lax.axis_index("dp")
    piece_index = lax.axis_index("tensor")
    piece_rows, width = tokens.shape
    shard, local = w_query.shape
    experts = w_router.shape[1]
    capacity = 3 * piece_rows // (2 * experts)
    slots = experts * capacity
    heads = local // HEAD_DIM
    total_rows = 4 * piece_rows
    small_rows = -(-(experts + 2) // 16) * 16
    scalars = jnp.concatenate(
        [jnp.stack([expert_index, piece_index]).astype(jnp.int32), lengths[0]]
    )
    sequences = lengths.shape[1]

    (packed,) = kernel_call(
        pack_kernel, [((shard + small_rows, 4 * local), LOW)], "pack", fetch=range(7)
    )(
        w_query,
        w_key,
        w_value,
        w_attn_out,
        w_router.T,
        norm_attn.reshape(1, shard),
        norm_moe.reshape(1, shard),
    )
    has_blocks = shard % 16 == 0
    scratch = []
    if has_blocks:
        behind, ahead, top, bottom = ring_gather(packed)
        partial = kernel_call(
            functools.partial(assemble_kernel, owners),
            [((width, 4 * local), LOW), ((owners, small_rows, shard), FULL)],
            "assemble",
            smem=(0,),
            store=(0,),
        )(scalars, packed, *behind, *ahead)
        blocks = [*partial, top, bottom]
        early = behind[0]
        scratch = [pltpu.VMEM((owners, small_rows, shard), FULL), pltpu.SemaphoreType.DMA]
    else:
        gathered = lax.all_gather(packed, "dp", axis=0, tiled=False)
        flat = gathered[:, shard:, :shard].transpose(1, 0, 2).reshape(small_rows, width)
        blocks = [gathered[:, :shard].reshape(width, 4 * local), flat.astype(FULL)]
        early = packed
    token_far = swap_far(tokens)
    token_near = swap_near(tokens)

    spread, cot_rows = kernel_call(
        functools.partial(spread_kernel, capacity, slots),
        [((piece_rows, slots), LOW), ((slots, width), LOW)],
        "spread",
        smem=(0,),
        fetch=(1, 2),
        store=(0,),
        time=2,
        wait=(early,),
    )(scalars, routes, cotangent)
    token_near_far = swap_near(token_far)

    cot_rows = add(cot_rows, wait=(blocks[1],))
    cot_own = exchange(cot_rows.reshape(experts, capacity, width))
    cot_own = cot_own.reshape(slots, width)

    outs = [
        ((piece_rows, width), FULL),
        ((piece_rows, width), FULL),
        ((piece_rows, width), LOW),
        ((piece_rows, width), LOW),
        ((total_rows, width), LOW),
        ((total_rows, 3 * local), LOW),
        ((total_rows, local), LOW),
        ((total_rows, width), LOW),
    ]
    outs += [((total_rows, total_rows), LOW)] * heads
    raw, alias, fetch = [], {}, [1]
    if has_blocks:
        outs += [((width, 4 * local), LOW), ((small_rows, width), FULL)]
        raw, alias, fetch = [len(outs) - 2], {5: len(outs) - 2}, [1, 5]
    made = kernel_call(
        functools.partial(attend_kernel, owners, sequences, has_blocks),
        outs,
        "attend",
        smem=(0,),
        fetch=fetch,
        store=(5, *range(8, 8 + heads)),
        raw=raw,
        alias=alias,
        scratch=scratch,
        time=4,
    )(scalars, tokens, token_far, token_near, token_near_far, *blocks)
    keep, keep_far, send, send_far = made[:4]
    ones, qkv, attended, group, *probs = made[4 : 8 + heads]
    weights, small = made[8 + heads :] if has_blocks else blocks

    def scatter(keep_far, send, send_far, wait=()):
        near_far = swap_near(send_far)
        near = swap_near(send)
        (out,) = kernel_call(far_kernel, [(keep_far.shape, LOW)], "far", time=0.1, wait=wait)(
            keep_far, near_far
        )
        return near, swap_far(out), out

    near, far, mark = scatter(keep_far, send, send_far)
    small_now = small
    ones, attended, group, small = save(ones, attended, group, small, wait=(mark,))
    tokens_here, spread_here = load(tokens, spread, wait=(mark, cot_own))
    middle, own_rows = kernel_call(
        functools.partial(middle_kernel, experts + 1),
        [((piece_rows, width), FULL), ((slots, width), LOW)],
        "middle",
        wait_hbm=(ones,),
    )(tokens_here, keep, near, far, small_now, spread_here)
    (middle,) = save(middle, wait=(own_rows,))

    def over_dp(rows):
        return exchange(rows.reshape(experts, capacity, width)).reshape(slots, width)

    own = over_dp(own_rows)
    cot_far = swap_far(cot_own)
    cot_near = swap_near(cot_own)
    cot_near_far = swap_near(cot_far)
    (small_expert,) = load(small, wait=(own_rows,))
    own = add(own, wait=(small_expert, cot_far), wait_hbm=(middle,))
    own_far = swap_far(own)
    own_near = swap_near(own)
    weight_in = w_expert_in[0]
    weight_out = w_expert_out[0]
    hidden_size = weight_in.shape[1]

    def expert_part(x_keep, x_send, cot_keep, cot_send, store):
        rows = 2 * slots
        return kernel_call(
            functools.partial(expert_kernel, experts),
            [
                ((slots, width), FULL),
                ((slots, width), LOW),
                ((rows, hidden_size), LOW),
                ((rows, hidden_size), LOW),
                ((rows, width), LOW),
                ((rows, 1), FULL),
                ((experts, width), FULL),
                ((rows, width), LOW),
            ],
            "expert",
            smem=(0,),
            store=store,
            time=4,
            scratch=[pltpu.VMEM((rows, width), LOW)],
        )(scalars, x_keep, x_send, cot_keep, cot_send, weight_in, weight_out, small_expert)

    keep, send, active_one, hidden_one, buffer_one, gate_one, router_one, rows_one = expert_part(
        own, own_near, cot_own, cot_near, (0, 3, 6, 7)
    )
    own_far = add(own_far, wait=(send,))
    keep_far, send_far, active_two, hidden_two, buffer_two, gate_two, router_two, rows_two = (
        expert_part(own_far, swap_near(own_far), cot_far, cot_near_far, ())
    )
    near, far, mark = scatter(keep_far, send, send_far)
    (keep,) = load(keep, wait=(mark,))
    rows_two, hidden_two, router_two = save(rows_two, hidden_two, router_two, wait=(mark,))
    forward_keep, forward_send, forward_keep_far, forward_send_far = kernel_call(
        forward_kernel,
        [((slots, width), kind) for kind in (FULL, LOW, FULL, LOW)],
        "forward",
        store=(0,),
        time=2,
        wait=(mark,),
    )(active_one, gate_one, active_two, gate_two, weight_out)
    (grad_expert_out,) = kernel_call(
        grad_w_kernel, [((1, *weight_out.shape), FULL)], "grad_out", store=(0,), time=3, wait=(mark,)
    )(active_one, active_two, buffer_one, buffer_two)
    (back_rows,) = kernel_call(
        join_kernel,
        [((slots, width), LOW)],
        "join",
        wait=(forward_send,),
        wait_hbm=(grad_expert_out, hidden_two),
    )(keep, near, far)
    back = over_dp(back_rows)
    out_near, out_far, out_mark = scatter(
        forward_keep_far, forward_send, forward_send_far, wait=(back_rows,)
    )
    (grad_expert_in,) = kernel_call(
        grad_w_kernel, [((1, *weight_in.shape), FULL)], "grad_in", fetch=range(4), store=(0,), time=3
    )(rows_one, rows_two, hidden_one, hidden_two)
    middle_here, cot_here, spread_here, small_here, forward_here = load(
        middle, cotangent, spread, small, forward_keep, wait=(out_mark,)
    )
    (out_rows,) = kernel_call(join_kernel, [((slots, width), LOW)], "join", time=0.1)(
        forward_here, out_near, out_far
    )
    out_back = over_dp(out_rows)

    grad_middle, grad_low, grad_gain_two = kernel_call(
        functools.partial(back_kernel, experts + 1),
        [((piece_rows, width), FULL), ((piece_rows, width), LOW), ((1, width), FULL)],
        "back",
        wait=(out_far,),
        wait_hbm=(grad_expert_in,),
    )(middle_here, cot_here, spread_here, back, small_here)
    grad_far = swap_far(grad_low)
    grad_near = swap_near(grad_low)
    grad_far = add(grad_far, wait=(out_rows,))
    grad_near_far = swap_near(grad_far)
    outs = [((total_rows, 3 * local), LOW)]
    middle_row = shard // 32 * 16
    scratch = [
        pltpu.VMEM((total_rows, width), LOW),
        pltpu.VMEM((2 * local, total_rows), FULL),
    ]
    if has_blocks:
        outs += [
            ((middle_row, 4 * local), LOW),
            ((shard - middle_row, 4 * local), LOW),
            ((width - shard, 4 * local), LOW),
        ]
        scratch = [pltpu.VMEM((width, 4 * local), LOW)] + scratch
    else:
        outs.append(((width, 4 * local), LOW))
    grads, *grad_w = kernel_call(
        functools.partial(attend_back_kernel, heads),
        outs,
        "attend_back",
        smem=(0,),
        fetch=range(5, 9 + heads),
        first=2 + heads,
        time=2,
        scratch=scratch,
    )(
        *(scalars, grad_low, grad_far, grad_near, grad_near_far),
        *(weights, qkv, *probs, attended, ones),
    )
    last = [((shard, local), FULL)] * 3 + [((local, shard), FULL)]
    held = {}

    def first(mark):
        keep, keep_far, send, send_far, payload = kernel_call(
            functools.partial(grad_one_kernel, experts),
            [((piece_rows, width), kind) for kind in (FULL, FULL, LOW, LOW)]
            + [((owners, small_rows, shard), FULL)],
            "grad_one",
            fetch=(1, 2, 3, 4),
            store=(0,),
            time=0.2,
            wait=(mark,),
        )(grads, weights, group, router_one, router_two, grad_gain_two)
        held["keep"], held["keep_far"] = keep, keep_far
        held["near_far"], held["near"] = swap_near(send_far), swap_near(send)
        held["small"] = (payload, swap(payload, "tensor", 1))
        return (send,), (), ()

    def second(mark):
        out_shape = [(held["keep_far"].shape, LOW)]
        (out,) = kernel_call(far_kernel, out_shape, "far", time=0.1, wait=(mark,))(
            held["keep_far"], held["near_far"]
        )
        held["far"] = swap_far(out)
        total = add(*held["small"], wait=(mark,))
        came = swap(total, "tensor", 2)
        held["small"] = (total, came)
        held["middle"] = save(grad_middle, wait=(mark,))
        return (out, total), (came,), held["middle"]

    def third(mark):
        total = add(*held["small"], wait=(mark,))
        held["small"] = exchange(total)
        return (total,), (held["far"],), ()

    def fourth(mark):
        held["last"] = kernel_call(
            functools.partial(last_kernel, experts),
            [
                ((piece_rows, width), FULL),
                ((piece_rows, width), LOW),
            ],
            "last",
            fetch=(0, 1, 4, 5, 6, 7),
            store=(0, 1),
            time=0.3,
            wait=(mark,),
        )(
            *(tokens, held["keep"], held["near"], held["far"]),
            *(*held["middle"], small, middle, spread, out_back),
        )
        return (), (), ()

    fillers = (first, second, third, fourth)
    last += [((1, shard), FULL), ((1, shard), FULL), ((experts, shard), FULL)]
    if has_blocks:
        parts = ring_reduce(*grad_w, shard, fillers, (out_back,))
        sums = kernel_call(
            functools.partial(ring_last_kernel, experts),
            last,
            "ring_last",
            store=range(7),
            wait_hbm=held["last"][:1],
        )(*parts, held["small"])
    else:
        for filler in fillers:
            filler(grad_w[0])
        sums = kernel_call(
            functools.partial(sum_kernel, experts), last, "sum", store=range(7)
        )(exchange(grad_w[0].reshape(owners, shard, 4 * local)), held["small"])
    grad_query, grad_key, grad_value, grad_out, grad_norm_attn, grad_norm_moe, grad_router = sums
    grad_tokens, result = held["last"]
    return (
        result,
        grad_tokens,
        grad_norm_attn.reshape(shard),
        grad_query,
        grad_key,
        grad_value,
        grad_out,
        grad_norm_moe.reshape(shard),
        grad_router.T,
        grad_expert_in,
        grad_expert_out,
    )


def solution(mesh):
    return jax.shard_map(
        on_device,
        mesh=mesh,
        in_specs=(
            P(("dp", "tensor"), None),
            P("dp", None),
            P("dp", None),
            P("dp"),
            P("dp", "tensor"),
            P("dp", "tensor"),
            P("dp", "tensor"),
            P("tensor", "dp"),
            P("dp"),
            P("dp", None),
            P("dp", None, "tensor"),
            P("dp", "tensor", None),
            P(("dp", "tensor"), None),
        ),
        out_specs=(
            P(("dp", "tensor"), None),
            P(("dp", "tensor"), None),
            P("dp"),
            P("dp", "tensor"),
            P("dp", "tensor"),
            P("dp", "tensor"),
            P("tensor", "dp"),
            P("dp"),
            P("dp", None),
            P("dp", None, "tensor"),
            P("dp", "tensor", None),
        ),
        check_vma=False,
    )
```

```python
import functools

import jax
import jax.numpy as jnp
from jax import lax
from jax.experimental import pallas as pl
from jax.experimental.pallas import tpu as pltpu
from jax.sharding import PartitionSpec as P

HEAD_DIM = 64
EPSILON = 1e-06
NEGATIVE = -1e30
LOW = jnp.bfloat16
FULL = jnp.float32
SCALE = HEAD_DIM ** (-0.5)
MIB = 1 << 20


def dot(a, b):
    return jnp.dot(a, b, preferred_element_type=FULL)


def dot_nt(a, b):
    return lax.dot_general(a, b, (((1,), (1,)), ((), ())), preferred_element_type=FULL)


def dot_tn(a, b):
    return lax.dot_general(a, b, (((0,), (0,)), ((), ())), preferred_element_type=FULL)


class Fetched:
    def __init__(self, ref, held, sem, late):
        self.held, self.waiting, self.late = held, True, late
        self.copy = pltpu.make_async_copy(ref, held, sem)
        self.shape = held.shape

    def wait(self):
        if self.waiting:
            self.copy.wait()
            self.waiting = False
            while self.late:
                self.late.pop(0).copy.start()

    def __getitem__(self, index):
        self.wait()
        return self.held[index]


class Stored:
    def __init__(self, ref, held, sem):
        self.ref, self.held, self.sem = ref, held, sem
        self.copy = None
        self.shape, self.dtype = held.shape, held.dtype

    def __getitem__(self, index):
        return self.held[index]

    def __setitem__(self, index, value):
        self.held[index] = value

    def flush(self):
        if self.copy is None:
            self.copy = pltpu.make_async_copy(self.held, self.ref, self.sem)
            self.copy.start()


def kernel_call(body, outs, name, fetch=(), store=(), smem=(), time=1, limit=24, scratch=(), wait=(), wait_hbm=(), first=99):
    def call(*operands):
        n_in, n_out, n_scratch = len(operands), len(outs), len(scratch)
        held = [pltpu.VMEM(operands[i].shape, operands[i].dtype) for i in fetch]
        held += [pltpu.VMEM(*outs[i]) for i in store]
        sems = [pltpu.SemaphoreType.DMA((len(held),))] if held else []

        def kernel(*refs):
            ins, refs = list(refs[:n_in]), refs[n_in + len(wait) + len(wait_hbm) :]
            results, rest = list(refs[:n_out]), refs[n_out:]
            own, buffers = rest[:n_scratch], rest[n_scratch : n_scratch + len(held)]
            sem = rest[-1] if held else None
            at, late = 0, []
            for i in fetch:
                ins[i] = Fetched(ins[i], buffers[at], sem.at[at], late)
                if at < first:
                    ins[i].copy.start()
                else:
                    late.append(ins[i])
                at += 1
            for i in store:
                results[i] = Stored(results[i], buffers[at], sem.at[at])
                at += 1
            body(*ins, *results, *own)
            for i in fetch:
                ins[i].wait()
            for i in store:
                results[i].flush()
            for i in store:
                results[i].copy.wait()

        def spec(i, hbm):
            return pl.BlockSpec(memory_space=pltpu.HBM if i in hbm else pltpu.VMEM)


        operands = [
            pltpu.with_memory_space_constraint(x, pltpu.HBM) if i in fetch else x
            for i, x in enumerate(operands)
        ]
        return pl.pallas_call(
            kernel,
            out_shape=[
                pltpu.HBM(*outs[i]) if i in store else jax.ShapeDtypeStruct(*outs[i])
                for i in range(n_out)
            ],
            in_specs=[
                pl.BlockSpec(memory_space=pltpu.SMEM) if i in smem else spec(i, fetch)
                for i in range(n_in)
            ]
            + [pl.BlockSpec(memory_space=pl.ANY) for _ in wait]
            + [pl.BlockSpec(memory_space=pltpu.HBM) for _ in wait_hbm],
            out_specs=[spec(i, store) for i in range(n_out)],
            scratch_shapes=[*scratch, *held, *sems],
            compiler_params=pltpu.CompilerParams(vmem_limit_bytes=limit * MIB),
            cost_estimate=pl.CostEstimate(
                flops=int(time * 1.1e9), bytes_accessed=MIB, transcendentals=0
            ),
            name=name,
        )(
            *operands,
            *wait,
            *(pltpu.with_memory_space_constraint(x, pltpu.HBM) for x in wait_hbm),
        )

    return call


def move_kernel(count, *refs):
    sources, targets, sem = refs[:count], refs[-1 - count : -1], refs[-1]
    copies = [
        pltpu.make_async_copy(source, target, sem.at[k])
        for k, (source, target) in enumerate(zip(sources, targets))
    ]
    for copy in copies:
        copy.start()
    for copy in copies:
        copy.wait()


def moved(arrays, source, target, name, wait):
    kinds = [(x.shape, x.dtype) for x in arrays]
    if source is pltpu.HBM:
        arrays = [pltpu.with_memory_space_constraint(x, pltpu.HBM) for x in arrays]
    return pl.pallas_call(
        functools.partial(move_kernel, len(kinds)),
        out_shape=[
            pltpu.HBM(*kind) if target is pltpu.HBM else jax.ShapeDtypeStruct(*kind)
            for kind in kinds
        ],
        in_specs=[pl.BlockSpec(memory_space=source) for _ in kinds]
        + [pl.BlockSpec(memory_space=pl.ANY) for _ in wait],
        out_specs=[pl.BlockSpec(memory_space=target) for _ in kinds],
        scratch_shapes=[pltpu.SemaphoreType.DMA((len(kinds),))],
        compiler_params=pltpu.CompilerParams(vmem_limit_bytes=16 * MIB),
        cost_estimate=pl.CostEstimate(flops=2 * 10**9, bytes_accessed=MIB, transcendentals=0),
        name=name,
    )(*arrays, *wait)


def save(*arrays, wait=()):
    return moved(arrays, pltpu.VMEM, pltpu.HBM, "save", wait)


def load(*arrays, wait=()):
    return moved(arrays, pltpu.HBM, pltpu.VMEM, "load", wait)


def swap(values, axis, bit):
    count = lax.axis_size(axis)
    return lax.ppermute(values, axis, [(i, i ^ bit) for i in range(count)])


def exchange(buffer):
    return lax.all_to_all(buffer, "dp", split_axis=0, concat_axis=0, tiled=True)


def swap_far(rows):
    return swap(rows, "tensor", 2)


def swap_near(rows):
    return swap(rows, "tensor", 1)


def ring_source(place, count):
    place = lax.rem(place + 2 * count, count)
    return jnp.where(place < count // 2, 2 * place, 2 * (count - 1 - place) + 1)


def ring_perms(count):
    order = list(range(0, count, 2)) + list(range(1, count, 2))[::-1]
    right = [(order[k], order[(k + 1) % count]) for k in range(count)]
    return right, [(b, a) for a, b in right]


def ring_gather(block):
    count = lax.axis_size("dp")
    right, left = ring_perms(count)
    behind, ahead = [block], [block]
    for _ in range(1, count // 2):
        behind.append(lax.ppermute(behind[-1], "dp", right))
        ahead.append(lax.ppermute(ahead[-1], "dp", left))
    middle = block.shape[0] // 32 * 16
    top = lax.ppermute(behind[-1][:middle], "dp", right)
    bottom = lax.ppermute(ahead[-1][middle:], "dp", left)
    return behind[1:], ahead[1:], top, bottom


def ring_place(me, count):
    return jnp.where(lax.rem(me, 2) == 0, me // 2, count - 1 - me // 2)


def fence_kernel(source, out):
    out[...] = source[0 : out.shape[0], 0 : out.shape[1]].astype(out.dtype)


def fence(source, wait=()):
    (out,) = kernel_call(fence_kernel, [((16, 128), LOW)], "fence", time=40, wait=wait)(source)
    return out


def add_kernel(*refs):
    total = refs[0][...].astype(FULL)
    for ref in refs[1:-1]:
        total = total + ref[...].astype(FULL)
    refs[-1][...] = total.astype(refs[-1].dtype)


def add(*values, wait=(), wait_hbm=()):
    kind = (values[0].shape, values[0].dtype)
    return kernel_call(add_kernel, [kind], "add", time=0.1, wait=wait, wait_hbm=wait_hbm)(*values)[0]


def ring_reduce(top, bottom, rest, shard, fillers, arrived=()):
    count = lax.axis_size("dp")
    right, left = ring_perms(count)
    width = rest.shape[1]
    ahead = lax.ppermute(top, "dp", right)
    behind = lax.ppermute(bottom, "dp", left)
    done, kept = (), ()
    for index, step in enumerate(range(count // 2 - 1, -1, -1)):
        if index < len(fillers):
            done, arrived, kept = fillers[index](fence(rest, arrived))
        if not step:
            return rest, ahead, behind
        block = (shard, width)
        to_right, to_left, rest = kernel_call(
            ring_add_kernel,
            [(block, LOW), (block, LOW), ((rest.shape[0] - 2 * shard, width), LOW)],
            "ring_add",
            wait=done,
            wait_hbm=kept,
        )(rest, ahead, behind)
        ahead = lax.ppermute(to_right, "dp", right)
        behind = lax.ppermute(to_left, "dp", left)


def root_of(values):
    return lax.rsqrt(jnp.mean(values * values, axis=1, keepdims=True) + EPSILON)


def pack_kernel(wq, wk, wv, wo, router, gain_one, gain_two, out):
    shard, local = wq.shape
    out[0:shard, 0:local] = wq[...]
    out[0:shard, local : 2 * local] = wk[...]
    out[0:shard, 2 * local : 3 * local] = wv[...]
    out[0:shard, 3 * local :] = wo[...].astype(FULL).T.astype(LOW)
    experts = router.shape[0]
    rows = out.shape[0] - shard
    small = jnp.concatenate(
        [
            router[...].astype(FULL),
            gain_one[...].astype(FULL),
            gain_two[...].astype(FULL),
            jnp.zeros((rows - experts - 2, shard), FULL),
        ],
        axis=0,
    )
    out[shard:, :] = jnp.zeros((rows, out.shape[1]), LOW)
    out[shard:, 0:shard] = small.astype(LOW)


def spread_kernel(capacity, slots, scalars, routes, cot, spread, rows):
    count = cot.shape[0]
    piece = scalars[1]
    route = routes[pl.ds(pl.multiple_of(piece * count, count), count), :]
    experts = slots // capacity
    ids = lax.broadcasted_iota(jnp.int32, (count, experts), 1)
    chosen = jnp.where(route == ids, 1.0, 0.0)
    first = lax.broadcasted_iota(jnp.int32, (count, count), 0)
    second = lax.broadcasted_iota(jnp.int32, (count, count), 1)
    before = jnp.where(second < first, 1.0, 0.0).astype(LOW)
    earlier = dot(before, chosen.astype(LOW))
    slot = jnp.sum(earlier * chosen, axis=1, keepdims=True).astype(jnp.int32)
    place = route * capacity + slot
    lanes = lax.broadcasted_iota(jnp.int32, (count, slots), 1)
    one_hot = jnp.where(place == lanes, 1.0, 0.0).astype(LOW)
    spread[...] = one_hot
    rows[...] = dot_tn(one_hot, cot[...]).astype(LOW)


def assemble_kernel(count, scalars, *refs):
    blocks, (weights, smalls) = refs[:-2], refs[-2:]
    me = scalars[0]
    place = ring_place(me, count)
    shard = weights.shape[0] // count
    half = count // 2
    steps = [0] + [-s for s in range(1, half)] + list(range(1, half))
    for step, block in zip(steps, blocks):
        source = ring_source(place + step, count) if step else me
        weights[pl.ds(pl.multiple_of(source * shard, 16), shard), :] = block[0:shard, :]
        smalls[source] = block[shard:, 0:shard].astype(FULL)


def finish_small(count, scalars, blocks, smalls, small_out):
    smalls[...] = blocks[1][...]
    top, bottom = blocks[2:]
    shard = smalls.shape[2]
    source = ring_source(ring_place(scalars[0], count) + count // 2, count)
    smalls[source] = bottom[shard - top.shape[0] :, 0:shard].astype(FULL)
    for d in range(count):
        small_out[:, d * shard : (d + 1) * shard] = smalls[d]


def finish(count, scalars, blocks, weights):
    shard = weights.shape[0] // count
    weights[...] = blocks[0][...]
    top, bottom = blocks[2:]
    source = ring_source(ring_place(scalars[0], count) + count // 2, count)
    middle = top.shape[0]
    start = pl.multiple_of(source * shard, 16)
    rest = shard - middle
    weights[pl.ds(start, middle), :] = top[...]
    weights[pl.ds(pl.multiple_of(start + middle, 16), rest), :] = bottom[0:rest, :]


def positions_of(piece, rows, shape, dim):
    index = lax.broadcasted_iota(jnp.int32, shape, dim)
    block = index // rows
    flip = jnp.where(block == 1, 2, jnp.where(block == 2, 1, block))
    return (piece ^ flip) * rows + lax.rem(index, rows)


def attend_kernel(count, sequences, has_blocks, *refs):
    scalars, tokens, far, near, near_far = refs[:5]
    given = 4 if has_blocks else 2
    blocks = refs[5 : 5 + given]
    outs = refs[5 + given :]
    heads = len(outs) - (11 if has_blocks else 8)
    keep, keep_far, send, send_far, ones, qkv_out, attended, group = outs[:8]
    probs_out = outs[8 : 8 + heads]
    if has_blocks:
        weights, small, smalls = outs[8 + heads :]
        finish_small(count, scalars, blocks, smalls, small)
    else:
        weights, small = blocks
    rows = tokens.shape[0]
    total = 4 * rows
    local = attended.shape[1]
    experts = count
    gain = small[experts : experts + 1, :]
    piece = scalars[1]
    for index, ref in ((1, far), (2, near), (3, near_far), (0, tokens)):
        group[index * rows : (index + 1) * rows, :] = ref[...]
        values = ref[...].astype(FULL)
        ones[index * rows : (index + 1) * rows, :] = (values * root_of(values) * gain).astype(LOW)
    if has_blocks:
        finish(count, scalars, blocks, weights)
    qkv = dot(ones[...], weights[:, 0 : 3 * local]).astype(LOW)
    qkv_out[...] = qkv
    qkv_out.flush()
    query_pos = positions_of(piece, rows, (total, 1), 0)
    key_pos = positions_of(piece, rows, (1, total), 1)
    start = jnp.zeros((total, 1), jnp.int32)
    end = jnp.int32(0)
    for s in range(sequences):
        end = end + scalars[2 + s]
        start = jnp.where(query_pos >= end, end, start)
    bias = jnp.where((key_pos <= query_pos) & (key_pos >= start), 0.0, NEGATIVE)
    for h in range(local // HEAD_DIM):
        at = h * HEAD_DIM
        q = qkv[:, at : at + HEAD_DIM]
        k = qkv[:, local + at : local + at + HEAD_DIM]
        v = qkv[:, 2 * local + at : 2 * local + at + HEAD_DIM]
        scores = dot_nt(q, k) * SCALE + bias
        shifted = jnp.exp(scores - jnp.max(scores, axis=1, keepdims=True))
        probs = (shifted * (1.0 / jnp.sum(shifted, axis=1, keepdims=True))).astype(LOW)
        probs_out[h][...] = probs
        attended[:, at : at + HEAD_DIM] = dot(probs, v).astype(LOW)
    for probs in probs_out:
        probs.flush()
    w_out_t = weights[:, 3 * local :]
    keep[...] = dot_nt(attended[0:rows, :], w_out_t)
    keep_far[...] = dot_nt(attended[rows : 2 * rows, :], w_out_t)
    send[...] = dot_nt(attended[2 * rows : 3 * rows, :], w_out_t).astype(LOW)
    send_far[...] = dot_nt(attended[3 * rows :, :], w_out_t).astype(LOW)


def middle_kernel(gain_row, tokens, keep, near, far, small, spread, middle, rows):
    total = tokens[...].astype(FULL) + (
        keep[...] + near[...].astype(FULL) + far[...].astype(FULL)
    )
    middle[...] = total
    moe = (total * root_of(total) * small[gain_row : gain_row + 1, :]).astype(LOW)
    rows[...] = dot_tn(spread[...], moe).astype(LOW)


def far_kernel(keep_far, near, out):
    out[...] = (keep_far[...] + near[...].astype(FULL)).astype(LOW)


GELU_A = 0.7978845608028654
GELU_B = 0.044715


def flush(ref):
    if isinstance(ref, Stored):
        ref.flush()


def expert_kernel(
    experts,
    scalars,
    x_keep,
    x_send,
    cot_keep,
    cot_send,
    w_in,
    w_out,
    small,
    part_keep,
    part_send,
    active_out,
    hidden_out,
    buffer_out,
    gate_out,
    router_out,
    x,
    cot,
):
    rows = x_keep.shape[0]
    x[0:rows, :] = x_keep[...]
    x[rows:, :] = x_send[...]
    cot[0:rows, :] = cot_keep[...]
    cot[rows:, :] = cot_send[...]
    flush(x)
    hidden = dot(x[...], w_in[...])
    pulled = dot_nt(cot[...], w_out[...])
    router_t = small[0:experts, :].astype(LOW)
    mine = lax.broadcasted_iota(jnp.int32, (2 * rows, experts), 1) == scalars[0]
    logits = dot_nt(x[...], router_t)
    raised = jnp.exp(logits - jnp.max(logits, axis=1, keepdims=True))
    chances = raised / jnp.sum(raised, axis=1, keepdims=True)
    gate = jnp.sum(jnp.where(mine, chances, 0.0), axis=1, keepdims=True)
    square = hidden * hidden
    wave = jnp.tanh(GELU_A * hidden * (1.0 + GELU_B * square))
    half = 0.5 + 0.5 * wave
    active = (hidden * half).astype(LOW)
    active_out[...] = active
    slope = half + 0.5 * GELU_A * hidden * (1.0 - wave * wave) * (1.0 + 3.0 * GELU_B * square)
    grad_hidden = (gate * pulled * slope).astype(LOW)
    hidden_out[...] = grad_hidden
    flush(hidden_out)
    grad_gate = jnp.sum(active.astype(FULL) * pulled, axis=1, keepdims=True)
    grad_logits = (gate * grad_gate * (jnp.where(mine, 1.0, 0.0) - chances)).astype(LOW)
    buffer_out[...] = (gate * cot[...].astype(FULL)).astype(LOW)
    gate_out[...] = gate
    router_out[...] = dot_tn(grad_logits, x[...])
    flush(router_out)
    part = dot_nt(grad_hidden, w_in[...]) + dot(grad_logits, router_t)
    part_keep[...] = part[0:rows, :]
    part_send[...] = part[rows:, :].astype(LOW)


def forward_kernel(
    first, first_gate, second, second_gate, w_out, keep, send, keep_far, send_far
):
    rows = keep.shape[0]
    part = second_gate[...] * dot(second[...], w_out[...])
    keep_far[...] = part[0:rows, :]
    send_far[...] = part[rows:, :].astype(LOW)
    part = first_gate[...] * dot(first[...], w_out[...])
    keep[...] = part[0:rows, :]
    keep.flush()
    send[...] = part[rows:, :].astype(LOW)


def join_kernel(keep, near, far, out):
    out[...] = (keep[...] + near[...].astype(FULL) + far[...].astype(FULL)).astype(LOW)


def grad_w_kernel(*refs):
    *parts, out = refs
    lefts, rights = parts[:-2], parts[-2:]

    def whole(parts):
        return jnp.concatenate([part[...] for part in parts], axis=0)

    out[0] = dot_tn(whole(lefts), whole(rights))


def back_kernel(gain_row, middle, cot, spread, back, small, grad_middle, grad_low, grad_gain):
    grad_two = dot(spread[...], back[...])
    values = middle[...]
    root = root_of(values)
    normed = values * root
    scaled = grad_two * small[gain_row : gain_row + 1, :]
    grad_gain[...] = jnp.sum(grad_two * normed, axis=0, keepdims=True)
    total = cot[...].astype(FULL) + root * (
        scaled - normed * jnp.mean(scaled * normed, axis=1, keepdims=True)
    )
    grad_middle[...] = total
    grad_low[...] = total.astype(LOW)


def attend_back_kernel(
    heads,
    scalars,
    own,
    far,
    near,
    near_far,
    attended,
    weights,
    qkv,
    *refs,
):
    probs, (ones, grads) = refs[:heads], refs[heads : heads + 2]
    *ring_rows, grad_w, joined, flipped = refs[heads + 2 :]
    rows = own.shape[0]
    local = attended.shape[1]
    joined[0:rows, :] = own[...]
    joined[rows : 2 * rows, :] = far[...]
    joined[2 * rows : 3 * rows, :] = near[...]
    joined[3 * rows :, :] = near_far[...]
    grad_w[:, 3 * local :] = dot_tn(joined[...], attended[...]).astype(LOW)
    w_out_t = weights[:, 3 * local :]
    grad_attended = dot(joined[...], w_out_t).astype(LOW)
    for h in range(heads):
        at = h * HEAD_DIM
        q = qkv[:, at : at + HEAD_DIM]
        k = qkv[:, local + at : local + at + HEAD_DIM]
        v = qkv[:, 2 * local + at : 2 * local + at + HEAD_DIM]
        upstream = grad_attended[:, at : at + HEAD_DIM]
        grad_p = dot_nt(upstream, v)
        low = probs[h][...]
        p = low.astype(FULL)
        inner = jnp.sum(p * grad_p, axis=1, keepdims=True)
        grad_s = (p * (grad_p - inner)).astype(LOW)
        grads[:, at : at + HEAD_DIM] = (dot(grad_s, k) * SCALE).astype(LOW)
        flipped[at : at + HEAD_DIM, :] = dot_tn(q, grad_s) * SCALE
        flipped[local + at : local + at + HEAD_DIM, :] = dot_tn(upstream, low)
    grads[:, local:] = flipped[...].T.astype(LOW)
    grad_w[:, 0 : 3 * local] = dot_tn(ones[...], grads[...]).astype(LOW)
    if ring_rows:
        top, bottom, rest = ring_rows
        middle = top.shape[0]
        shard = middle + bottom.shape[0]
        count = grad_w.shape[0] // shard
        place = ring_place(scalars[0], count)

        def start_of(step):
            return pl.multiple_of(ring_source(place + step, count) * shard, 16)

        start = start_of(count // 2)
        top[...] = grad_w[pl.ds(start, middle), :]
        bottom[...] = grad_w[pl.ds(pl.multiple_of(start + middle, 16), shard - middle), :]
        steps = [sign * k for k in range(count // 2 - 1, 0, -1) for sign in (1, -1)] + [0]
        for index, step in enumerate(steps):
            rest[index * shard : (index + 1) * shard, :] = grad_w[pl.ds(start_of(step), shard), :]


def grad_one_kernel(
    experts,
    grads,
    weights,
    group,
    router_one,
    router_two,
    gain_two,
    keep,
    keep_far,
    send,
    send_far,
    payload,
):
    rows = keep.shape[0]
    w_qkv = weights[:, 0 : grads.shape[1]]
    gain_one = None
    for index, out in enumerate((keep, keep_far, send, send_far)):
        at = slice(index * rows, (index + 1) * rows)
        part = dot_nt(grads[at, :], w_qkv)
        out[...] = part.astype(out.dtype)
        values = group[at, :].astype(FULL)
        gain = jnp.sum(part * (values * root_of(values)), axis=0, keepdims=True)
        gain_one = gain if gain_one is None else gain_one + gain
        if index == 0:
            keep.flush()
    owners, height, shard = payload.shape
    whole = jnp.concatenate(
        [
            router_one[...] + router_two[...],
            gain_one,
            gain_two[...],
            jnp.zeros((height - experts - 2, gain_one.shape[1]), FULL),
        ],
        axis=0,
    )
    for d in range(owners):
        payload[d] = whole[:, d * shard : (d + 1) * shard]


def last_kernel(
    experts,
    tokens,
    keep,
    near,
    far,
    grad_middle,
    small,
    middle,
    spread,
    back,
    grad_tokens,
    result,
):
    values = tokens[...].astype(FULL)
    root = root_of(values)
    normed = values * root
    grad_one = keep[...] + near[...].astype(FULL) + far[...].astype(FULL)
    scaled = grad_one * small[experts : experts + 1, :]
    grad_tokens[...] = grad_middle[...] + root * (
        scaled - normed * jnp.mean(scaled * normed, axis=1, keepdims=True)
    )
    grad_tokens.flush()
    result[...] = (middle[...] + dot(spread[...], back[...])).astype(LOW)


def ring_add_kernel(rest, ahead, behind, to_right, to_left, left_over):
    shard = to_right.shape[0]
    left_over[...] = rest[2 * shard :, :]
    if ahead.shape[0] == shard:
        to_right[...] = (rest[0:shard, :].astype(FULL) + ahead[...].astype(FULL)).astype(LOW)
        to_left[...] = (
            rest[shard : 2 * shard, :].astype(FULL) + behind[...].astype(FULL)
        ).astype(LOW)
        return
    middle = ahead.shape[0]
    to_right[0:middle, :] = (rest[0:middle, :].astype(FULL) + ahead[...].astype(FULL)).astype(LOW)
    to_right[middle:, :] = rest[middle:shard, :]
    to_left[0:middle, :] = rest[shard : shard + middle, :]
    to_left[middle:, :] = (
        rest[shard + middle : 2 * shard, :].astype(FULL) + behind[...].astype(FULL)
    ).astype(LOW)


def write_sums(total, query, key, value, out):
    local = query.shape[1]
    query[...] = total[:, 0:local]
    key[...] = total[:, local : 2 * local]
    value[...] = total[:, 2 * local : 3 * local]
    out[...] = total[:, 3 * local :].T


def ring_last_kernel(experts, mine, ahead, behind, parts, query, key, value, out, *small):
    total = mine[...].astype(FULL) + (ahead[...].astype(FULL) + behind[...].astype(FULL))
    write_sums(total, query, key, value, out)
    write_small(experts, parts, *small)


def write_small(experts, parts, gain_one, gain_two, router):
    total = jnp.sum(parts[...], axis=0)
    router[...] = total[0:experts, :]
    gain_one[...] = total[experts : experts + 1, :]
    gain_two[...] = total[experts + 1 : experts + 2, :]


def sum_kernel(experts, blocks, parts, query, key, value, out, *small):
    total = blocks[0].astype(FULL)
    for d in range(1, blocks.shape[0]):
        total = total + blocks[d].astype(FULL)
    write_sums(total, query, key, value, out)
    write_small(experts, parts, *small)


def on_device(
    tokens,
    lengths,
    routes,
    norm_attn,
    w_query,
    w_key,
    w_value,
    w_attn_out,
    norm_moe,
    w_router,
    w_expert_in,
    w_expert_out,
    cotangent,
):
    owners = lax.axis_size("dp")
    expert_index = lax.axis_index("dp")
    piece_index = lax.axis_index("tensor")
    piece_rows, width = tokens.shape
    shard, local = w_query.shape
    experts = w_router.shape[1]
    capacity = 3 * piece_rows // (2 * experts)
    slots = experts * capacity
    heads = local // HEAD_DIM
    total_rows = 4 * piece_rows
    small_rows = -(-(experts + 2) // 16) * 16
    scalars = jnp.concatenate(
        [jnp.stack([expert_index, piece_index]).astype(jnp.int32), lengths[0]]
    )
    sequences = lengths.shape[1]

    (packed,) = kernel_call(
        pack_kernel, [((shard + small_rows, 4 * local), LOW)], "pack", fetch=range(7)
    )(
        w_query,
        w_key,
        w_value,
        w_attn_out,
        w_router.T,
        norm_attn.reshape(1, shard),
        norm_moe.reshape(1, shard),
    )
    has_blocks = shard % 16 == 0
    scratch = []
    if has_blocks:
        behind, ahead, top, bottom = ring_gather(packed)
        partial = kernel_call(
            functools.partial(assemble_kernel, owners),
            [((width, 4 * local), LOW), ((owners, small_rows, shard), FULL)],
            "assemble",
            smem=(0,),
        )(scalars, packed, *behind, *ahead)
        blocks = [*partial, top, bottom]
        early, late = behind[0], (ahead[-1], behind[-1])
        scratch = [pltpu.VMEM((owners, small_rows, shard), FULL)]
    else:
        gathered = lax.all_gather(packed, "dp", axis=0, tiled=False)
        flat = gathered[:, shard:, :shard].transpose(1, 0, 2).reshape(small_rows, width)
        blocks = [gathered[:, :shard].reshape(width, 4 * local), flat.astype(FULL)]
        early, late = packed, (blocks[1],)
    token_far = swap_far(tokens)
    token_near = swap_near(tokens)

    spread, cot_rows = kernel_call(
        functools.partial(spread_kernel, capacity, slots),
        [((piece_rows, slots), LOW), ((slots, width), LOW)],
        "spread",
        smem=(0,),
        fetch=(1, 2),
        store=(0,),
        time=2,
        wait=(early,),
    )(scalars, routes, cotangent)
    token_near_far = swap_near(token_far)

    cot_rows = add(cot_rows, wait=late)
    cot_own = exchange(cot_rows.reshape(experts, capacity, width))
    cot_own = cot_own.reshape(slots, width)

    outs = [
        ((piece_rows, width), FULL),
        ((piece_rows, width), FULL),
        ((piece_rows, width), LOW),
        ((piece_rows, width), LOW),
        ((total_rows, width), LOW),
        ((total_rows, 3 * local), LOW),
        ((total_rows, local), LOW),
        ((total_rows, width), LOW),
    ]
    outs += [((total_rows, total_rows), LOW)] * heads
    if has_blocks:
        outs += [((width, 4 * local), LOW), ((small_rows, width), FULL)]
    made = kernel_call(
        functools.partial(attend_kernel, owners, sequences, has_blocks),
        outs,
        "attend",
        smem=(0,),
        fetch=(1,),
        store=(5, *range(8, 8 + heads)),
        scratch=scratch,
        time=4,
    )(scalars, tokens, token_far, token_near, token_near_far, *blocks)
    keep, keep_far, send, send_far = made[:4]
    ones, qkv, attended, group, *probs = made[4 : 8 + heads]
    weights, small = made[8 + heads :] if has_blocks else blocks

    def scatter(keep_far, send, send_far, wait=()):
        near_far = swap_near(send_far)
        near = swap_near(send)
        (out,) = kernel_call(far_kernel, [(keep_far.shape, LOW)], "far", time=0.1, wait=wait)(
            keep_far, near_far
        )
        return near, swap_far(out), out

    near, far, mark = scatter(keep_far, send, send_far)
    small_now = small
    ones, attended, group, small, weights = save(
        ones, attended, group, small, weights, wait=(mark,)
    )
    tokens_here, spread_here = load(tokens, spread, wait=(mark, cot_own))
    middle, own_rows = kernel_call(
        functools.partial(middle_kernel, experts + 1),
        [((piece_rows, width), FULL), ((slots, width), LOW)],
        "middle",
        wait_hbm=(ones,),
    )(tokens_here, keep, near, far, small_now, spread_here)
    (middle,) = save(middle, wait=(own_rows,))

    def over_dp(rows):
        return exchange(rows.reshape(experts, capacity, width)).reshape(slots, width)

    own = over_dp(own_rows)
    cot_far = swap_far(cot_own)
    cot_near = swap_near(cot_own)
    cot_near_far = swap_near(cot_far)
    (small_expert,) = load(small, wait=(own_rows,))
    own = add(own, wait=(small_expert, cot_far), wait_hbm=(middle,))
    own_far = swap_far(own)
    own_near = swap_near(own)
    weight_in = w_expert_in[0]
    weight_out = w_expert_out[0]
    hidden_size = weight_in.shape[1]

    def expert_part(x_keep, x_send, cot_keep, cot_send, store):
        rows = 2 * slots
        return kernel_call(
            functools.partial(expert_kernel, experts),
            [
                ((slots, width), FULL),
                ((slots, width), LOW),
                ((rows, hidden_size), LOW),
                ((rows, hidden_size), LOW),
                ((rows, width), LOW),
                ((rows, 1), FULL),
                ((experts, width), FULL),
                ((rows, width), LOW),
            ],
            "expert",
            smem=(0,),
            store=store,
            time=4,
            scratch=[pltpu.VMEM((rows, width), LOW)],
        )(scalars, x_keep, x_send, cot_keep, cot_send, weight_in, weight_out, small_expert)

    keep, send, active_one, hidden_one, buffer_one, gate_one, router_one, rows_one = expert_part(
        own, own_near, cot_own, cot_near, (0, 3, 6, 7)
    )
    own_far = add(own_far, wait=(send,))
    keep_far, send_far, active_two, hidden_two, buffer_two, gate_two, router_two, rows_two = (
        expert_part(own_far, swap_near(own_far), cot_far, cot_near_far, ())
    )
    near, far, mark = scatter(keep_far, send, send_far)
    (keep,) = load(keep, wait=(mark,))
    rows_two, hidden_two, router_two = save(rows_two, hidden_two, router_two, wait=(mark,))
    forward_keep, forward_send, forward_keep_far, forward_send_far = kernel_call(
        forward_kernel,
        [((slots, width), kind) for kind in (FULL, LOW, FULL, LOW)],
        "forward",
        store=(0,),
        time=2,
        wait=(mark,),
    )(active_one, gate_one, active_two, gate_two, weight_out)
    (grad_expert_out,) = kernel_call(
        grad_w_kernel, [((1, *weight_out.shape), FULL)], "grad_out", store=(0,), time=3, wait=(mark,)
    )(active_one, active_two, buffer_one, buffer_two)
    (back_rows,) = kernel_call(
        join_kernel,
        [((slots, width), LOW)],
        "join",
        wait=(forward_send,),
        wait_hbm=(grad_expert_out, hidden_two),
    )(keep, near, far)
    back = over_dp(back_rows)
    out_near, out_far, out_mark = scatter(
        forward_keep_far, forward_send, forward_send_far, wait=(back_rows,)
    )
    (grad_expert_in,) = kernel_call(
        grad_w_kernel, [((1, *weight_in.shape), FULL)], "grad_in", fetch=range(4), store=(0,), time=3
    )(rows_one, rows_two, hidden_one, hidden_two)
    middle_here, cot_here, spread_here, small_here, forward_here = load(
        middle, cotangent, spread, small, forward_keep, wait=(out_mark,)
    )
    (out_rows,) = kernel_call(join_kernel, [((slots, width), LOW)], "join", time=0.1)(
        forward_here, out_near, out_far
    )
    out_back = over_dp(out_rows)

    grad_middle, grad_low, grad_gain_two = kernel_call(
        functools.partial(back_kernel, experts + 1),
        [((piece_rows, width), FULL), ((piece_rows, width), LOW), ((1, width), FULL)],
        "back",
        wait=(out_far,),
        wait_hbm=(grad_expert_in,),
    )(middle_here, cot_here, spread_here, back, small_here)
    grad_far = swap_far(grad_low)
    grad_near = swap_near(grad_low)
    grad_far = add(grad_far, wait=(out_rows,))
    grad_near_far = swap_near(grad_far)
    outs = [((total_rows, 3 * local), LOW)]
    middle_row = shard // 32 * 16
    scratch = [
        pltpu.VMEM((total_rows, width), LOW),
        pltpu.VMEM((2 * local, total_rows), FULL),
    ]
    if has_blocks:
        outs += [
            ((middle_row, 4 * local), LOW),
            ((shard - middle_row, 4 * local), LOW),
            ((width - shard, 4 * local), LOW),
        ]
        scratch = [pltpu.VMEM((width, 4 * local), LOW)] + scratch
    else:
        outs.append(((width, 4 * local), LOW))
    grads, *grad_w = kernel_call(
        functools.partial(attend_back_kernel, heads),
        outs,
        "attend_back",
        smem=(0,),
        fetch=range(5, 9 + heads),
        first=3 + heads,
        time=2,
        scratch=scratch,
    )(
        *(scalars, grad_low, grad_far, grad_near, grad_near_far),
        *(attended, weights, qkv, *probs, ones),
    )
    last = [((shard, local), FULL)] * 3 + [((local, shard), FULL)]
    held = {}

    def first(mark):
        keep, keep_far, send, send_far, payload = kernel_call(
            functools.partial(grad_one_kernel, experts),
            [((piece_rows, width), kind) for kind in (FULL, FULL, LOW, LOW)]
            + [((owners, small_rows, shard), FULL)],
            "grad_one",
            fetch=(1, 2, 3, 4),
            store=(0,),
            time=0.2,
            wait=(mark,),
        )(grads, weights, group, router_one, router_two, grad_gain_two)
        held["keep"], held["keep_far"] = keep, keep_far
        held["near_far"], held["near"] = swap_near(send_far), swap_near(send)
        held["small"] = (payload, swap(payload, "tensor", 1))
        return (send,), (), ()

    def second(mark):
        out_shape = [(held["keep_far"].shape, LOW)]
        (out,) = kernel_call(far_kernel, out_shape, "far", time=0.1, wait=(mark,))(
            held["keep_far"], held["near_far"]
        )
        held["far"] = swap_far(out)
        total = add(*held["small"], wait=(mark,))
        came = swap(total, "tensor", 2)
        held["small"] = (total, came)
        held["middle"] = save(grad_middle, wait=(mark,))
        return (out, total), (came,), held["middle"]

    def third(mark):
        total = add(*held["small"], wait=(mark,))
        held["small"] = exchange(total)
        return (total,), (held["far"],), ()

    def fourth(mark):
        held["last"] = kernel_call(
            functools.partial(last_kernel, experts),
            [
                ((piece_rows, width), FULL),
                ((piece_rows, width), LOW),
            ],
            "last",
            fetch=(0, 1, 4, 5, 6, 7),
            store=(0, 1),
            time=0.3,
            wait=(mark,),
        )(
            *(tokens, held["keep"], held["near"], held["far"]),
            *(*held["middle"], small, middle, spread, out_back),
        )
        return (), (), ()

    fillers = (first, second, third, fourth)
    last += [((1, shard), FULL), ((1, shard), FULL), ((experts, shard), FULL)]
    if has_blocks:
        parts = ring_reduce(*grad_w, shard, fillers, (out_back,))
        sums = kernel_call(
            functools.partial(ring_last_kernel, experts),
            last,
            "ring_last",
            store=range(7),
            wait_hbm=held["last"][:1],
        )(*parts, held["small"])
    else:
        for filler in fillers:
            filler(grad_w[0])
        sums = kernel_call(
            functools.partial(sum_kernel, experts), last, "sum", store=range(7)
        )(exchange(grad_w[0].reshape(owners, shard, 4 * local)), held["small"])
    grad_query, grad_key, grad_value, grad_out, grad_norm_attn, grad_norm_moe, grad_router = sums
    grad_tokens, result = held["last"]
    return (
        result,
        grad_tokens,
        grad_norm_attn.reshape(shard),
        grad_query,
        grad_key,
        grad_value,
        grad_out,
        grad_norm_moe.reshape(shard),
        grad_router.T,
        grad_expert_in,
        grad_expert_out,
    )


def solution(mesh):
    return jax.shard_map(
        on_device,
        mesh=mesh,
        in_specs=(
            P(("dp", "tensor"), None),
            P("dp", None),
            P("dp", None),
            P("dp"),
            P("dp", "tensor"),
            P("dp", "tensor"),
            P("dp", "tensor"),
            P("tensor", "dp"),
            P("dp"),
            P("dp", None),
            P("dp", None, "tensor"),
            P("dp", "tensor", None),
            P(("dp", "tensor"), None),
        ),
        out_specs=(
            P(("dp", "tensor"), None),
            P(("dp", "tensor"), None),
            P("dp"),
            P("dp", "tensor"),
            P("dp", "tensor"),
            P("dp", "tensor"),
            P("tensor", "dp"),
            P("dp"),
            P("dp", None),
            P("dp", None, "tensor"),
            P("dp", "tensor", None),
        ),
        check_vma=False,
    )
```

```python
import functools

import jax
import jax.numpy as jnp
from jax import lax
from jax.experimental import pallas as pl
from jax.experimental.pallas import tpu as pltpu
from jax.sharding import PartitionSpec as P

HEAD_DIM = 64
EPSILON = 1e-06
NEGATIVE = -1e30
LOW = jnp.bfloat16
FULL = jnp.float32
SCALE = HEAD_DIM ** (-0.5)
MIB = 1 << 20


def dot(a, b):
    return jnp.dot(a, b, preferred_element_type=FULL)


def dot_nt(a, b):
    return lax.dot_general(a, b, (((1,), (1,)), ((), ())), preferred_element_type=FULL)


def dot_tn(a, b):
    return lax.dot_general(a, b, (((0,), (0,)), ((), ())), preferred_element_type=FULL)


class Fetched:
    def __init__(self, ref, held, sem, late):
        self.held, self.waiting, self.late = held, True, late
        self.copy = pltpu.make_async_copy(ref, held, sem)
        self.shape = held.shape

    def wait(self):
        if self.waiting:
            self.copy.wait()
            self.waiting = False
            while self.late:
                self.late.pop(0).copy.start()

    def __getitem__(self, index):
        self.wait()
        return self.held[index]


class Stored:
    def __init__(self, ref, held, sem):
        self.ref, self.held, self.sem = ref, held, sem
        self.copy = None
        self.shape, self.dtype = held.shape, held.dtype

    def __getitem__(self, index):
        return self.held[index]

    def __setitem__(self, index, value):
        self.held[index] = value

    def flush(self):
        if self.copy is None:
            self.copy = pltpu.make_async_copy(self.held, self.ref, self.sem)
            self.copy.start()


def kernel_call(body, outs, name, fetch=(), store=(), smem=(), time=1, limit=24, scratch=(), wait=(), wait_hbm=(), first=99):
    def call(*operands):
        n_in, n_out, n_scratch = len(operands), len(outs), len(scratch)
        held = [pltpu.VMEM(operands[i].shape, operands[i].dtype) for i in fetch]
        held += [pltpu.VMEM(*outs[i]) for i in store]
        sems = [pltpu.SemaphoreType.DMA((len(held),))] if held else []

        def kernel(*refs):
            ins, refs = list(refs[:n_in]), refs[n_in + len(wait) + len(wait_hbm) :]
            results, rest = list(refs[:n_out]), refs[n_out:]
            own, buffers = rest[:n_scratch], rest[n_scratch : n_scratch + len(held)]
            sem = rest[-1] if held else None
            at, late = 0, []
            for i in fetch:
                ins[i] = Fetched(ins[i], buffers[at], sem.at[at], late)
                if at < first:
                    ins[i].copy.start()
                else:
                    late.append(ins[i])
                at += 1
            for i in store:
                results[i] = Stored(results[i], buffers[at], sem.at[at])
                at += 1
            body(*ins, *results, *own)
            for i in fetch:
                ins[i].wait()
            for i in store:
                results[i].flush()
            for i in store:
                results[i].copy.wait()

        def spec(i, hbm):
            return pl.BlockSpec(memory_space=pltpu.HBM if i in hbm else pltpu.VMEM)


        operands = [
            pltpu.with_memory_space_constraint(x, pltpu.HBM) if i in fetch else x
            for i, x in enumerate(operands)
        ]
        return pl.pallas_call(
            kernel,
            out_shape=[
                pltpu.HBM(*outs[i]) if i in store else jax.ShapeDtypeStruct(*outs[i])
                for i in range(n_out)
            ],
            in_specs=[
                pl.BlockSpec(memory_space=pltpu.SMEM) if i in smem else spec(i, fetch)
                for i in range(n_in)
            ]
            + [pl.BlockSpec(memory_space=pl.ANY) for _ in wait]
            + [pl.BlockSpec(memory_space=pltpu.HBM) for _ in wait_hbm],
            out_specs=[spec(i, store) for i in range(n_out)],
            scratch_shapes=[*scratch, *held, *sems],
            compiler_params=pltpu.CompilerParams(vmem_limit_bytes=limit * MIB),
            cost_estimate=pl.CostEstimate(
                flops=int(time * 1.1e9), bytes_accessed=MIB, transcendentals=0
            ),
            name=name,
        )(
            *operands,
            *wait,
            *(pltpu.with_memory_space_constraint(x, pltpu.HBM) for x in wait_hbm),
        )

    return call


def move_kernel(count, *refs):
    sources, targets, sem = refs[:count], refs[-1 - count : -1], refs[-1]
    copies = [
        pltpu.make_async_copy(source, target, sem.at[k])
        for k, (source, target) in enumerate(zip(sources, targets))
    ]
    for copy in copies:
        copy.start()
    for copy in copies:
        copy.wait()


def moved(arrays, source, target, name, wait):
    kinds = [(x.shape, x.dtype) for x in arrays]
    if source is pltpu.HBM:
        arrays = [pltpu.with_memory_space_constraint(x, pltpu.HBM) for x in arrays]
    return pl.pallas_call(
        functools.partial(move_kernel, len(kinds)),
        out_shape=[
            pltpu.HBM(*kind) if target is pltpu.HBM else jax.ShapeDtypeStruct(*kind)
            for kind in kinds
        ],
        in_specs=[pl.BlockSpec(memory_space=source) for _ in kinds]
        + [pl.BlockSpec(memory_space=pl.ANY) for _ in wait],
        out_specs=[pl.BlockSpec(memory_space=target) for _ in kinds],
        scratch_shapes=[pltpu.SemaphoreType.DMA((len(kinds),))],
        compiler_params=pltpu.CompilerParams(vmem_limit_bytes=16 * MIB),
        cost_estimate=pl.CostEstimate(flops=2 * 10**9, bytes_accessed=MIB, transcendentals=0),
        name=name,
    )(*arrays, *wait)


def save(*arrays, wait=()):
    return moved(arrays, pltpu.VMEM, pltpu.HBM, "save", wait)


def load(*arrays, wait=()):
    return moved(arrays, pltpu.HBM, pltpu.VMEM, "load", wait)


def swap(values, axis, bit):
    count = lax.axis_size(axis)
    return lax.ppermute(values, axis, [(i, i ^ bit) for i in range(count)])


def exchange(buffer):
    return lax.all_to_all(buffer, "dp", split_axis=0, concat_axis=0, tiled=True)


def swap_far(rows):
    return swap(rows, "tensor", 2)


def swap_near(rows):
    return swap(rows, "tensor", 1)


def ring_source(place, count):
    place = lax.rem(place + 2 * count, count)
    return jnp.where(place < count // 2, 2 * place, 2 * (count - 1 - place) + 1)


def ring_perms(count):
    order = list(range(0, count, 2)) + list(range(1, count, 2))[::-1]
    right = [(order[k], order[(k + 1) % count]) for k in range(count)]
    return right, [(b, a) for a, b in right]


def ring_gather(block):
    count = lax.axis_size("dp")
    right, left = ring_perms(count)
    behind, ahead = [block], [block]
    for _ in range(1, count // 2):
        behind.append(lax.ppermute(behind[-1], "dp", right))
        ahead.append(lax.ppermute(ahead[-1], "dp", left))
    middle = block.shape[0] // 32 * 16
    top = lax.ppermute(behind[-1][:middle], "dp", right)
    bottom = lax.ppermute(ahead[-1][middle:], "dp", left)
    return behind[1:], ahead[1:], top, bottom


def ring_place(me, count):
    return jnp.where(lax.rem(me, 2) == 0, me // 2, count - 1 - me // 2)


def fence_kernel(source, out):
    out[...] = source[0 : out.shape[0], 0 : out.shape[1]].astype(out.dtype)


def fence(source, wait=()):
    (out,) = kernel_call(fence_kernel, [((16, 128), LOW)], "fence", time=40, wait=wait)(source)
    return out


def add_kernel(*refs):
    total = refs[0][...].astype(FULL)
    for ref in refs[1:-1]:
        total = total + ref[...].astype(FULL)
    refs[-1][...] = total.astype(refs[-1].dtype)


def add(*values, wait=(), wait_hbm=()):
    kind = (values[0].shape, values[0].dtype)
    return kernel_call(add_kernel, [kind], "add", time=0.1, wait=wait, wait_hbm=wait_hbm)(*values)[0]


def ring_reduce(top, bottom, rest, shard, fillers, arrived=()):
    count = lax.axis_size("dp")
    right, left = ring_perms(count)
    width = rest.shape[1]
    ahead = lax.ppermute(top, "dp", right)
    behind = lax.ppermute(bottom, "dp", left)
    done, kept = (), ()
    for index, step in enumerate(range(count // 2 - 1, -1, -1)):
        if index < len(fillers):
            done, arrived, kept = fillers[index](fence(rest, arrived))
        if not step:
            return rest, ahead, behind
        block = (shard, width)
        to_right, to_left, rest = kernel_call(
            ring_add_kernel,
            [(block, LOW), (block, LOW), ((rest.shape[0] - 2 * shard, width), LOW)],
            "ring_add",
            wait=done,
            wait_hbm=kept,
        )(rest, ahead, behind)
        ahead = lax.ppermute(to_right, "dp", right)
        behind = lax.ppermute(to_left, "dp", left)


def root_of(values):
    return lax.rsqrt(jnp.mean(values * values, axis=1, keepdims=True) + EPSILON)


def pack_kernel(wq, wk, wv, wo, router, gain_one, gain_two, out):
    shard, local = wq.shape
    out[0:shard, 0:local] = wq[...]
    out[0:shard, local : 2 * local] = wk[...]
    out[0:shard, 2 * local : 3 * local] = wv[...]
    out[0:shard, 3 * local :] = wo[...].astype(FULL).T.astype(LOW)
    experts = router.shape[0]
    rows = out.shape[0] - shard
    small = jnp.concatenate(
        [
            router[...].astype(FULL),
            gain_one[...].astype(FULL),
            gain_two[...].astype(FULL),
            jnp.zeros((rows - experts - 2, shard), FULL),
        ],
        axis=0,
    )
    out[shard:, :] = jnp.zeros((rows, out.shape[1]), LOW)
    out[shard:, 0:shard] = small.astype(LOW)


def spread_kernel(capacity, slots, scalars, routes, cot, spread, rows):
    count = cot.shape[0]
    piece = scalars[1]
    route = routes[pl.ds(pl.multiple_of(piece * count, count), count), :]
    experts = slots // capacity
    ids = lax.broadcasted_iota(jnp.int32, (count, experts), 1)
    chosen = jnp.where(route == ids, 1.0, 0.0)
    first = lax.broadcasted_iota(jnp.int32, (count, count), 0)
    second = lax.broadcasted_iota(jnp.int32, (count, count), 1)
    before = jnp.where(second < first, 1.0, 0.0).astype(LOW)
    earlier = dot(before, chosen.astype(LOW))
    slot = jnp.sum(earlier * chosen, axis=1, keepdims=True).astype(jnp.int32)
    place = route * capacity + slot
    lanes = lax.broadcasted_iota(jnp.int32, (count, slots), 1)
    one_hot = jnp.where(place == lanes, 1.0, 0.0).astype(LOW)
    spread[...] = one_hot
    rows[...] = dot_tn(one_hot, cot[...]).astype(LOW)


def assemble_kernel(count, scalars, *refs):
    blocks, (weights, smalls) = refs[:-2], refs[-2:]
    me = scalars[0]
    place = ring_place(me, count)
    shard = weights.shape[0] // count
    half = count // 2
    steps = [0] + [-s for s in range(1, half)] + list(range(1, half))
    for step, block in zip(steps, blocks):
        source = ring_source(place + step, count) if step else me
        weights[pl.ds(pl.multiple_of(source * shard, 16), shard), :] = block[0:shard, :]
        smalls[source] = block[shard:, 0:shard].astype(FULL)


def finish_small(count, scalars, blocks, smalls, small_out):
    smalls[...] = blocks[1][...]
    top, bottom = blocks[2:]
    shard = smalls.shape[2]
    source = ring_source(ring_place(scalars[0], count) + count // 2, count)
    smalls[source] = bottom[shard - top.shape[0] :, 0:shard].astype(FULL)
    for d in range(count):
        small_out[:, d * shard : (d + 1) * shard] = smalls[d]


def finish(count, scalars, blocks, weights):
    shard = weights.shape[0] // count
    weights[...] = blocks[0][...]
    top, bottom = blocks[2:]
    source = ring_source(ring_place(scalars[0], count) + count // 2, count)
    middle = top.shape[0]
    start = pl.multiple_of(source * shard, 16)
    rest = shard - middle
    weights[pl.ds(start, middle), :] = top[...]
    weights[pl.ds(pl.multiple_of(start + middle, 16), rest), :] = bottom[0:rest, :]


def positions_of(piece, rows, shape, dim):
    index = lax.broadcasted_iota(jnp.int32, shape, dim)
    block = index // rows
    flip = jnp.where(block == 1, 2, jnp.where(block == 2, 1, block))
    return (piece ^ flip) * rows + lax.rem(index, rows)


def attend_kernel(count, sequences, has_blocks, *refs):
    scalars, tokens, far, near, near_far = refs[:5]
    given = 4 if has_blocks else 2
    blocks = refs[5 : 5 + given]
    outs = refs[5 + given :]
    heads = len(outs) - (11 if has_blocks else 8)
    keep, keep_far, send, send_far, ones, qkv_out, attended, group = outs[:8]
    probs_out = outs[8 : 8 + heads]
    if has_blocks:
        weights, small, smalls = outs[8 + heads :]
        finish_small(count, scalars, blocks, smalls, small)
    else:
        weights, small = blocks
    rows = tokens.shape[0]
    total = 4 * rows
    local = attended.shape[1]
    experts = count
    gain = small[experts : experts + 1, :]
    piece = scalars[1]
    for index, ref in ((1, far), (2, near), (3, near_far), (0, tokens)):
        group[index * rows : (index + 1) * rows, :] = ref[...]
        values = ref[...].astype(FULL)
        ones[index * rows : (index + 1) * rows, :] = (values * root_of(values) * gain).astype(LOW)
    if has_blocks:
        finish(count, scalars, blocks, weights)
    qkv = dot(ones[...], weights[:, 0 : 3 * local]).astype(LOW)
    qkv_out[...] = qkv
    qkv_out.flush()
    query_pos = positions_of(piece, rows, (total, 1), 0)
    key_pos = positions_of(piece, rows, (1, total), 1)
    start = jnp.zeros((total, 1), jnp.int32)
    end = jnp.int32(0)
    for s in range(sequences):
        end = end + scalars[2 + s]
        start = jnp.where(query_pos >= end, end, start)
    bias = jnp.where((key_pos <= query_pos) & (key_pos >= start), 0.0, NEGATIVE)
    for h in range(local // HEAD_DIM):
        at = h * HEAD_DIM
        q = qkv[:, at : at + HEAD_DIM]
        k = qkv[:, local + at : local + at + HEAD_DIM]
        v = qkv[:, 2 * local + at : 2 * local + at + HEAD_DIM]
        scores = dot_nt(q, k) * SCALE + bias
        shifted = jnp.exp(scores - jnp.max(scores, axis=1, keepdims=True))
        probs = (shifted * (1.0 / jnp.sum(shifted, axis=1, keepdims=True))).astype(LOW)
        probs_out[h][...] = probs
        attended[:, at : at + HEAD_DIM] = dot(probs, v).astype(LOW)
    for probs in probs_out:
        probs.flush()
    w_out_t = weights[:, 3 * local :]
    keep[...] = dot_nt(attended[0:rows, :], w_out_t)
    keep_far[...] = dot_nt(attended[rows : 2 * rows, :], w_out_t)
    send[...] = dot_nt(attended[2 * rows : 3 * rows, :], w_out_t).astype(LOW)
    send_far[...] = dot_nt(attended[3 * rows :, :], w_out_t).astype(LOW)


def middle_kernel(gain_row, tokens, keep, near, far, small, spread, middle, rows):
    total = tokens[...].astype(FULL) + (
        keep[...] + near[...].astype(FULL) + far[...].astype(FULL)
    )
    middle[...] = total
    moe = (total * root_of(total) * small[gain_row : gain_row + 1, :]).astype(LOW)
    rows[...] = dot_tn(spread[...], moe).astype(LOW)


def far_kernel(keep_far, near, out):
    out[...] = (keep_far[...] + near[...].astype(FULL)).astype(LOW)


GELU_A = 0.7978845608028654
GELU_B = 0.044715


def flush(ref):
    if isinstance(ref, Stored):
        ref.flush()


def expert_kernel(
    experts,
    scalars,
    x_keep,
    x_send,
    cot_keep,
    cot_send,
    w_in,
    w_out,
    small,
    part_keep,
    part_send,
    active_out,
    hidden_out,
    buffer_out,
    gate_out,
    router_out,
    x,
    cot,
):
    rows = x_keep.shape[0]
    x[0:rows, :] = x_keep[...]
    x[rows:, :] = x_send[...]
    cot[0:rows, :] = cot_keep[...]
    cot[rows:, :] = cot_send[...]
    flush(x)
    hidden = dot(x[...], w_in[...])
    pulled = dot_nt(cot[...], w_out[...])
    router_t = small[0:experts, :].astype(LOW)
    mine = lax.broadcasted_iota(jnp.int32, (2 * rows, experts), 1) == scalars[0]
    logits = dot_nt(x[...], router_t)
    raised = jnp.exp(logits - jnp.max(logits, axis=1, keepdims=True))
    chances = raised / jnp.sum(raised, axis=1, keepdims=True)
    gate = jnp.sum(jnp.where(mine, chances, 0.0), axis=1, keepdims=True)
    square = hidden * hidden
    wave = jnp.tanh(GELU_A * hidden * (1.0 + GELU_B * square))
    half = 0.5 + 0.5 * wave
    active = (hidden * half).astype(LOW)
    active_out[...] = active
    slope = half + 0.5 * GELU_A * hidden * (1.0 - wave * wave) * (1.0 + 3.0 * GELU_B * square)
    grad_hidden = (gate * pulled * slope).astype(LOW)
    hidden_out[...] = grad_hidden
    flush(hidden_out)
    grad_gate = jnp.sum(active.astype(FULL) * pulled, axis=1, keepdims=True)
    grad_logits = (gate * grad_gate * (jnp.where(mine, 1.0, 0.0) - chances)).astype(LOW)
    buffer_out[...] = (gate * cot[...].astype(FULL)).astype(LOW)
    gate_out[...] = gate
    router_out[...] = dot_tn(grad_logits, x[...])
    flush(router_out)
    part = dot_nt(grad_hidden, w_in[...]) + dot(grad_logits, router_t)
    part_keep[...] = part[0:rows, :]
    part_send[...] = part[rows:, :].astype(LOW)


def forward_kernel(
    first, first_gate, second, second_gate, w_out, keep, send, keep_far, send_far
):
    rows = keep.shape[0]
    part = second_gate[...] * dot(second[...], w_out[...])
    keep_far[...] = part[0:rows, :]
    send_far[...] = part[rows:, :].astype(LOW)
    part = first_gate[...] * dot(first[...], w_out[...])
    keep[...] = part[0:rows, :]
    keep.flush()
    send[...] = part[rows:, :].astype(LOW)


def join_kernel(keep, near, far, out):
    out[...] = (keep[...] + near[...].astype(FULL) + far[...].astype(FULL)).astype(LOW)


def grad_w_kernel(*refs):
    *parts, out = refs
    lefts, rights = parts[:-2], parts[-2:]

    def whole(parts):
        return jnp.concatenate([part[...] for part in parts], axis=0)

    out[0] = dot_tn(whole(lefts), whole(rights))


def back_kernel(gain_row, middle, cot, spread, back, small, grad_middle, grad_low, grad_gain):
    grad_two = dot(spread[...], back[...])
    values = middle[...]
    root = root_of(values)
    normed = values * root
    scaled = grad_two * small[gain_row : gain_row + 1, :]
    grad_gain[...] = jnp.sum(grad_two * normed, axis=0, keepdims=True)
    total = cot[...].astype(FULL) + root * (
        scaled - normed * jnp.mean(scaled * normed, axis=1, keepdims=True)
    )
    grad_middle[...] = total
    grad_low[...] = total.astype(LOW)


def attend_back_kernel(
    heads,
    scalars,
    own,
    far,
    near,
    near_far,
    attended,
    weights,
    qkv,
    *refs,
):
    probs, (ones, grads) = refs[:heads], refs[heads : heads + 2]
    *ring_rows, grad_w, joined, flipped = refs[heads + 2 :]
    rows = own.shape[0]
    local = attended.shape[1]
    joined[0:rows, :] = own[...]
    joined[rows : 2 * rows, :] = far[...]
    joined[2 * rows : 3 * rows, :] = near[...]
    joined[3 * rows :, :] = near_far[...]
    grad_w[:, 3 * local :] = dot_tn(joined[...], attended[...]).astype(LOW)
    w_out_t = weights[:, 3 * local :]
    grad_attended = dot(joined[...], w_out_t).astype(LOW)
    for h in range(heads):
        at = h * HEAD_DIM
        q = qkv[:, at : at + HEAD_DIM]
        k = qkv[:, local + at : local + at + HEAD_DIM]
        v = qkv[:, 2 * local + at : 2 * local + at + HEAD_DIM]
        upstream = grad_attended[:, at : at + HEAD_DIM]
        grad_p = dot_nt(upstream, v)
        low = probs[h][...]
        p = low.astype(FULL)
        inner = jnp.sum(p * grad_p, axis=1, keepdims=True)
        grad_s = (p * (grad_p - inner)).astype(LOW)
        grads[:, at : at + HEAD_DIM] = (dot(grad_s, k) * SCALE).astype(LOW)
        flipped[at : at + HEAD_DIM, :] = dot_tn(q, grad_s) * SCALE
        flipped[local + at : local + at + HEAD_DIM, :] = dot_tn(upstream, low)
    grads[:, local:] = flipped[...].T.astype(LOW)
    grad_w[:, 0 : 3 * local] = dot_tn(ones[...], grads[...]).astype(LOW)
    if ring_rows:
        top, bottom, rest = ring_rows
        middle = top.shape[0]
        shard = middle + bottom.shape[0]
        count = grad_w.shape[0] // shard
        place = ring_place(scalars[0], count)

        def start_of(step):
            return pl.multiple_of(ring_source(place + step, count) * shard, 16)

        start = start_of(count // 2)
        top[...] = grad_w[pl.ds(start, middle), :]
        bottom[...] = grad_w[pl.ds(pl.multiple_of(start + middle, 16), shard - middle), :]
        steps = [sign * k for k in range(count // 2 - 1, 0, -1) for sign in (1, -1)] + [0]
        for index, step in enumerate(steps):
            rest[index * shard : (index + 1) * shard, :] = grad_w[pl.ds(start_of(step), shard), :]


def grad_one_kernel(
    experts,
    grads,
    weights,
    group,
    router_one,
    router_two,
    gain_two,
    keep,
    keep_far,
    send,
    send_far,
    payload,
):
    rows = keep.shape[0]
    w_qkv = weights[:, 0 : grads.shape[1]]
    gain_one = None
    for index, out in enumerate((keep, keep_far, send, send_far)):
        at = slice(index * rows, (index + 1) * rows)
        part = dot_nt(grads[at, :], w_qkv)
        out[...] = part.astype(out.dtype)
        values = group[at, :].astype(FULL)
        gain = jnp.sum(part * (values * root_of(values)), axis=0, keepdims=True)
        gain_one = gain if gain_one is None else gain_one + gain
        if index == 0:
            keep.flush()
    owners, height, shard = payload.shape
    whole = jnp.concatenate(
        [
            router_one[...] + router_two[...],
            gain_one,
            gain_two[...],
            jnp.zeros((height - experts - 2, gain_one.shape[1]), FULL),
        ],
        axis=0,
    )
    for d in range(owners):
        payload[d] = whole[:, d * shard : (d + 1) * shard]


def last_kernel(
    experts,
    tokens,
    keep,
    near,
    far,
    grad_middle,
    small,
    middle,
    spread,
    back,
    grad_tokens,
    result,
):
    values = tokens[...].astype(FULL)
    root = root_of(values)
    normed = values * root
    grad_one = keep[...] + near[...].astype(FULL) + far[...].astype(FULL)
    scaled = grad_one * small[experts : experts + 1, :]
    grad_tokens[...] = grad_middle[...] + root * (
        scaled - normed * jnp.mean(scaled * normed, axis=1, keepdims=True)
    )
    grad_tokens.flush()
    result[...] = (middle[...] + dot(spread[...], back[...])).astype(LOW)


def ring_add_kernel(rest, ahead, behind, to_right, to_left, left_over):
    shard = to_right.shape[0]
    left_over[...] = rest[2 * shard :, :]
    if ahead.shape[0] == shard:
        to_right[...] = (rest[0:shard, :].astype(FULL) + ahead[...].astype(FULL)).astype(LOW)
        to_left[...] = (
            rest[shard : 2 * shard, :].astype(FULL) + behind[...].astype(FULL)
        ).astype(LOW)
        return
    middle = ahead.shape[0]
    to_right[0:middle, :] = (rest[0:middle, :].astype(FULL) + ahead[...].astype(FULL)).astype(LOW)
    to_right[middle:, :] = rest[middle:shard, :]
    to_left[0:middle, :] = rest[shard : shard + middle, :]
    to_left[middle:, :] = (
        rest[shard + middle : 2 * shard, :].astype(FULL) + behind[...].astype(FULL)
    ).astype(LOW)


def write_sums(total, query, key, value, out):
    local = query.shape[1]
    query[...] = total[:, 0:local]
    key[...] = total[:, local : 2 * local]
    value[...] = total[:, 2 * local : 3 * local]
    out[...] = total[:, 3 * local :].T


def ring_last_kernel(experts, mine, ahead, behind, parts, query, key, value, out, *small):
    total = mine[...].astype(FULL) + (ahead[...].astype(FULL) + behind[...].astype(FULL))
    write_sums(total, query, key, value, out)
    write_small(experts, parts, *small)


def write_small(experts, parts, gain_one, gain_two, router):
    total = jnp.sum(parts[...], axis=0)
    router[...] = total[0:experts, :]
    gain_one[...] = total[experts : experts + 1, :]
    gain_two[...] = total[experts + 1 : experts + 2, :]


def sum_kernel(experts, blocks, parts, query, key, value, out, *small):
    total = blocks[0].astype(FULL)
    for d in range(1, blocks.shape[0]):
        total = total + blocks[d].astype(FULL)
    write_sums(total, query, key, value, out)
    write_small(experts, parts, *small)


def on_device(
    tokens,
    lengths,
    routes,
    norm_attn,
    w_query,
    w_key,
    w_value,
    w_attn_out,
    norm_moe,
    w_router,
    w_expert_in,
    w_expert_out,
    cotangent,
):
    owners = lax.axis_size("dp")
    expert_index = lax.axis_index("dp")
    piece_index = lax.axis_index("tensor")
    piece_rows, width = tokens.shape
    shard, local = w_query.shape
    experts = w_router.shape[1]
    capacity = 3 * piece_rows // (2 * experts)
    slots = experts * capacity
    heads = local // HEAD_DIM
    total_rows = 4 * piece_rows
    small_rows = -(-(experts + 2) // 16) * 16
    scalars = jnp.concatenate(
        [jnp.stack([expert_index, piece_index]).astype(jnp.int32), lengths[0]]
    )
    sequences = lengths.shape[1]

    (packed,) = kernel_call(
        pack_kernel, [((shard + small_rows, 4 * local), LOW)], "pack", fetch=range(7)
    )(
        w_query,
        w_key,
        w_value,
        w_attn_out,
        w_router.T,
        norm_attn.reshape(1, shard),
        norm_moe.reshape(1, shard),
    )
    has_blocks = shard % 16 == 0
    scratch = []
    if has_blocks:
        behind, ahead, top, bottom = ring_gather(packed)
        partial = kernel_call(
            functools.partial(assemble_kernel, owners),
            [((width, 4 * local), LOW), ((owners, small_rows, shard), FULL)],
            "assemble",
            smem=(0,),
        )(scalars, packed, *behind, *ahead)
        blocks = [*partial, top, bottom]
        early, late = behind[0], (ahead[-1], behind[-1])
        scratch = [pltpu.VMEM((owners, small_rows, shard), FULL)]
    else:
        gathered = lax.all_gather(packed, "dp", axis=0, tiled=False)
        flat = gathered[:, shard:, :shard].transpose(1, 0, 2).reshape(small_rows, width)
        blocks = [gathered[:, :shard].reshape(width, 4 * local), flat.astype(FULL)]
        early, late = packed, (blocks[1],)
    token_far = swap_far(tokens)
    token_near = swap_near(tokens)

    spread, cot_rows = kernel_call(
        functools.partial(spread_kernel, capacity, slots),
        [((piece_rows, slots), LOW), ((slots, width), LOW)],
        "spread",
        smem=(0,),
        fetch=(1, 2),
        store=(0,),
        time=2,
        wait=(early,),
    )(scalars, routes, cotangent)
    token_near_far = swap_near(token_far)

    cot_rows = add(cot_rows, wait=late)
    cot_own = exchange(cot_rows.reshape(experts, capacity, width))
    cot_own = cot_own.reshape(slots, width)

    outs = [
        ((piece_rows, width), FULL),
        ((piece_rows, width), FULL),
        ((piece_rows, width), LOW),
        ((piece_rows, width), LOW),
        ((total_rows, width), LOW),
        ((total_rows, 3 * local), LOW),
        ((total_rows, local), LOW),
        ((total_rows, width), LOW),
    ]
    outs += [((total_rows, total_rows), LOW)] * heads
    if has_blocks:
        outs += [((width, 4 * local), LOW), ((small_rows, width), FULL)]
    made = kernel_call(
        functools.partial(attend_kernel, owners, sequences, has_blocks),
        outs,
        "attend",
        smem=(0,),
        fetch=(1,),
        store=(5, *range(8, 8 + heads)),
        scratch=scratch,
        time=4,
    )(scalars, tokens, token_far, token_near, token_near_far, *blocks)
    keep, keep_far, send, send_far = made[:4]
    ones, qkv, attended, group, *probs = made[4 : 8 + heads]
    weights, small = made[8 + heads :] if has_blocks else blocks

    def scatter(keep_far, send, send_far, wait=()):
        near_far = swap_near(send_far)
        near = swap_near(send)
        (out,) = kernel_call(far_kernel, [(keep_far.shape, LOW)], "far", time=0.1, wait=wait)(
            keep_far, near_far
        )
        return near, swap_far(out), out

    near, far, mark = scatter(keep_far, send, send_far)
    small_now = small
    ones, attended, group, small, weights = save(
        ones, attended, group, small, weights, wait=(mark,)
    )
    tokens_here, spread_here = load(tokens, spread, wait=(mark, cot_own))
    middle, own_rows = kernel_call(
        functools.partial(middle_kernel, experts + 1),
        [((piece_rows, width), FULL), ((slots, width), LOW)],
        "middle",
        wait_hbm=(ones,),
    )(tokens_here, keep, near, far, small_now, spread_here)
    (middle,) = save(middle, wait=(own_rows,))

    def over_dp(rows):
        return exchange(rows.reshape(experts, capacity, width)).reshape(slots, width)

    own = over_dp(own_rows)
    cot_far = swap_far(cot_own)
    cot_near = swap_near(cot_own)
    cot_near_far = swap_near(cot_far)
    (small_expert,) = load(small, wait=(own_rows,))
    own = add(own, wait=(small_expert, cot_far), wait_hbm=(middle,))
    own_far = swap_far(own)
    own_near = swap_near(own)
    weight_in = w_expert_in[0]
    weight_out = w_expert_out[0]
    hidden_size = weight_in.shape[1]

    def expert_part(x_keep, x_send, cot_keep, cot_send, store):
        rows = 2 * slots
        return kernel_call(
            functools.partial(expert_kernel, experts),
            [
                ((slots, width), FULL),
                ((slots, width), LOW),
                ((rows, hidden_size), LOW),
                ((rows, hidden_size), LOW),
                ((rows, width), LOW),
                ((rows, 1), FULL),
                ((experts, width), FULL),
                ((rows, width), LOW),
            ],
            "expert",
            smem=(0,),
            store=store,
            time=4,
            scratch=[pltpu.VMEM((rows, width), LOW)],
        )(scalars, x_keep, x_send, cot_keep, cot_send, weight_in, weight_out, small_expert)

    keep, send, active_one, hidden_one, buffer_one, gate_one, router_one, rows_one = expert_part(
        own, own_near, cot_own, cot_near, (0, 3, 6, 7)
    )
    own_far = add(own_far, wait=(send,))
    keep_far, send_far, active_two, hidden_two, buffer_two, gate_two, router_two, rows_two = (
        expert_part(own_far, swap_near(own_far), cot_far, cot_near_far, ())
    )
    near, far, mark = scatter(keep_far, send, send_far)
    (keep,) = load(keep, wait=(mark,))
    rows_two, hidden_two, router_two = save(rows_two, hidden_two, router_two, wait=(mark,))
    forward_keep, forward_send, forward_keep_far, forward_send_far = kernel_call(
        forward_kernel,
        [((slots, width), kind) for kind in (FULL, LOW, FULL, LOW)],
        "forward",
        store=(0,),
        time=2,
        wait=(mark,),
    )(active_one, gate_one, active_two, gate_two, weight_out)
    (grad_expert_out,) = kernel_call(
        grad_w_kernel, [((1, *weight_out.shape), FULL)], "grad_out", store=(0,), time=3, wait=(mark,)
    )(active_one, active_two, buffer_one, buffer_two)
    (back_rows,) = kernel_call(
        join_kernel,
        [((slots, width), LOW)],
        "join",
        wait=(forward_send,),
        wait_hbm=(grad_expert_out, hidden_two),
    )(keep, near, far)
    back = over_dp(back_rows)
    out_near, out_far, out_mark = scatter(
        forward_keep_far, forward_send, forward_send_far, wait=(back_rows,)
    )
    (grad_expert_in,) = kernel_call(
        grad_w_kernel, [((1, *weight_in.shape), FULL)], "grad_in", fetch=range(4), store=(0,), time=3
    )(rows_one, rows_two, hidden_one, hidden_two)
    middle_here, cot_here, spread_here, small_here, forward_here = load(
        middle, cotangent, spread, small, forward_keep, wait=(out_mark,)
    )
    (out_rows,) = kernel_call(join_kernel, [((slots, width), LOW)], "join", time=0.1)(
        forward_here, out_near, out_far
    )
    out_back = over_dp(out_rows)

    grad_middle, grad_low, grad_gain_two = kernel_call(
        functools.partial(back_kernel, experts + 1),
        [((piece_rows, width), FULL), ((piece_rows, width), LOW), ((1, width), FULL)],
        "back",
        wait=(out_far,),
        wait_hbm=(grad_expert_in,),
    )(middle_here, cot_here, spread_here, back, small_here)
    grad_far = swap_far(grad_low)
    grad_near = swap_near(grad_low)
    grad_far = add(grad_far, wait=(out_rows,))
    grad_near_far = swap_near(grad_far)
    outs = [((total_rows, 3 * local), LOW)]
    middle_row = shard // 32 * 16
    scratch = [
        pltpu.VMEM((total_rows, width), LOW),
        pltpu.VMEM((2 * local, total_rows), FULL),
    ]
    if has_blocks:
        outs += [
            ((middle_row, 4 * local), LOW),
            ((shard - middle_row, 4 * local), LOW),
            ((width - shard, 4 * local), LOW),
        ]
        scratch = [pltpu.VMEM((width, 4 * local), LOW)] + scratch
    else:
        outs.append(((width, 4 * local), LOW))
    grads, *grad_w = kernel_call(
        functools.partial(attend_back_kernel, heads),
        outs,
        "attend_back",
        smem=(0,),
        fetch=range(5, 9 + heads),
        first=3 + heads,
        time=2,
        scratch=scratch,
    )(
        *(scalars, grad_low, grad_far, grad_near, grad_near_far),
        *(attended, weights, qkv, *probs, ones),
    )
    last = [((shard, local), FULL)] * 3 + [((local, shard), FULL)]
    held = {}

    def first(mark):
        keep, keep_far, send, send_far, payload = kernel_call(
            functools.partial(grad_one_kernel, experts),
            [((piece_rows, width), kind) for kind in (FULL, FULL, LOW, LOW)]
            + [((owners, small_rows, shard), FULL)],
            "grad_one",
            fetch=(1, 2, 3, 4),
            first=1,
            store=(0,),
            time=0.2,
            wait=(mark,),
        )(grads, weights, group, router_one, router_two, grad_gain_two)
        held["keep"], held["keep_far"] = keep, keep_far
        held["near_far"], held["near"] = swap_near(send_far), swap_near(send)
        held["small"] = (payload, swap(payload, "tensor", 1))
        return (send,), (), ()

    def second(mark):
        out_shape = [(held["keep_far"].shape, LOW)]
        (out,) = kernel_call(far_kernel, out_shape, "far", time=0.1, wait=(mark,))(
            held["keep_far"], held["near_far"]
        )
        held["far"] = swap_far(out)
        total = add(*held["small"], wait=(mark,))
        came = swap(total, "tensor", 2)
        held["small"] = (total, came)
        held["middle"] = save(grad_middle, wait=(mark,))
        return (out, total), (came,), held["middle"]

    def third(mark):
        total = add(*held["small"], wait=(mark,))
        held["small"] = exchange(total)
        return (total,), (held["far"],), ()

    def fourth(mark):
        held["last"] = kernel_call(
            functools.partial(last_kernel, experts),
            [
                ((piece_rows, width), FULL),
                ((piece_rows, width), LOW),
            ],
            "last",
            fetch=(0, 1, 4, 5, 6, 7),
            store=(0, 1),
            time=0.3,
            wait=(mark,),
        )(
            *(tokens, held["keep"], held["near"], held["far"]),
            *(*held["middle"], small, middle, spread, out_back),
        )
        return (), (), ()

    fillers = (first, second, third, fourth)
    last += [((1, shard), FULL), ((1, shard), FULL), ((experts, shard), FULL)]
    if has_blocks:
        parts = ring_reduce(*grad_w, shard, fillers, (out_back,))
        sums = kernel_call(
            functools.partial(ring_last_kernel, experts),
            last,
            "ring_last",
            store=range(7),
            wait_hbm=held["last"][:1],
        )(*parts, held["small"])
    else:
        for filler in fillers:
            filler(grad_w[0])
        sums = kernel_call(
            functools.partial(sum_kernel, experts), last, "sum", store=range(7)
        )(exchange(grad_w[0].reshape(owners, shard, 4 * local)), held["small"])
    grad_query, grad_key, grad_value, grad_out, grad_norm_attn, grad_norm_moe, grad_router = sums
    grad_tokens, result = held["last"]
    return (
        result,
        grad_tokens,
        grad_norm_attn.reshape(shard),
        grad_query,
        grad_key,
        grad_value,
        grad_out,
        grad_norm_moe.reshape(shard),
        grad_router.T,
        grad_expert_in,
        grad_expert_out,
    )


def solution(mesh):
    return jax.shard_map(
        on_device,
        mesh=mesh,
        in_specs=(
            P(("dp", "tensor"), None),
            P("dp", None),
            P("dp", None),
            P("dp"),
            P("dp", "tensor"),
            P("dp", "tensor"),
            P("dp", "tensor"),
            P("tensor", "dp"),
            P("dp"),
            P("dp", None),
            P("dp", None, "tensor"),
            P("dp", "tensor", None),
            P(("dp", "tensor"), None),
        ),
        out_specs=(
            P(("dp", "tensor"), None),
            P(("dp", "tensor"), None),
            P("dp"),
            P("dp", "tensor"),
            P("dp", "tensor"),
            P("dp", "tensor"),
            P("tensor", "dp"),
            P("dp"),
            P("dp", None),
            P("dp", None, "tensor"),
            P("dp", "tensor", None),
        ),
        check_vma=False,
    )
```
